256 devices in a mesh: section: 8 (over z), dp: 8 (over y, x_lo), mp: 4 (over x_hi, core).
Axes of the slice: x: 4 (x_hi: 2, x_lo: 2; x = x_hi * 2 + x_lo), y: 4, z: 8, core: 2. Of those that a mesh axis runs over, the one named last changes fastest.
Arguments:
- enc_input: bfloat16 [4, 8, 16, 4096], P(None, 'dp', None, 'mp'), may hold values from -6 to 6
- dec_input: bfloat16 [4, 8, 16, 4096], P(None, 'dp', None, 'mp'), may hold values from -6 to 6
- cotangent: bfloat16 [4, 8, 16, 4096], P(None, 'dp', None, 'mp'), may hold values from -6 to 6
- target_lengths: int32 [4, 8], P(None, 'dp'), may hold values from 1 to 16, 96 in all within a row
- weights: bfloat16 [8, 4, 4096, 2048], P('section', None, 'dp', 'mp'), may hold values from -0.09375 to 0.09375
Outputs:
- weight_grads: float32 [8, 4, 4096, 2048], P('section', None, 'dp', 'mp')
The draws below stay inside these ranges and needn't reach their ends.
Inputs may be any that keep to these rules, and one draw needn't show every extreme that they name: `target_lengths`: in every micro-batch the 8 lengths sum to 96 and the largest is 16.
All inputs are finite; a program needn't handle non-finite values. No bound on the sum of `target_lengths` on one device may be relied on, other than what follows from the above.
Results may differ from the reference program's by a relative error of at most 0.039.
Values may be sent and summed in bfloat16 or wider, within the bound.
A program may use at most 128 MiB of HBM per device.

```python
import math
import jax
import jax.numpy as jnp
import numpy as np
from jax import lax

D = 4096
HEADS = 8
HEAD_DIM = 256
LEN = 16
MICRO = 4
SECTIONS = 8
BATCH = 8
N_MP = 4


def block_scale(stream_key, extent, cuts, least, largest):
    def one(dim, blocks):
        draws = jax.random.uniform(jax.random.fold_in(jax.random.fold_in(stream_key, 6), dim), (blocks,), jnp.float32, least / len(cuts), largest / len(cuts))
        return jnp.repeat(jnp.exp(draws), extent[dim] // blocks).reshape((-1,) + (1,) * (len(extent) - dim - 1))

    loudness = one(*cuts[0])
    for cut in cuts[1:]:
        loudness = loudness * one(*cut)
    return loudness


def length_profile(count, total, limit, skew):
    portions = [(1 << 20) // math.isqrt(grade ** skew) + 1 for grade in range(2, count + 1)]
    surplus, given = total - limit - (count - 1), [1] * (count - 1)
    while surplus > 0:
        movable = [i for i in range(count - 1) if given[i] < limit]
        whole, remaining = sum([portions[i] for i in movable]), surplus
        for i in movable:
            addition = min(limit - given[i], max(1, remaining * portions[i] // whole), surplus)
            given[i] = given[i] + addition
            surplus = surplus - addition
    return np.array([limit] + given)


def uneven(own_key, count, total, reach, slope):
    if count == 2:
        one = jax.random.randint(own_key, (), max(1, total - reach), min(reach, total - 1) + 1)
        return jnp.stack([one, total - one])
    lengths = jnp.asarray(length_profile(count, total, reach, slope), jnp.int32)
    pairs = (count - 1) // 2
    giver, sink = lengths[1:1 + 2 * pairs:2], lengths[2:2 + 2 * pairs:2]
    slack = jnp.minimum(giver - 1, reach - sink)
    passed = jax.random.randint(jax.random.fold_in(own_key, 1), (pairs,), 0, 1 << 20) % (slack + 1)
    lengths = lengths.at[1:1 + 2 * pairs:2].set(giver - passed).at[2:2 + 2 * pairs:2].set(sink + passed)
    return lengths[jax.random.permutation(jax.random.fold_in(own_key, 2), count)]


def centred(rng, extent, scale, bound, shards=(), held_as=jnp.bfloat16):
    array = jax.random.normal(rng, extent, jnp.float32) * scale
    if len(shards) > 0:
        array = block_scale(rng, extent, shards, -0.22, 0.18) * array
    return jnp.clip(array, min=-bound, max=bound).astype(held_as)


def setup_inputs(seed: int = 0) -> dict:
    seeds = jax.random.split(jax.random.key(seed), 6)
    enc_input = centred(seeds[0], (MICRO, BATCH, LEN, D), 1.0, 6.0, ((1, 8), (3, 4)))
    dec_input = centred(seeds[1], (MICRO, BATCH, LEN, D), 1.0, 6.0, ((1, 8), (3, 4)))
    cotangent = centred(seeds[2], (MICRO, BATCH, LEN, D), 1.0, 6.0, ((1, 8), (3, 4)))
    target_lengths = jax.vmap(lambda own: uneven(own, BATCH, BATCH * LEN * 3 // 4, LEN, 1))(jax.random.split(seeds[3], MICRO)).reshape((MICRO, BATCH)).astype(jnp.int32)
    weights = centred(seeds[4], (SECTIONS, 4, D, HEADS * HEAD_DIM), D ** -0.5, 0.09375, ((0, 8), (2, 8), (3, 4)))
    return {"enc_input": enc_input, "dec_input": dec_input, "cotangent": cotangent, "target_lengths": target_lengths, "weights": weights}


epsilon = 1e-06

def normalize(values_in):
    widened = values_in.astype(jnp.float32)
    factor = lax.rsqrt(lax.optimization_barrier(jnp.mean(widened * widened, axis=-1, keepdims=True)) + epsilon)
    return (widened * factor, factor)

def norm_back(normed, factor, incoming):
    return factor * (incoming - normed * lax.optimization_barrier(jnp.mean(incoming * normed, axis=-1, keepdims=True)))

def rounded(values_in):
    return lax.optimization_barrier(values_in.astype(jnp.bfloat16))

def project(left_side, matrix):
    return jnp.einsum('mbld,dc->mblc', left_side.astype(jnp.float32), matrix.astype(jnp.float32))

def by_heads(flat_rows):
    return flat_rows.astype(jnp.float32).reshape(flat_rows.shape[:-1] + (HEADS, HEAD_DIM))

def by_groups(flat_rows):
    return flat_rows.astype(jnp.float32).reshape(flat_rows.shape[:-1] + (N_MP, HEADS * HEAD_DIM // N_MP))

def group_sum(group_terms):
    return lax.optimization_barrier(jnp.sum(rounded(group_terms).astype(jnp.float32), axis=0))

def layer_forward(query_rows, key_rows, matrices):
    query_normed, query_factor = normalize(query_rows)
    key_normed, key_factor = normalize(key_rows)
    query_low = rounded(query_normed)
    key_low = rounded(key_normed)
    query_vectors = rounded(project(query_low, matrices[0]))
    key_vectors = rounded(project(key_low, matrices[1]))
    value_vectors = rounded(project(key_low, matrices[2]))
    scores = jnp.einsum('mbqhe,mbkhe->mbhqk', by_heads(query_vectors), by_heads(key_vectors)) * HEAD_DIM ** (-0.5)
    raised = jnp.exp(scores)
    attention = rounded(raised / lax.optimization_barrier(jnp.sum(raised, axis=-1, keepdims=True)))
    context = jnp.einsum('mbhqk,mbkhe->mbqhe', attention.astype(jnp.float32), by_heads(value_vectors))
    context = rounded(context).reshape(query_vectors.shape)
    return (query_normed, query_factor, key_normed, key_factor, query_low, key_low, query_vectors, key_vectors, value_vectors, attention, context)

def sequence_sum(left_side, right_side):
    partial_sums = jnp.einsum('mbld,mblc->bdc', left_side.astype(jnp.float32), right_side.astype(jnp.float32))
    return lax.optimization_barrier(jnp.sum(rounded(partial_sums).astype(jnp.float32), axis=0))

def layer_backward(saved, grad_out, matrices):
    query_normed, query_factor, key_normed, key_factor, query_low, key_low, query_vectors, key_vectors, value_vectors, attention, context = saved
    grad_context = rounded(project(grad_out, matrices[3]))
    split_grad = by_heads(grad_context)
    widened = attention.astype(jnp.float32)
    grad_attention = jnp.einsum('mbqhe,mbkhe->mbhqk', split_grad, by_heads(value_vectors))
    grad_values = rounded(jnp.einsum('mbhqk,mbqhe->mbkhe', widened, split_grad)).reshape(grad_context.shape)
    grad_scores = rounded(widened * (grad_attention - lax.optimization_barrier(jnp.sum(grad_attention * widened, axis=-1, keepdims=True))) * HEAD_DIM ** (-0.5))
    grad_scores = grad_scores.astype(jnp.float32)
    grad_queries = rounded(jnp.einsum('mbhqk,mbkhe->mbqhe', grad_scores, by_heads(key_vectors))).reshape(grad_context.shape)
    grad_keys = rounded(jnp.einsum('mbhqk,mbqhe->mbkhe', grad_scores, by_heads(query_vectors))).reshape(grad_context.shape)
    back_query = jnp.einsum('mblgc,dgc->gmbld', by_groups(grad_queries), by_groups(matrices[0]))
    back_key = jnp.einsum('mblgc,dgc->gmbld', by_groups(grad_keys), by_groups(matrices[1]))
    back_key = back_key + jnp.einsum('mblgc,dgc->gmbld', by_groups(grad_values), by_groups(matrices[2]))
    from_query = group_sum(norm_back(query_normed, query_factor, back_query))
    from_key = group_sum(norm_back(key_normed, key_factor, back_key))
    gradients = jnp.stack([sequence_sum(query_low, grad_queries), sequence_sum(key_low, grad_keys), sequence_sum(key_low, grad_values), sequence_sum(grad_out, context)])
    return (from_query, from_key, gradients)

def reference(enc_input, dec_input, cotangent, target_lengths, weights):
    section_total = weights.shape[0]
    half_point = section_total // 2
    stream_enc = enc_input
    stream_dec = dec_input
    saved_layers = []
    for section_index in range(section_total):
        query_rows = stream_dec if section_index >= half_point else stream_enc
        saved = layer_forward(query_rows, stream_enc, weights[section_index])
        added = group_sum(jnp.einsum('mblgc,dgc->gmbld', by_groups(saved[-1]), by_groups(weights[section_index, 3])))
        updated = (query_rows.astype(jnp.float32) + added).astype(jnp.bfloat16)
        saved_layers.append(saved)
        if section_index >= half_point:
            stream_dec = updated
        else:
            stream_enc = updated
    offsets = lax.broadcasted_iota(jnp.int32, cotangent.shape[:3], 2)
    live_rows = (offsets < target_lengths[:, :, None].astype(jnp.int32)).astype(jnp.float32)
    loss_scale = (MICRO * BATCH * LEN) ** (-0.5)
    grad_dec = (cotangent.astype(jnp.float32) * live_rows[..., None] * loss_scale).astype(jnp.bfloat16)
    grad_enc = jnp.zeros(enc_input.shape, jnp.bfloat16)
    results = [None] * section_total
    for section_index in reversed(range(section_total)):
        decoder_side = section_index >= half_point
        grad_out = grad_dec if decoder_side else grad_enc
        from_query, from_key, gradients = layer_backward(saved_layers[section_index], grad_out, weights[section_index])
        if decoder_side:
            grad_dec = (grad_dec.astype(jnp.float32) + from_query).astype(jnp.bfloat16)
            grad_enc = (grad_enc.astype(jnp.float32) + from_key).astype(jnp.bfloat16)
        else:
            grad_enc = (grad_enc.astype(jnp.float32) + from_key + from_query).astype(jnp.bfloat16)
        results[section_index] = gradients
    return jnp.stack(results)
```

```python
import functools

import jax
import jax.numpy as jnp
from jax import lax
from jax.experimental import pallas as pl
from jax.experimental.pallas import tpu as pltpu
from jax.sharding import PartitionSpec as P

HEAD_DIM = 256
EPSILON = 1e-06
MICRO = 4
BF = jnp.bfloat16
F32 = jnp.float32
MESH = pl.DeviceIdType.MESH
NT = (((1,), (1,)), ((), ()))
NN = (((1,), (0,)), ((), ()))
TN = (((0,), (0,)), ((), ()))


def dot(a, b, dims=NN):
    return lax.dot_general(a, b, dims, preferred_element_type=F32)


def layer_kernel(
    width,
    start_ref, weights_ref, out_ref,
    w, xs, part, qrecv, qs, ks, vs, ps, rr, cs, oown, ost, orecv, xn,
    dpart, drecv, dd, cc, uown, ust, urecv, wown, wst, wrecv, gn, gein, geout, ob,
    g_ss, g_rs, i_ss, x_rs, f_ss, q_ss, q_rs, c_ss, c_rs, o_ss, o_rs, n_ss,
    d_ss, d_rs, dd_ss, dd_rs, cc_ss, cc_rs, u_ss, u_rs, w_ss, w_rs, e_ss, e_rs, gn_ss,
    b_ss, b_rs,
):
    s = lax.axis_index("section")
    d = lax.axis_index("dp")
    p = lax.axis_index("mp")
    t = d // 2
    c = lax.rem(p, 2)
    j = 2 * (p // 2) + lax.rem(d, 2)
    decoder = s >= 4
    sel = jnp.where(decoder, 1, 0)
    starts = (s == 0) | (s == 4) | (s == 7)
    start_stream = jnp.where(s == 0, 0, jnp.where(s == 4, 1, 2))

    def place(tt, jj, ccc):
        return 2 * tt + lax.rem(jj, 2), 2 * (jj // 2) + ccc

    def member(k):
        return place(t, lax.rem(j + k, 4), c)

    gather_to = [place(k, p, d // 4) for k in range(4)]
    owner = [(4 * c + b, j) for b in range(4)]
    start_to = [place(t, jnp.int32(k), p // 2) for k in range(4)]
    start_from = [(2 * t + a, 2 * c + e) for a in range(2) for e in range(2)]

    def same(dev):
        return (dev[0] == d) & (dev[1] == p)

    def remote(src, dst, ss, rs, dev, sec=None):
        ids = {"dp": dev[0], "mp": dev[1]}
        if sec is not None:
            ids["section"] = sec
        return pltpu.make_async_remote_copy(
            src_ref=src, dst_ref=dst, send_sem=ss, recv_sem=rs, device_id=ids, device_id_type=MESH
        )

    def arrived(ref, sem):
        pltpu.make_async_copy(ref, ref, sem).wait()

    def send_any(src, dst, ss, rs, dev):
        here = same(dev)

        @pl.when(here)
        def _():
            pltpu.make_async_copy(src, dst, rs).start()

        @pl.when(jnp.logical_not(here))
        def _():
            remote(src, dst, ss, rs, dev).start()

    def sent_any(src, ss, dev):
        @pl.when(jnp.logical_not(same(dev)))
        def _():
            arrived(src, ss)

    bar = pltpu.get_barrier_semaphore()

    def greet(dev, sec=None):
        ids = {"dp": dev[0], "mp": dev[1]}
        if sec is not None:
            ids["section"] = sec
        pl.semaphore_signal(bar, inc=1, device_id=ids, device_id_type=MESH)

    greet((d, p + 1 - 2 * c))
    for k in range(1, 4):
        greet(member(k))

    @pl.when(s > 0)
    def _():
        for k in range(4):
            greet(member(k), s - 1)

    @pl.when(s < 7)
    def _():
        for k in range(4):
            greet(member(k), s + 1)

    for dev in gather_to + owner:
        @pl.when(jnp.logical_not(same(dev)))
        def _(dev=dev):
            greet(dev)

    @pl.when(starts)
    def _():
        for dev in start_from:
            @pl.when(jnp.logical_not(same(dev)))
            def _(dev=dev):
                greet(dev)

    own_shard = sum(jnp.where(same(dev), 1, 0) for dev in gather_to)
    own_start = sum(jnp.where(same(dev), 1, 0) for dev in start_to)
    count = 4 + jnp.where(s > 0, 4, 0) + jnp.where(s < 7, 4, 0) + 8 - 2 * own_shard
    count = count + jnp.where(starts, 4 - own_start, 0)
    pl.semaphore_wait(bar, count)

    @pl.when(starts)
    def _():
        for m in range(MICRO):
            for k in range(4):
                send_any(
                    start_ref.at[m],
                    xs.at[start_stream, m, pl.ds(2 * lax.rem(p, 2), 2), lax.rem(d, 2)],
                    i_ss.at[m, k], x_rs.at[start_stream, m], start_to[k],
                )

    for mat in range(4):
        for k in range(4):
            send_any(
                weights_ref.at[mat], w.at[mat, lax.rem(d, 4)], g_ss.at[mat, k], g_rs.at[mat],
                gather_to[k],
            )
    for mat in range(4):
        arrived(w.at[mat], g_rs.at[mat])

    def rows(value):
        return value.reshape(32, 512)

    def attend(m):
        arrived(xs.at[0, m], x_rs.at[0, m])

        @pl.when(decoder)
        def _():
            @pl.when(s < 7)
            def _():
                remote(
                    xs.at[0, m], xs.at[0, m], f_ss.at[m], x_rs.at[0, m], (d, p), s + 1
                ).start()

            arrived(xs.at[1, m], x_rs.at[1, m])

        sums = [None, None, None]
        squares = [None, None]
        for b in range(4):
            query = rows(xs[sel, m, b])
            key = rows(xs[0, m, b])
            for i, left in enumerate((query, key, key)):
                term = dot(left, w[i, b])
                sums[i] = term if b == 0 else sums[i] + term
            for i, left in enumerate((query, key)):
                wide = left.astype(F32)
                term = jnp.sum(wide * wide, axis=-1, keepdims=True)
                squares[i] = term if b == 0 else squares[i] + term
        for i in range(3):
            part[m, :, :, i * 512:(i + 1) * 512] = sums[i].reshape(2, 16, 512)
        for i in range(2):
            part[m, :, :, 1536 + i * 128:1664 + i * 128] = jnp.broadcast_to(
                squares[i], (32, 128)
            ).reshape(2, 16, 128)
        other = (d, p + 1 - 2 * c)
        remote(part.at[m, 1 - c], qrecv.at[m], q_ss.at[m], q_rs.at[m], other).start()
        arrived(qrecv.at[m], q_rs.at[m])
        total = part[m, c] + qrecv[m]
        factor_q = lax.rsqrt(total[:, 1536:1537] * (1.0 / width) + EPSILON)
        factor_k = lax.rsqrt(total[:, 1664:1665] * (1.0 / width) + EPSILON)
        rr[m, 0] = jnp.broadcast_to(factor_q, (16, 128))
        rr[m, 1] = jnp.broadcast_to(factor_k, (16, 128))
        query = (total[:, :512] * factor_q).astype(BF)
        key = (total[:, 512:1024] * factor_k).astype(BF)
        value = (total[:, 1024:1536] * factor_k).astype(BF)
        qs[m] = query
        ks[m] = key
        vs[m] = value
        contexts = []
        for h in range(2):
            cols = slice(h * HEAD_DIM, (h + 1) * HEAD_DIM)
            raised = jnp.exp(dot(query[:, cols], key[:, cols], NT) * HEAD_DIM ** (-0.5))
            weight = (raised / jnp.sum(raised, axis=-1, keepdims=True)).astype(BF)
            ps[m, h] = weight.astype(F32)
            contexts.append(dot(weight, value[:, cols]).astype(BF))
        cs[m, c] = jnp.concatenate(contexts, axis=1)
        remote(cs.at[m, c], cs.at[m, c], c_ss.at[m], c_rs.at[m], other).start()
        arrived(cs.at[m, c], c_rs.at[m])

        @pl.when(s < 7)
        def _():
            context = rows(cs[m])
            for k in (1, 2, 3, 0):
                term = dot(context, w[3, lax.rem(j + k, 4)], NT)
                if k == 0:
                    oown[m] = term
                else:
                    ost[m, k - 1] = term.astype(BF)
                    remote(
                        ost.at[m, k - 1], orecv.at[m, k - 1], o_ss.at[m, k - 1], o_rs.at[m],
                        member(k),
                    ).start()

    def advance(m):
        arrived(orecv.at[m], o_rs.at[m])
        total = rows(xs[sel, m, j]).astype(F32) + oown[m]
        for k in range(3):
            total = total + orecv[m, k].astype(F32)
        xn[m] = total.astype(BF).reshape(2, 16, 512)
        for k in range(4):
            remote(
                xn.at[m], xs.at[sel, m, j], n_ss.at[m, k], x_rs.at[sel, m], member(k), s + 1
            ).start()

    def forward_step(i, carry):
        @pl.when(i < MICRO)
        def _():
            attend(i)

        @pl.when((i > 0) & (s < 7))
        def _():
            advance(i - 1)

        return carry

    lax.fori_loop(0, MICRO + 1, forward_step, 0)

    def to_owners(src_of, slot):
        for b in range(4):
            send_any(src_of(b), ob.at[slot, :, t], b_ss.at[slot, b], b_rs.at[slot], owner[b])

    def owners_sent(src_of, slot):
        for b in range(4):
            sent_any(src_of(b), b_ss.at[slot, b], owner[b])

    to_owners(lambda b: xs.at[sel, :, b], 0)

    @pl.when(decoder)
    def _():
        to_owners(lambda b: xs.at[0, :, b], 1)

    to_owners(lambda b: cs, 3)

    def attend_back(m):
        arrived(xs.at[2, m], x_rs.at[2, m])
        total = None
        for b in range(4):
            term = dot(rows(xs[2, m, b]), w[3, b])
            total = term if b == 0 else total + term
        dpart[m] = total.reshape(2, 16, 512)
        other = (d, p + 1 - 2 * c)
        remote(dpart.at[m, 1 - c], drecv.at[m], d_ss.at[m], d_rs.at[m], other).start()
        arrived(drecv.at[m], d_rs.at[m])
        grad = (dpart[m, c] + drecv[m]).astype(BF)
        query, key, value = qs[m], ks[m], vs[m]
        pieces = [[], [], []]
        for h in range(2):
            cols = slice(h * HEAD_DIM, (h + 1) * HEAD_DIM)
            weight = ps[m, h]
            grad_weight = dot(grad[:, cols], value[:, cols], NT)
            pieces[2].append(dot(weight.astype(BF), grad[:, cols], TN))
            inner = jnp.sum(grad_weight * weight, axis=-1, keepdims=True)
            scores = (weight * (grad_weight - inner) * HEAD_DIM ** (-0.5)).astype(BF)
            pieces[0].append(dot(scores, key[:, cols]))
            pieces[1].append(dot(scores, query[:, cols], TN))
        grads = [jnp.concatenate(piece, axis=1) for piece in pieces]
        factors = [rr[m, 0][:, :1], rr[m, 1][:, :1], rr[m, 1][:, :1]]
        means = [
            jnp.sum(g * v.astype(F32), axis=-1, keepdims=True) * (1.0 / width)
            for g, v in zip(grads, (query, key, value))
        ]
        for i in range(3):
            dd[m, i, c] = (grads[i] * factors[i]).astype(BF)
        cc[m, 0, c] = jnp.broadcast_to(means[0] * factors[0] * factors[0], (16, 128))
        cc[m, 1, c] = jnp.broadcast_to((means[1] + means[2]) * factors[1] * factors[1], (16, 128))
        remote(dd.at[m, :, c], dd.at[m, :, c], dd_ss.at[m], dd_rs.at[m], other).start()
        remote(cc.at[m, :, c], cc.at[m, :, c], cc_ss.at[m], cc_rs.at[m], other).start()
        arrived(dd.at[m, :, c], dd_rs.at[m])
        arrived(cc.at[m, :, c], cc_rs.at[m])

        def spread(pairs, stream, kinds, own, stage, recv, ss, rs):
            lefts = [rows(dd[m, i]) for i in pairs]
            shift = sum(cc[m, i].reshape(32, 128)[:, :1] for i in kinds)
            for k in (1, 2, 3, 0):
                block = lax.rem(j + k, 4)
                term = -rows(xs[stream, m, block]).astype(F32) * shift
                for i, left in zip(pairs, lefts):
                    term = term + dot(left, w[i, block], NT)
                if k == 0:
                    own[m] = term
                else:
                    stage[m, k - 1] = term.astype(BF)
                    remote(
                        stage.at[m, k - 1], recv.at[m, k - 1], ss.at[m, k - 1], rs.at[m], member(k)
                    ).start()

        @pl.when((s > 0) & (s < 4))
        def _():
            spread((0, 1, 2), 0, (0, 1), uown, ust, urecv, u_ss, u_rs)

        @pl.when(s > 4)
        def _():
            spread((0,), 1, (0,), uown, ust, urecv, u_ss, u_rs)

        @pl.when(s >= 4)
        def _():
            spread((1, 2), 0, (1,), wown, wst, wrecv, w_ss, w_rs)

    def hand_back(m):
        for k in range(4):
            remote(
                gn.at[m], xs.at[2, m, j], gn_ss.at[m, k], x_rs.at[2, m], member(k), s - 1
            ).start()

    def advance_back(m):
        @pl.when(s != 4)
        def _():
            arrived(urecv.at[m], u_rs.at[m])
            total = rows(xs[2, m, j]).astype(F32) + uown[m]
            for k in range(3):
                total = total + urecv[m, k].astype(F32)
            gn[m] = total.astype(BF).reshape(2, 16, 512)
            hand_back(m)

        @pl.when(s >= 4)
        def _():
            arrived(wrecv.at[m], w_rs.at[m])
            total = wown[m]
            for k in range(3):
                total = total + wrecv[m, k].astype(F32)
            geout[m] = total.astype(BF).reshape(2, 16, 512)

            @pl.when(s < 7)
            def _():
                arrived(gein.at[m], e_rs.at[m])
                geout[m] = (total + rows(gein[m]).astype(F32)).astype(BF).reshape(2, 16, 512)

            @pl.when(s > 4)
            def _():
                remote(geout.at[m], gein.at[m], e_ss.at[m], e_rs.at[m], (d, p), s - 1).start()

            @pl.when(s == 4)
            def _():
                gn[m] = geout[m]
                hand_back(m)

    def backward_step(i, carry):
        @pl.when(i < MICRO)
        def _():
            attend_back(i)

        @pl.when((i > 0) & (s > 0))
        def _():
            advance_back(i - 1)

        return carry

    lax.fori_loop(0, MICRO + 1, backward_step, 0)

    to_owners(lambda b: xs.at[2, :, b], 2)
    for i in range(3):
        to_owners(lambda b: dd.at[:, i], 4 + i)

    key_slot = jnp.where(decoder, 1, 0)
    arrived(ob.at[3], b_rs.at[3])
    arrived(ob.at[2], b_rs.at[2])
    out_ref[3] = dot(ob[2].reshape(512, 512), ob[3].reshape(512, 512), TN)
    arrived(ob.at[0], b_rs.at[0])

    @pl.when(decoder)
    def _():
        arrived(ob.at[1], b_rs.at[1])

    for i in range(3):
        arrived(ob.at[4 + i], b_rs.at[4 + i])
        left = ob[0] if i == 0 else ob[key_slot]
        out_ref[i] = dot(left.reshape(512, 512), ob[4 + i].reshape(512, 512), TN)

    @pl.when(starts)
    def _():
        for m in range(MICRO):
            for k in range(4):
                sent_any(start_ref.at[m], i_ss.at[m, k], start_to[k])

    for mat in range(4):
        for k in range(4):
            sent_any(weights_ref.at[mat], g_ss.at[mat, k], gather_to[k])
    owners_sent(lambda b: xs.at[sel, :, b], 0)

    @pl.when(decoder)
    def _():
        owners_sent(lambda b: xs.at[0, :, b], 1)

    owners_sent(lambda b: xs.at[2, :, b], 2)
    owners_sent(lambda b: cs, 3)
    for i in range(3):
        owners_sent(lambda b: dd.at[:, i], 4 + i)

    def finish(m, carry):
        arrived(part.at[m, 0], q_ss.at[m])
        arrived(cs.at[m, 0], c_ss.at[m])
        arrived(dpart.at[m, 0], d_ss.at[m])
        arrived(dd.at[m, :, 0], dd_ss.at[m])
        arrived(cc.at[m, :, 0], cc_ss.at[m])

        @pl.when(decoder & (s < 7))
        def _():
            arrived(xs.at[0, m], f_ss.at[m])

        @pl.when(s < 7)
        def _():
            for k in range(3):
                arrived(ost.at[m, k], o_ss.at[m, k])
            for k in range(4):
                arrived(xn.at[m], n_ss.at[m, k])

        @pl.when((s > 0) & (s != 4))
        def _():
            for k in range(3):
                arrived(ust.at[m, k], u_ss.at[m, k])

        @pl.when(s > 0)
        def _():
            for k in range(4):
                arrived(gn.at[m], gn_ss.at[m, k])

        @pl.when(s >= 4)
        def _():
            for k in range(3):
                arrived(wst.at[m, k], w_ss.at[m, k])

        @pl.when(s > 4)
        def _():
            arrived(geout.at[m], e_ss.at[m])

        return carry

    lax.fori_loop(0, MICRO, finish, 0)


def per_device(enc_input, dec_input, cotangent, target_lengths, weights):
    section = lax.axis_index("section")
    micro_count, sequences, seq_length, feature_part = enc_input.shape
    scale = lax.rsqrt(jnp.float32(micro_count * lax.axis_size("dp") * sequences * seq_length))
    offsets = lax.broadcasted_iota(jnp.int32, (micro_count, sequences, seq_length), 2)
    live = (offsets < target_lengths[:, :, None]).astype(F32)
    seed = (cotangent.astype(F32) * live[..., None] * scale).astype(BF)
    start = jnp.where(section == 0, enc_input, jnp.where(section == 4, dec_input, seed))
    start = start.reshape(MICRO, 16, 2, 512).transpose(0, 2, 1, 3)
    dma = pltpu.SemaphoreType.DMA
    tile = (2, 16, 512)
    scratch = [
        pltpu.VMEM((4, 4, 512, 512), BF),
        pltpu.VMEM((3, MICRO, 4) + tile, BF),
        pltpu.VMEM((MICRO, 2, 16, 1792), F32),
        pltpu.VMEM((MICRO, 16, 1792), F32),
        pltpu.VMEM((MICRO, 16, 512), BF),
        pltpu.VMEM((MICRO, 16, 512), BF),
        pltpu.VMEM((MICRO, 16, 512), BF),
        pltpu.VMEM((MICRO, 2, 16, 16), F32),
        pltpu.VMEM((MICRO, 2, 16, 128), F32),
        pltpu.VMEM((MICRO,) + tile, BF),
        pltpu.VMEM((MICRO, 32, 512), F32),
        pltpu.VMEM((MICRO, 3, 32, 512), BF),
        pltpu.VMEM((MICRO, 3, 32, 512), BF),
        pltpu.VMEM((MICRO,) + tile, BF),
        pltpu.VMEM((MICRO,) + tile, F32),
        pltpu.VMEM((MICRO, 16, 512), F32),
        pltpu.VMEM((MICRO, 3) + tile, BF),
        pltpu.VMEM((MICRO, 2, 2, 16, 128), F32),
        pltpu.VMEM((MICRO, 32, 512), F32),
        pltpu.VMEM((MICRO, 3, 32, 512), BF),
        pltpu.VMEM((MICRO, 3, 32, 512), BF),
        pltpu.VMEM((MICRO, 32, 512), F32),
        pltpu.VMEM((MICRO, 3, 32, 512), BF),
        pltpu.VMEM((MICRO, 3, 32, 512), BF),
        pltpu.VMEM((MICRO,) + tile, BF),
        pltpu.VMEM((MICRO,) + tile, BF),
        pltpu.VMEM((MICRO,) + tile, BF),
        pltpu.VMEM((7, MICRO, 4) + tile, BF),
        dma((4, 4)), dma((4,)),
        dma((MICRO, 4)), dma((3, MICRO)),
        dma((MICRO,)),
        dma((MICRO,)), dma((MICRO,)),
        dma((MICRO,)), dma((MICRO,)),
        dma((MICRO, 3)), dma((MICRO,)),
        dma((MICRO, 4)),
        dma((MICRO,)), dma((MICRO,)),
        dma((MICRO,)), dma((MICRO,)),
        dma((MICRO,)), dma((MICRO,)),
        dma((MICRO, 3)), dma((MICRO,)),
        dma((MICRO, 3)), dma((MICRO,)),
        dma((MICRO,)), dma((MICRO,)),
        dma((MICRO, 4)),
        dma((7, 4)), dma((7,)),
    ]
    grads = pl.pallas_call(
        functools.partial(layer_kernel, 4096),
        out_shape=jax.ShapeDtypeStruct((4, 512, 512), F32),
        in_specs=[pl.BlockSpec(memory_space=pltpu.VMEM), pl.BlockSpec(memory_space=pl.ANY)],
        out_specs=pl.BlockSpec(memory_space=pltpu.VMEM),
        scratch_shapes=scratch,
        compiler_params=pltpu.CompilerParams(
            collective_id=0, has_side_effects=True, vmem_limit_bytes=48 << 20
        ),
        name="layers",
    )(start, weights[0])
    return grads[None]


def solution(mesh):
    in_specs = (
        P(None, "dp", None, "mp"),
        P(None, "dp", None, "mp"),
        P(None, "dp", None, "mp"),
        P(None, "dp"),
        P("section", None, "dp", "mp"),
    )
    return jax.shard_map(
        per_device,
        mesh=mesh,
        in_specs=in_specs,
        out_specs=P("section", None, "dp", "mp"),
        check_vma=False,
    )
```

```python
import functools

import jax
import jax.numpy as jnp
from jax import lax
from jax.experimental import pallas as pl
from jax.experimental.pallas import tpu as pltpu
from jax.sharding import PartitionSpec as P

HEAD_DIM = 256
EPSILON = 1e-06
MICRO = 4
BF = jnp.bfloat16
F32 = jnp.float32
MESH = pl.DeviceIdType.MESH
ORDER = (2, 1, 3, 0)
NT = (((1,), (1,)), ((), ()))
NN = (((1,), (0,)), ((), ()))
TN = (((0,), (0,)), ((), ()))


def dot(a, b, dims=NN):
    return lax.dot_general(a, b, dims, preferred_element_type=F32)


def layer_kernel(
    width,
    start_ref, weights_ref, out_ref,
    w, xs, part, qrecv, qs, ks, vs, ps, rr, cs, oown, ost, orecv, xn,
    dpart, drecv, dd, cc, uown, ust, urecv, wown, wst, wrecv, gn, gein, geout, ob,
    ga_ss, ga_rs, gb_ss, gb_rs, gc_ss, gc_rs, i_ss, x_rs, f_ss, fp_ss, q_ss, q_rs, kv_ss, kv_rs,
    c_ss, c_rs, o_ss, o_rs, n_ss,
    d_ss, d_rs, dd_ss, dd_rs, cc_ss, cc_rs, u_ss, u_rs, w_ss, w_rs, e_ss, e_rs, gn_ss,
    b_ss, b_rs,
):
    s = lax.axis_index("section")
    d = lax.axis_index("dp")
    p = lax.axis_index("mp")
    t = d // 2
    c = lax.rem(p, 2)
    j = 2 * (p // 2) + lax.rem(d, 2)
    odd = lax.rem(t, 2)
    decoder = s >= 4
    sel = jnp.where(decoder, 1, 0)
    starts = (s == 0) | (s == 4) | (s == 7)
    start_stream = jnp.where(s == 0, 0, jnp.where(s == 4, 1, 2))
    other = (d, p + 1 - 2 * c)

    def place(tt, jj, ccc):
        return 2 * tt + lax.rem(jj, 2), 2 * (jj // 2) + ccc

    def member(k):
        return place(t, lax.rem(j + k, 4), c)

    def column(tt):
        return 2 * tt + lax.rem(d, 2), p

    collector = place(t, p, d // 4)
    inner = t // 2 == c
    beside = column(t + 1 - 2 * odd)
    across = column(lax.rem(t + 3 - 2 * odd, 4))
    senders = [place(k, p, d // 4) for k in range(4)]
    owner = [(4 * c + b, j) for b in range(4)]
    start_to = [place(t, jnp.int32(k), p // 2) for k in range(4)]
    start_from = [(2 * t + a, 2 * c + e) for a in range(2) for e in range(2)]

    def same(dev):
        return (dev[0] == d) & (dev[1] == p)

    def remote(src, dst, ss, rs, dev, sec=None):
        ids = {"dp": dev[0], "mp": dev[1]}
        if sec is not None:
            ids["section"] = sec
        return pltpu.make_async_remote_copy(
            src_ref=src, dst_ref=dst, send_sem=ss, recv_sem=rs, device_id=ids, device_id_type=MESH
        )

    def arrived(ref, sem):
        pltpu.make_async_copy(ref, ref, sem).wait()

    def send_any(src, dst, ss, rs, dev):
        here = same(dev)

        @pl.when(here)
        def _():
            pltpu.make_async_copy(src, dst, rs).start()

        @pl.when(jnp.logical_not(here))
        def _():
            remote(src, dst, ss, rs, dev).start()

    def sent_any(src, ss, dev):
        @pl.when(jnp.logical_not(same(dev)))
        def _():
            arrived(src, ss)

    bar = pltpu.get_barrier_semaphore()

    def greet(dev, sec=None):
        ids = {"dp": dev[0], "mp": dev[1]}
        if sec is not None:
            ids["section"] = sec
        pl.semaphore_signal(bar, inc=1, device_id=ids, device_id_type=MESH)

    def greet_other(dev):
        @pl.when(jnp.logical_not(same(dev)))
        def _():
            greet(dev)

    greet(other)
    greet(beside)
    greet(across)
    for k in range(1, 4):
        greet(member(k))

    @pl.when(s > 0)
    def _():
        for k in range(4):
            greet(member(k), s - 1)

    @pl.when(s < 7)
    def _():
        for k in range(4):
            greet(member(k), s + 1)

    for dev in senders:
        greet_other(dev)

    @pl.when(inner)
    def _():
        for e in range(2):
            greet_other((2 * t + e, j))

    @pl.when(starts)
    def _():
        for dev in start_from:
            greet_other(dev)

    def others(devs):
        return sum(jnp.where(same(dev), 0, 1) for dev in devs)

    count = 6 + jnp.where(s > 0, 4, 0) + jnp.where(s < 7, 4, 0) + others(owner)
    count = count + others([collector]) + jnp.where(starts, others(start_to), 0)
    pl.semaphore_wait(bar, count)

    for mat in range(4):
        send_any(
            weights_ref.at[mat], w.at[mat, lax.rem(d, 4)], ga_ss.at[mat], ga_rs.at[mat], collector
        )

    @pl.when(starts)
    def _():
        for m in range(MICRO):
            for k in range(4):
                for e in range(2):
                    block = 2 * lax.rem(p, 2) + e
                    send_any(
                        start_ref.at[m, e], xs.at[start_stream, m, block, lax.rem(d, 2)],
                        i_ss.at[m, k], x_rs.at[start_stream, m, block], start_to[k],
                    )

    def pair(mat, first):
        return w.at[mat, pl.ds(2 * first, 2)]

    @pl.when(inner)
    def _():
        def pass_on(mat):
            arrived(pair(mat, 1 - odd), gb_rs.at[mat])
            piece = w.at[mat, 2 * (1 - odd)]
            remote(piece, piece, gc_ss.at[mat], gc_rs.at[mat], across).start()

        for mat in range(4):
            mine = pair(mat, odd)
            arrived(mine, ga_rs.at[mat])
            remote(mine, mine, gb_ss.at[mat, 0], gb_rs.at[mat], beside).start()
            remote(mine, mine, gb_ss.at[mat, 1], gb_rs.at[mat], across).start()
            if mat > 0:
                pass_on(mat - 1)
        pass_on(3)

    @pl.when(jnp.logical_not(inner))
    def _():
        for mat in range(4):
            arrived(pair(mat, 1 - odd), gb_rs.at[mat])
            piece = w.at[mat, 2 * (1 - odd) + 1]
            remote(piece, piece, gc_ss.at[mat], gc_rs.at[mat], beside).start()
        for mat in range(4):
            arrived(pair(mat, odd), gc_rs.at[mat])

    def rows(value):
        return value.reshape(32, 512)

    def block_at(k):
        return lax.rem(j + 4 - k, 4)

    def project(m, stream, mats, start, ss, rs, relayed=None):
        sums = [None] * len(mats)
        squares = None
        for k in ORDER:
            block = block_at(k)
            if k == 0 and relayed is not None:
                @pl.when(jnp.logical_not(relayed))
                def _():
                    arrived(xs.at[stream, m, block], x_rs.at[stream, m, block])
            else:
                arrived(xs.at[stream, m, block], x_rs.at[stream, m, block])
            left = rows(xs[stream, m, block])
            wide = left.astype(F32)
            square = jnp.sum(wide * wide, axis=-1, keepdims=True)
            squares = square if squares is None else squares + square
            for i, mat in enumerate(mats):
                term = dot(left, w[mat, block])
                sums[i] = term if sums[i] is None else sums[i] + term
        squares = jnp.broadcast_to(squares, (32, 128)).reshape(2, 16, 128)
        for i, mat in enumerate(mats):
            first = (0, 640, 1152)[mat]
            part[m, :, :, first:first + 512] = sums[i].reshape(2, 16, 512)
        if 0 in mats:
            part[m, :, :, 512:640] = squares
        if 1 in mats:
            part[m, :, :, 1664:1792] = squares
        cols = pl.ds(*start)
        remote(part.at[m, 1 - c, :, cols], qrecv.at[m, :, cols], ss.at[m], rs.at[m], other).start()

    def project_all(m):
        project(m, 0, (0, 1, 2), (0, 1792), q_ss, q_rs)

    def project_query(m):
        project(m, 1, (0,), (0, 640), q_ss, q_rs)

    def project_key(m):
        project(m, 0, (1, 2), (640, 1152), kv_ss, kv_rs, s > 4)

        @pl.when(s == 4)
        def _():
            onward(m)

    def onward(m):
        remote(
            xs.at[0, m, j], xs.at[0, m, j], f_ss.at[m], x_rs.at[0, m, j], (d, p), s + 1
        ).start()

    def relay(m):
        arrived(xs.at[0, m, j], x_rs.at[0, m, j])

        @pl.when(s < 7)
        def _():
            onward(m)

        for k in (2, 1, 3):
            remote(
                xs.at[0, m, j], xs.at[0, m, j], fp_ss.at[m, k - 1], x_rs.at[0, m, j], member(k)
            ).start()

    def attend(m):
        @pl.when(decoder)
        def _():
            arrived(qrecv.at[m, :, pl.ds(0, 640)], q_rs.at[m])
            arrived(qrecv.at[m, :, pl.ds(640, 1152)], kv_rs.at[m])

        @pl.when(jnp.logical_not(decoder))
        def _():
            arrived(qrecv.at[m], q_rs.at[m])

        total = part[m, c] + qrecv[m]
        factor_q = lax.rsqrt(total[:, 512:513] * (1.0 / width) + EPSILON)
        factor_k = lax.rsqrt(total[:, 1664:1665] * (1.0 / width) + EPSILON)
        rr[m, 0] = jnp.broadcast_to(factor_q, (16, 128))
        rr[m, 1] = jnp.broadcast_to(factor_k, (16, 128))
        query = (total[:, :512] * factor_q).astype(BF)
        key = (total[:, 640:1152] * factor_k).astype(BF)
        value = (total[:, 1152:1664] * factor_k).astype(BF)
        qs[m] = query
        ks[m] = key
        vs[m] = value
        contexts = []
        for h in range(2):
            cols = slice(h * HEAD_DIM, (h + 1) * HEAD_DIM)
            raised = jnp.exp(dot(query[:, cols], key[:, cols], NT) * HEAD_DIM ** (-0.5))
            weight = (raised / jnp.sum(raised, axis=-1, keepdims=True)).astype(BF)
            ps[m, h] = weight.astype(F32)
            contexts.append(dot(weight, value[:, cols]).astype(BF))
        cs[m, c] = jnp.concatenate(contexts, axis=1)
        remote(cs.at[m, c], cs.at[m, c], c_ss.at[m], c_rs.at[m], other).start()
        arrived(cs.at[m, c], c_rs.at[m])

        @pl.when(s < 7)
        def _():
            context = rows(cs[m])
            for k in ORDER:
                term = dot(context, w[3, lax.rem(j + k, 4)], NT)
                if k == 0:
                    oown[m] = term
                else:
                    ost[m, k - 1] = term.astype(BF)
                    remote(
                        ost.at[m, k - 1], orecv.at[m, k - 1], o_ss.at[m, k - 1], o_rs.at[m],
                        member(k),
                    ).start()

    def advance(m):
        total = rows(xs[sel, m, j]).astype(F32) + oown[m]
        arrived(orecv.at[m], o_rs.at[m])
        for k in range(3):
            total = total + orecv[m, k].astype(F32)
        xn[m] = total.astype(BF).reshape(2, 16, 512)
        for k in ORDER:
            remote(
                xn.at[m], xs.at[sel, m, j], n_ss.at[m, k], x_rs.at[sel, m, j], member(k), s + 1
            ).start()

    def forward_step(i):
        @pl.when((i < MICRO) & (s < 4))
        def _():
            project_all(i)

        @pl.when((i < MICRO - 1) & (s == 4))
        def _():
            project_query(i + 1)

        @pl.when(((i < MICRO) & (s == 4)) | ((i < MICRO - 1) & (s > 4)))
        def _():
            project_key(i + jnp.where(s > 4, 1, 0))

        @pl.when((i < MICRO) & (s > 4))
        def _():
            project_query(i)

            @pl.when(i < MICRO - 2)
            def _():
                relay(i + 2)

        @pl.when((i > 0) & (s < 7))
        def _():
            advance(i - 1)

        @pl.when(i < MICRO)
        def _():
            attend(i)

    def to_owners(src_of, slot, m=None):
        for b in range(4):
            dst = ob.at[slot, :, t] if m is None else ob.at[slot, m, t]
            send_any(src_of(b), dst, b_ss.at[slot, b], b_rs.at[slot], owner[b])

    def owners_sent(src_of, slot):
        for b in range(4):
            sent_any(src_of(b), b_ss.at[slot, b], owner[b])

    def project_back(m):
        total = None
        for k in ORDER:
            block = block_at(k)
            arrived(xs.at[2, m, block], x_rs.at[2, m, block])
            term = dot(rows(xs[2, m, block]), w[3, block])
            total = term if total is None else total + term
        dpart[m] = total.reshape(2, 16, 512)
        remote(dpart.at[m, 1 - c], drecv.at[m], d_ss.at[m], d_rs.at[m], other).start()

    def attend_back(m):
        query, key, value = qs[m], ks[m], vs[m]
        arrived(drecv.at[m], d_rs.at[m])
        grad = (dpart[m, c] + drecv[m]).astype(BF)
        pieces = [[], [], []]
        for h in range(2):
            cols = slice(h * HEAD_DIM, (h + 1) * HEAD_DIM)
            weight = ps[m, h]
            grad_weight = dot(grad[:, cols], value[:, cols], NT)
            pieces[2].append(dot(weight.astype(BF), grad[:, cols], TN))
            inside = jnp.sum(grad_weight * weight, axis=-1, keepdims=True)
            scores = (weight * (grad_weight - inside) * HEAD_DIM ** (-0.5)).astype(BF)
            pieces[0].append(dot(scores, key[:, cols]))
            pieces[1].append(dot(scores, query[:, cols], TN))
        grads = [jnp.concatenate(piece, axis=1) for piece in pieces]
        factors = [rr[m, 0][:, :1], rr[m, 1][:, :1], rr[m, 1][:, :1]]
        for i in range(3):
            dd[m, i, c] = (grads[i] * factors[i]).astype(BF)
        remote(dd.at[m, :, c], dd.at[m, :, c], dd_ss.at[m], dd_rs.at[m], other).start()
        means = [
            jnp.sum(g * v.astype(F32), axis=-1, keepdims=True) * (1.0 / width)
            for g, v in zip(grads, (query, key, value))
        ]
        cc[m, 0, c] = jnp.broadcast_to(means[0] * factors[0] * factors[0], (16, 128))
        cc[m, 1, c] = jnp.broadcast_to((means[1] + means[2]) * factors[1] * factors[1], (16, 128))
        remote(cc.at[m, :, c], cc.at[m, :, c], cc_ss.at[m], cc_rs.at[m], other).start()
        arrived(dd.at[m, :, c], dd_rs.at[m])
        arrived(cc.at[m, :, c], cc_rs.at[m])

        def spread(pairs, stream, kinds, own, stage, recv, ss, rs):
            lefts = [rows(dd[m, i]) for i in pairs]
            shift = sum(cc[m, i].reshape(32, 128)[:, :1] for i in kinds)
            for k in ORDER:
                block = lax.rem(j + k, 4)
                term = -rows(xs[stream, m, block]).astype(F32) * shift
                for i, left in zip(pairs, lefts):
                    term = term + dot(left, w[i, block], NT)
                if k == 0:
                    own[m] = term
                else:
                    stage[m, k - 1] = term.astype(BF)
                    remote(
                        stage.at[m, k - 1], recv.at[m, k - 1], ss.at[m, k - 1], rs.at[m], member(k)
                    ).start()

        @pl.when((s > 0) & (s < 4))
        def _():
            spread((0, 1, 2), 0, (0, 1), uown, ust, urecv, u_ss, u_rs)

        @pl.when(s > 4)
        def _():
            spread((0,), 1, (0,), uown, ust, urecv, u_ss, u_rs)

        @pl.when(s >= 4)
        def _():
            spread((1, 2), 0, (1,), wown, wst, wrecv, w_ss, w_rs)

    def hand_back(m):
        for k in ORDER:
            remote(
                gn.at[m], xs.at[2, m, j], gn_ss.at[m, k], x_rs.at[2, m, j], member(k), s - 1
            ).start()

    def advance_back(m):
        total = rows(xs[2, m, j]).astype(F32) + uown[m]
        arrived(urecv.at[m], u_rs.at[m])
        for k in range(3):
            total = total + urecv[m, k].astype(F32)
        gn[m] = total.astype(BF).reshape(2, 16, 512)
        hand_back(m)

    def advance_key(m):
        arrived(wrecv.at[m], w_rs.at[m])
        total = wown[m]
        for k in range(3):
            total = total + wrecv[m, k].astype(F32)
        geout[m] = total.astype(BF).reshape(2, 16, 512)

        @pl.when(s < 7)
        def _():
            arrived(gein.at[m], e_rs.at[m])
            geout[m] = (total + rows(gein[m]).astype(F32)).astype(BF).reshape(2, 16, 512)

        @pl.when(s > 4)
        def _():
            remote(geout.at[m], gein.at[m], e_ss.at[m], e_rs.at[m], (d, p), s - 1).start()

        @pl.when(s == 4)
        def _():
            gn[m] = geout[m]
            hand_back(m)

    def backward_step(i):
        @pl.when(i < MICRO)
        def _():
            project_back(i)

        @pl.when((i > 0) & (s > 0) & (s != 4))
        def _():
            advance_back(i - 1)

        @pl.when((i > 0) & (s == 4))
        def _():
            advance_key(i - 1)

        @pl.when(i < MICRO)
        def _():
            attend_back(i)

            @pl.when(s == 0)
            def _():
                to_owners(lambda b: xs.at[2, i, b], 2, i)
                for k in range(3):
                    to_owners(lambda b: dd.at[i, k], 4 + k, i)

        @pl.when((i > 0) & (s > 4))
        def _():
            advance_key(i - 1)

    @pl.when(s == 4)
    def _():
        project_query(0)

    @pl.when(s > 4)
    def _():
        relay(0)
        relay(1)
        project_key(0)

    def step(n, carry):
        @pl.when(n <= MICRO)
        def _():
            forward_step(n)

        @pl.when(n == MICRO + 1)
        def _():
            to_owners(lambda b: xs.at[sel, :, b], 0)

            @pl.when(decoder)
            def _():
                to_owners(lambda b: xs.at[0, :, b], 1)

            to_owners(lambda b: cs, 3)

        back = n - jnp.where(s == 7, 0, MICRO + 1)

        @pl.when((back >= 0) & (back <= MICRO))
        def _():
            backward_step(back)

        return carry

    lax.fori_loop(0, 2 * MICRO + 2, step, 0)

    @pl.when(s > 0)
    def _():
        to_owners(lambda b: xs.at[2, :, b], 2)
        for i in range(3):
            to_owners(lambda b: dd.at[:, i], 4 + i)

    key_slot = jnp.where(decoder, 1, 0)
    arrived(ob.at[3], b_rs.at[3])
    arrived(ob.at[2], b_rs.at[2])
    out_ref[3] = dot(ob[2].reshape(512, 512), ob[3].reshape(512, 512), TN)
    arrived(ob.at[0], b_rs.at[0])

    @pl.when(decoder)
    def _():
        arrived(ob.at[1], b_rs.at[1])

    for i in range(3):
        arrived(ob.at[4 + i], b_rs.at[4 + i])
        left = ob[0] if i == 0 else ob[key_slot]
        out_ref[i] = dot(left.reshape(512, 512), ob[4 + i].reshape(512, 512), TN)

    @pl.when(starts)
    def _():
        for m in range(MICRO):
            for k in range(4):
                sent_any(start_ref.at[m], i_ss.at[m, k], start_to[k])

    for mat in range(4):
        sent_any(weights_ref.at[mat], ga_ss.at[mat], collector)
        arrived(w.at[mat, 0], gc_ss.at[mat])

        @pl.when(inner)
        def _():
            for k in range(2):
                arrived(pair(mat, 0), gb_ss.at[mat, k])

    owners_sent(lambda b: xs.at[sel, :, b], 0)

    @pl.when(decoder)
    def _():
        owners_sent(lambda b: xs.at[0, :, b], 1)

    owners_sent(lambda b: xs.at[2, :, b], 2)
    owners_sent(lambda b: cs, 3)
    for i in range(3):
        owners_sent(lambda b: dd.at[:, i], 4 + i)

    def finish(m, carry):
        @pl.when(decoder)
        def _():
            arrived(part.at[m, 0, :, pl.ds(0, 640)], q_ss.at[m])
            arrived(part.at[m, 0, :, pl.ds(640, 1152)], kv_ss.at[m])

        @pl.when(jnp.logical_not(decoder))
        def _():
            arrived(part.at[m, 0], q_ss.at[m])

        arrived(cs.at[m, 0], c_ss.at[m])
        arrived(dpart.at[m, 0], d_ss.at[m])
        arrived(dd.at[m, :, 0], dd_ss.at[m])
        arrived(cc.at[m, :, 0], cc_ss.at[m])

        @pl.when(decoder & (s < 7))
        def _():
            arrived(xs.at[0, m, 0], f_ss.at[m])

        @pl.when(s > 4)
        def _():
            for k in range(3):
                arrived(xs.at[0, m, 0], fp_ss.at[m, k])

        @pl.when(s < 7)
        def _():
            for k in range(3):
                arrived(ost.at[m, k], o_ss.at[m, k])
            for k in range(4):
                arrived(xn.at[m], n_ss.at[m, k])

        @pl.when((s > 0) & (s != 4))
        def _():
            for k in range(3):
                arrived(ust.at[m, k], u_ss.at[m, k])

        @pl.when(s > 0)
        def _():
            for k in range(4):
                arrived(gn.at[m], gn_ss.at[m, k])

        @pl.when(s >= 4)
        def _():
            for k in range(3):
                arrived(wst.at[m, k], w_ss.at[m, k])

        @pl.when(s > 4)
        def _():
            arrived(geout.at[m], e_ss.at[m])

        return carry

    lax.fori_loop(0, MICRO, finish, 0)


def per_device(enc_input, dec_input, cotangent, target_lengths, weights):
    section = lax.axis_index("section")
    micro_count, sequences, seq_length, feature_part = enc_input.shape
    scale = lax.rsqrt(jnp.float32(micro_count * lax.axis_size("dp") * sequences * seq_length))
    offsets = lax.broadcasted_iota(jnp.int32, (micro_count, sequences, seq_length), 2)
    live = (offsets < target_lengths[:, :, None]).astype(F32)
    seed = (cotangent.astype(F32) * live[..., None] * scale).astype(BF)
    start = jnp.where(section == 0, enc_input, jnp.where(section == 4, dec_input, seed))
    start = start.reshape(MICRO, 16, 2, 512).transpose(0, 2, 1, 3)
    dma = pltpu.SemaphoreType.DMA
    tile = (2, 16, 512)
    scratch = [
        pltpu.VMEM((4, 4, 512, 512), BF),
        pltpu.VMEM((3, MICRO, 4) + tile, BF),
        pltpu.VMEM((MICRO, 2, 16, 1792), F32),
        pltpu.VMEM((MICRO, 16, 1792), F32),
        pltpu.VMEM((MICRO, 16, 512), BF),
        pltpu.VMEM((MICRO, 16, 512), BF),
        pltpu.VMEM((MICRO, 16, 512), BF),
        pltpu.VMEM((MICRO, 2, 16, 16), F32),
        pltpu.VMEM((MICRO, 2, 16, 128), F32),
        pltpu.VMEM((MICRO,) + tile, BF),
        pltpu.VMEM((MICRO, 32, 512), F32),
        pltpu.VMEM((MICRO, 3, 32, 512), BF),
        pltpu.VMEM((MICRO, 3, 32, 512), BF),
        pltpu.VMEM((MICRO,) + tile, BF),
        pltpu.VMEM((MICRO,) + tile, F32),
        pltpu.VMEM((MICRO, 16, 512), F32),
        pltpu.VMEM((MICRO, 3) + tile, BF),
        pltpu.VMEM((MICRO, 2, 2, 16, 128), F32),
        pltpu.VMEM((MICRO, 32, 512), F32),
        pltpu.VMEM((MICRO, 3, 32, 512), BF),
        pltpu.VMEM((MICRO, 3, 32, 512), BF),
        pltpu.VMEM((MICRO, 32, 512), F32),
        pltpu.VMEM((MICRO, 3, 32, 512), BF),
        pltpu.VMEM((MICRO, 3, 32, 512), BF),
        pltpu.VMEM((MICRO,) + tile, BF),
        pltpu.VMEM((MICRO,) + tile, BF),
        pltpu.VMEM((MICRO,) + tile, BF),
        pltpu.VMEM((7, MICRO, 4) + tile, BF),
        dma((4,)), dma((4,)),
        dma((4, 2)), dma((4,)),
        dma((4,)), dma((4,)),
        dma((MICRO, 4)), dma((3, MICRO, 4)),
        dma((MICRO,)), dma((MICRO, 3)),
        dma((MICRO,)), dma((MICRO,)),
        dma((MICRO,)), dma((MICRO,)),
        dma((MICRO,)), dma((MICRO,)),
        dma((MICRO, 3)), dma((MICRO,)),
        dma((MICRO, 4)),
        dma((MICRO,)), dma((MICRO,)),
        dma((MICRO,)), dma((MICRO,)),
        dma((MICRO,)), dma((MICRO,)),
        dma((MICRO, 3)), dma((MICRO,)),
        dma((MICRO, 3)), dma((MICRO,)),
        dma((MICRO,)), dma((MICRO,)),
        dma((MICRO, 4)),
        dma((7, 4)), dma((7,)),
    ]
    grads = pl.pallas_call(
        functools.partial(layer_kernel, 4096),
        out_shape=jax.ShapeDtypeStruct((4, 512, 512), F32),
        in_specs=[pl.BlockSpec(memory_space=pltpu.VMEM), pl.BlockSpec(memory_space=pl.ANY)],
        out_specs=pl.BlockSpec(memory_space=pltpu.VMEM),
        scratch_shapes=scratch,
        compiler_params=pltpu.CompilerParams(
            collective_id=0, has_side_effects=True, vmem_limit_bytes=48 << 20
        ),
        name="layers",
    )(start, weights[0])
    return grads[None]


def solution(mesh):
    in_specs = (
        P(None, "dp", None, "mp"),
        P(None, "dp", None, "mp"),
        P(None, "dp", None, "mp"),
        P(None, "dp"),
        P("section", None, "dp", "mp"),
    )
    return jax.shard_map(
        per_device,
        mesh=mesh,
        in_specs=in_specs,
        out_specs=P("section", None, "dp", "mp"),
        check_vma=False,
    )
```

```python
import functools

import jax
import jax.numpy as jnp
from jax import lax
from jax.experimental import pallas as pl
from jax.experimental.pallas import tpu as pltpu
from jax.sharding import PartitionSpec as P

HEAD_DIM = 256
EPSILON = 1e-06
MICRO = 4
BF = jnp.bfloat16
F32 = jnp.float32
MESH = pl.DeviceIdType.MESH
ORDER = (2, 1, 3, 0)
NT = (((1,), (1,)), ((), ()))
NN = (((1,), (0,)), ((), ()))
TN = (((0,), (0,)), ((), ()))


def dot(a, b, dims=NN):
    return lax.dot_general(a, b, dims, preferred_element_type=F32)


def layer_kernel(
    width, loss_scale,
    lengths_ref, enc_ref, dec_ref, cot_ref, weights_ref, out_ref,
    w, xs, seed, seed_in, part, qrecv, qs, ks, vs, ps, rr, cs, oown, ost, orecv, xn,
    dpart, drecv, dd, cc, uown, ust, urecv, wown, wst, wrecv, gn, gein, geout, ob,
    s_sem, ga_ss, ga_rs, gb_ss, gb_rs, gc_ss, gc_rs, i_ss, x_rs, f_ss, fp_ss, q_ss, q_rs, kv_ss, kv_rs,
    c_ss, c_rs, o_ss, o_rs, n_ss,
    d_ss, d_rs, dd_ss, dd_rs, cc_ss, cc_rs, u_ss, u_rs, w_ss, w_rs, e_ss, e_rs, gn_ss,
    b_ss, b_rs,
):
    s = lax.axis_index("section")
    d = lax.axis_index("dp")
    p = lax.axis_index("mp")
    t = d // 2
    c = lax.rem(p, 2)
    j = 2 * (p // 2) + lax.rem(d, 2)
    odd = lax.rem(t, 2)
    decoder = s >= 4
    sel = jnp.where(decoder, 1, 0)
    starts = (s == 0) | (s == 4) | (s == 7)
    other = (d, p + 1 - 2 * c)

    def place(tt, jj, ccc):
        return 2 * tt + lax.rem(jj, 2), 2 * (jj // 2) + ccc

    def member(k):
        return place(t, lax.rem(j + k, 4), c)

    def column(tt):
        return 2 * tt + lax.rem(d, 2), p

    collector = place(t, p, d // 4)
    inner = t // 2 == c
    beside = column(t + 1 - 2 * odd)
    across = column(lax.rem(t + 3 - 2 * odd, 4))
    senders = [place(k, p, d // 4) for k in range(4)]
    owner = [(4 * c + b, j) for b in range(4)]
    start_to = [place(t, jnp.int32(k), p // 2) for k in range(4)]
    start_from = [(2 * t + a, 2 * c + e) for a in range(2) for e in range(2)]

    def same(dev):
        return (dev[0] == d) & (dev[1] == p)

    def remote(src, dst, ss, rs, dev, sec=None):
        ids = {"dp": dev[0], "mp": dev[1]}
        if sec is not None:
            ids["section"] = sec
        return pltpu.make_async_remote_copy(
            src_ref=src, dst_ref=dst, send_sem=ss, recv_sem=rs, device_id=ids, device_id_type=MESH
        )

    def arrived(ref, sem):
        pltpu.make_async_copy(ref, ref, sem).wait()

    def send_any(src, dst, ss, rs, dev):
        here = same(dev)

        @pl.when(here)
        def _():
            pltpu.make_async_copy(src, dst, rs).start()

        @pl.when(jnp.logical_not(here))
        def _():
            remote(src, dst, ss, rs, dev).start()

    def sent_any(src, ss, dev):
        @pl.when(jnp.logical_not(same(dev)))
        def _():
            arrived(src, ss)

    bar = pltpu.get_barrier_semaphore()

    def greet(dev, sec=None):
        ids = {"dp": dev[0], "mp": dev[1]}
        if sec is not None:
            ids["section"] = sec
        pl.semaphore_signal(bar, inc=1, device_id=ids, device_id_type=MESH)

    def greet_other(dev):
        @pl.when(jnp.logical_not(same(dev)))
        def _():
            greet(dev)

    greet(other)
    greet(beside)
    greet(across)
    for k in range(1, 4):
        greet(member(k))

    @pl.when(s > 0)
    def _():
        for k in range(4):
            greet(member(k), s - 1)

    @pl.when(s < 7)
    def _():
        for k in range(4):
            greet(member(k), s + 1)

    for dev in senders:
        greet_other(dev)

    @pl.when(inner)
    def _():
        for e in range(2):
            greet_other((2 * t + e, j))

    @pl.when(starts)
    def _():
        for dev in start_from:
            greet_other(dev)

    def others(devs):
        return sum(jnp.where(same(dev), 0, 1) for dev in devs)

    count = 6 + jnp.where(s > 0, 4, 0) + jnp.where(s < 7, 4, 0) + others(owner)
    count = count + others([collector]) + jnp.where(starts, others(start_to), 0)
    pl.semaphore_wait(bar, count)

    def shards(piece, first, number):
        return w.at[piece // 2, pl.ds(first, number), pl.ds(256 * lax.rem(piece, 2), 256)]

    def shard(piece, which):
        return w.at[piece // 2, which, pl.ds(256 * lax.rem(piece, 2), 256)]

    def own_shard(piece):
        return weights_ref.at[0, piece // 2, pl.ds(256 * lax.rem(piece, 2), 256)]

    def give(piece, carry):
        send_any(
            own_shard(piece), shard(piece, lax.rem(d, 4)), ga_ss.at[piece], ga_rs.at[piece],
            collector,
        )
        return carry

    lax.fori_loop(0, 8, give, 0)

    def begin(src_of, stream):
        for m in range(MICRO):
            for k in range(4):
                for e in range(2):
                    block = 2 * lax.rem(p, 2) + e
                    send_any(
                        src_of(m, e), xs.at[stream, m, block, lax.rem(d, 2)],
                        i_ss.at[m, k], x_rs.at[stream, m, block], start_to[k],
                    )

    @pl.when(s == 0)
    def _():
        begin(lambda m, e: enc_ref.at[m, 0, :, pl.ds(512 * e, 512)], 0)

    @pl.when(s == 4)
    def _():
        begin(lambda m, e: dec_ref.at[m, 0, :, pl.ds(512 * e, 512)], 1)

    @pl.when(s == 7)
    def _():
        loss = pltpu.make_async_copy(cot_ref.at[:, 0], seed_in, s_sem)
        loss.start()
        loss.wait()
        for m in range(MICRO):
            offsets = lax.broadcasted_iota(jnp.int32, (16, 1024), 0)
            live = jnp.where(offsets < lengths_ref[m, 0], loss_scale, 0.0)
            value = (seed_in[m].astype(F32) * live).astype(BF)
            for e in range(2):
                seed[m, e] = value[:, 512 * e:512 * e + 512]
        begin(lambda m, e: seed.at[m, e], 2)

    def pass_on(piece):
        arrived(shards(piece, 2 * (1 - odd), 2), gb_rs.at[piece])
        half = shard(piece, 2 * (1 - odd))
        remote(half, half, gc_ss.at[piece], gc_rs.at[piece], across).start()

    def collected(piece):
        mine = shards(piece, 2 * odd, 2)
        arrived(mine, ga_rs.at[piece])
        remote(mine, mine, gb_ss.at[piece, 0], gb_rs.at[piece], beside).start()
        remote(mine, mine, gb_ss.at[piece, 1], gb_rs.at[piece], across).start()

    def swap(piece):
        arrived(shards(piece, 2 * (1 - odd), 2), gb_rs.at[piece])
        half = shard(piece, 2 * (1 - odd) + 1)
        remote(half, half, gc_ss.at[piece], gc_rs.at[piece], beside).start()

    def swapped(piece):
        arrived(shards(piece, 2 * odd, 2), gc_rs.at[piece])

    def gather_most():
        @pl.when(inner)
        def _():
            def one(piece, carry):
                collected(piece)

                @pl.when(piece > 0)
                def _():
                    pass_on(piece - 1)

                return carry

            lax.fori_loop(0, 7, one, 0)
            collected(7)

        @pl.when(jnp.logical_not(inner))
        def _():
            def one(piece, carry):
                swap(piece)
                return carry

            def other_one(piece, carry):
                swapped(piece)
                return carry

            lax.fori_loop(0, 6, one, 0)
            lax.fori_loop(0, 6, other_one, 0)

    def gather_one(piece):
        @pl.when(inner)
        def _():
            pass_on(piece)

        @pl.when(jnp.logical_not(inner))
        def _():
            swap(piece)

    gather_most()

    def rows(value):
        return value.reshape(32, 512)

    def block_at(k):
        return lax.rem(j + 4 - k, 4)

    def project(m, stream, mats, start, ss, rs, relayed=None):
        sums = [None] * len(mats)
        squares = None
        for k in ORDER:
            block = block_at(k)
            if k == 0 and relayed is not None:
                @pl.when(jnp.logical_not(relayed))
                def _():
                    arrived(xs.at[stream, m, block], x_rs.at[stream, m, block])
            else:
                arrived(xs.at[stream, m, block], x_rs.at[stream, m, block])
            left = rows(xs[stream, m, block])
            wide = left.astype(F32)
            square = jnp.sum(wide * wide, axis=-1, keepdims=True)
            squares = square if squares is None else squares + square
            for i, mat in enumerate(mats):
                term = dot(left, w[mat, block])
                sums[i] = term if sums[i] is None else sums[i] + term
        squares = jnp.broadcast_to(squares, (32, 128)).reshape(2, 16, 128)
        for i, mat in enumerate(mats):
            first = (0, 640, 1152)[mat]
            part[m, :, :, first:first + 512] = sums[i].reshape(2, 16, 512)
        if 0 in mats:
            part[m, :, :, 512:640] = squares
        if 1 in mats:
            part[m, :, :, 1664:1792] = squares
        cols = pl.ds(*start)
        remote(part.at[m, 1 - c, :, cols], qrecv.at[m, :, cols], ss.at[m], rs.at[m], other).start()

    def project_all(m):
        project(m, 0, (0, 1, 2), (0, 1792), q_ss, q_rs)

    def project_query(m):
        project(m, 1, (0,), (0, 640), q_ss, q_rs)

    def project_key(m):
        project(m, 0, (1, 2), (640, 1152), kv_ss, kv_rs, s > 4)

        @pl.when(s == 4)
        def _():
            onward(m)

    def onward(m):
        remote(
            xs.at[0, m, j], xs.at[0, m, j], f_ss.at[m], x_rs.at[0, m, j], (d, p), s + 1
        ).start()

    def relay(m):
        arrived(xs.at[0, m, j], x_rs.at[0, m, j])

        @pl.when(s < 7)
        def _():
            onward(m)

        for k in (2, 1, 3):
            remote(
                xs.at[0, m, j], xs.at[0, m, j], fp_ss.at[m, k - 1], x_rs.at[0, m, j], member(k)
            ).start()

    def attend(m):
        @pl.when(decoder)
        def _():
            arrived(qrecv.at[m, :, pl.ds(0, 640)], q_rs.at[m])
            arrived(qrecv.at[m, :, pl.ds(640, 1152)], kv_rs.at[m])

        @pl.when(jnp.logical_not(decoder))
        def _():
            arrived(qrecv.at[m], q_rs.at[m])

        total = part[m, c] + qrecv[m]
        factor_q = lax.rsqrt(total[:, 512:513] * (1.0 / width) + EPSILON)
        factor_k = lax.rsqrt(total[:, 1664:1665] * (1.0 / width) + EPSILON)
        rr[m, 0] = jnp.broadcast_to(factor_q, (16, 128))
        rr[m, 1] = jnp.broadcast_to(factor_k, (16, 128))
        query = (total[:, :512] * factor_q).astype(BF)
        key = (total[:, 640:1152] * factor_k).astype(BF)
        value = (total[:, 1152:1664] * factor_k).astype(BF)
        qs[m] = query
        ks[m] = key
        vs[m] = value
        contexts = []
        for h in range(2):
            cols = slice(h * HEAD_DIM, (h + 1) * HEAD_DIM)
            raised = jnp.exp(dot(query[:, cols], key[:, cols], NT) * HEAD_DIM ** (-0.5))
            weight = (raised / jnp.sum(raised, axis=-1, keepdims=True)).astype(BF)
            ps[m, h] = weight.astype(F32)
            contexts.append(dot(weight, value[:, cols]).astype(BF))
        cs[m, c] = jnp.concatenate(contexts, axis=1)
        remote(cs.at[m, c], cs.at[m, c], c_ss.at[m], c_rs.at[m], other).start()

    def output(m):
        arrived(cs.at[m, c], c_rs.at[m])

        @pl.when(s < 7)
        def _():
            context = rows(cs[m])
            for k in ORDER:
                term = dot(context, w[3, lax.rem(j + k, 4)], NT)
                if k == 0:
                    oown[m] = term
                else:
                    ost[m, k - 1] = term.astype(BF)
                    remote(
                        ost.at[m, k - 1], orecv.at[m, k - 1], o_ss.at[m, k - 1], o_rs.at[m],
                        member(k),
                    ).start()

    def advance(m):
        total = rows(xs[sel, m, j]).astype(F32) + oown[m]
        arrived(orecv.at[m], o_rs.at[m])
        for k in range(3):
            total = total + orecv[m, k].astype(F32)
        xn[m] = total.astype(BF).reshape(2, 16, 512)
        for k in ORDER:
            remote(
                xn.at[m], xs.at[sel, m, j], n_ss.at[m, k], x_rs.at[sel, m, j], member(k), s + 1
            ).start()

    def forward_step(i):
        @pl.when((i < MICRO) & (s < 4) & (s > 0))
        def _():
            project_all(i)

        @pl.when((i < MICRO - 1) & (s == 4))
        def _():
            project_query(i + 1)

        @pl.when(((i < MICRO) & (s == 4)) | ((i < MICRO - 1) & (s > 4)))
        def _():
            project_key(i + jnp.where(s > 4, 1, 0))

        @pl.when((i < MICRO) & (s > 4))
        def _():
            project_query(i)

            @pl.when(i < MICRO - 2)
            def _():
                relay(i + 2)

        @pl.when((i > 0) & (s < 7))
        def _():
            advance(i - 1)

        @pl.when(i < MICRO)
        def _():
            @pl.when(s > 0)
            def _():
                attend(i)

            output(i)

    def to_owners(src_of, slot, m=None):
        for b in range(4):
            dst = ob.at[slot, :, t] if m is None else ob.at[slot, m, t]
            send_any(src_of(b), dst, b_ss.at[slot, b], b_rs.at[slot], owner[b])

    def owners_sent(src_of, slot):
        for b in range(4):
            sent_any(src_of(b), b_ss.at[slot, b], owner[b])

    def project_back(m):
        total = None
        for k in ORDER:
            block = block_at(k)
            arrived(xs.at[2, m, block], x_rs.at[2, m, block])
            term = dot(rows(xs[2, m, block]), w[3, block])
            total = term if total is None else total + term
        dpart[m] = total.reshape(2, 16, 512)
        remote(dpart.at[m, 1 - c], drecv.at[m], d_ss.at[m], d_rs.at[m], other).start()

    def attend_back(m):
        query, key, value = qs[m], ks[m], vs[m]
        arrived(drecv.at[m], d_rs.at[m])
        grad = (dpart[m, c] + drecv[m]).astype(BF)
        pieces = [[], [], []]
        for h in range(2):
            cols = slice(h * HEAD_DIM, (h + 1) * HEAD_DIM)
            weight = ps[m, h]
            grad_weight = dot(grad[:, cols], value[:, cols], NT)
            pieces[2].append(dot(weight.astype(BF), grad[:, cols], TN))
            inside = jnp.sum(grad_weight * weight, axis=-1, keepdims=True)
            scores = (weight * (grad_weight - inside) * HEAD_DIM ** (-0.5)).astype(BF)
            pieces[0].append(dot(scores, key[:, cols]))
            pieces[1].append(dot(scores, query[:, cols], TN))
        grads = [jnp.concatenate(piece, axis=1) for piece in pieces]
        factors = [rr[m, 0][:, :1], rr[m, 1][:, :1], rr[m, 1][:, :1]]
        for i in range(3):
            dd[m, i, c] = (grads[i] * factors[i]).astype(BF)
        remote(dd.at[m, :, c], dd.at[m, :, c], dd_ss.at[m], dd_rs.at[m], other).start()
        means = [
            jnp.sum(g * v.astype(F32), axis=-1, keepdims=True) * (1.0 / width)
            for g, v in zip(grads, (query, key, value))
        ]
        cc[m, 0, c] = jnp.broadcast_to(means[0] * factors[0] * factors[0], (16, 128))
        cc[m, 1, c] = jnp.broadcast_to((means[1] + means[2]) * factors[1] * factors[1], (16, 128))
        remote(cc.at[m, :, c], cc.at[m, :, c], cc_ss.at[m], cc_rs.at[m], other).start()
        arrived(dd.at[m, :, c], dd_rs.at[m])
        arrived(cc.at[m, :, c], cc_rs.at[m])

        def spread(pairs, stream, kinds, own, stage, recv, ss, rs):
            lefts = [rows(dd[m, i]) for i in pairs]
            shift = sum(cc[m, i].reshape(32, 128)[:, :1] for i in kinds)
            for k in ORDER:
                block = lax.rem(j + k, 4)
                term = -rows(xs[stream, m, block]).astype(F32) * shift
                for i, left in zip(pairs, lefts):
                    term = term + dot(left, w[i, block], NT)
                if k == 0:
                    own[m] = term
                else:
                    stage[m, k - 1] = term.astype(BF)
                    remote(
                        stage.at[m, k - 1], recv.at[m, k - 1], ss.at[m, k - 1], rs.at[m], member(k)
                    ).start()

        @pl.when((s > 0) & (s < 4))
        def _():
            spread((0, 1, 2), 0, (0, 1), uown, ust, urecv, u_ss, u_rs)

        @pl.when(s > 4)
        def _():
            spread((0,), 1, (0,), uown, ust, urecv, u_ss, u_rs)

        @pl.when(s >= 4)
        def _():
            spread((1, 2), 0, (1,), wown, wst, wrecv, w_ss, w_rs)

    def hand_back(m):
        for k in ORDER:
            remote(
                gn.at[m], xs.at[2, m, j], gn_ss.at[m, k], x_rs.at[2, m, j], member(k), s - 1
            ).start()

    def advance_back(m):
        total = rows(xs[2, m, j]).astype(F32) + uown[m]
        arrived(urecv.at[m], u_rs.at[m])
        for k in range(3):
            total = total + urecv[m, k].astype(F32)
        gn[m] = total.astype(BF).reshape(2, 16, 512)
        hand_back(m)

    def advance_key(m):
        arrived(wrecv.at[m], w_rs.at[m])
        total = wown[m]
        for k in range(3):
            total = total + wrecv[m, k].astype(F32)
        geout[m] = total.astype(BF).reshape(2, 16, 512)

        @pl.when(s < 7)
        def _():
            arrived(gein.at[m], e_rs.at[m])
            geout[m] = (total + rows(gein[m]).astype(F32)).astype(BF).reshape(2, 16, 512)

        @pl.when(s > 4)
        def _():
            remote(geout.at[m], gein.at[m], e_ss.at[m], e_rs.at[m], (d, p), s - 1).start()

        @pl.when(s == 4)
        def _():
            gn[m] = geout[m]
            hand_back(m)

    def backward_step(i):
        @pl.when(i < MICRO)
        def _():
            project_back(i)

        @pl.when((i > 0) & (s > 0) & (s != 4))
        def _():
            advance_back(i - 1)

        @pl.when((i > 0) & (s == 4))
        def _():
            advance_key(i - 1)

        @pl.when(i < MICRO)
        def _():
            attend_back(i)

            @pl.when(s < 2)
            def _():
                to_owners(lambda b: xs.at[2, i, b], 2, i)
                for k in range(3):
                    to_owners(lambda b: dd.at[i, k], 4 + k, i)

        @pl.when((i > 0) & (s > 4))
        def _():
            advance_key(i - 1)

    def early(what):
        @pl.when(s == 0)
        def _():
            def one(m, carry):
                what(m)
                return carry

            lax.fori_loop(0, MICRO, one, 0)

    early(project_all)
    gather_one(6)
    early(attend)
    gather_one(7)

    @pl.when(jnp.logical_not(inner))
    def _():
        swapped(6)
        swapped(7)

    @pl.when(s == 4)
    def _():
        project_query(0)

    @pl.when(s > 4)
    def _():
        relay(0)
        relay(1)
        project_key(0)

    def step(n, carry):
        @pl.when(n <= MICRO)
        def _():
            forward_step(n)

        @pl.when(n == MICRO + 1)
        def _():
            to_owners(lambda b: xs.at[sel, :, b], 0)

            @pl.when(decoder)
            def _():
                to_owners(lambda b: xs.at[0, :, b], 1)

            to_owners(lambda b: cs, 3)

        back = n - jnp.where(s == 7, 0, MICRO + 1)

        @pl.when((back >= 0) & (back <= MICRO))
        def _():
            backward_step(back)

        return carry

    lax.fori_loop(0, 2 * MICRO + 2, step, 0)

    @pl.when(s > 1)
    def _():
        to_owners(lambda b: xs.at[2, :, b], 2)
        for i in range(3):
            to_owners(lambda b: dd.at[:, i], 4 + i)

    key_slot = jnp.where(decoder, 1, 0)
    arrived(ob.at[3], b_rs.at[3])
    arrived(ob.at[2], b_rs.at[2])
    out_ref[3] = dot(ob[2].reshape(512, 512), ob[3].reshape(512, 512), TN).astype(BF)
    arrived(ob.at[0], b_rs.at[0])

    @pl.when(decoder)
    def _():
        arrived(ob.at[1], b_rs.at[1])

    for i in range(3):
        arrived(ob.at[4 + i], b_rs.at[4 + i])
        left = ob[0] if i == 0 else ob[key_slot]
        out_ref[i] = dot(left.reshape(512, 512), ob[4 + i].reshape(512, 512), TN).astype(BF)

    @pl.when(starts)
    def _():
        for m in range(MICRO):
            for k in range(4):
                sent_any(seed.at[m], i_ss.at[m, k], start_to[k])

    def given(piece, carry):
        sent_any(own_shard(piece), ga_ss.at[piece], collector)
        arrived(shard(piece, 0), gc_ss.at[piece])

        @pl.when(inner)
        def _():
            for k in range(2):
                arrived(shards(piece, 0, 2), gb_ss.at[piece, k])

        return carry

    lax.fori_loop(0, 8, given, 0)

    owners_sent(lambda b: xs.at[sel, :, b], 0)

    @pl.when(decoder)
    def _():
        owners_sent(lambda b: xs.at[0, :, b], 1)

    owners_sent(lambda b: xs.at[2, :, b], 2)
    owners_sent(lambda b: cs, 3)
    for i in range(3):
        owners_sent(lambda b: dd.at[:, i], 4 + i)

    def finish(m, carry):
        @pl.when(decoder)
        def _():
            arrived(part.at[m, 0, :, pl.ds(0, 640)], q_ss.at[m])
            arrived(part.at[m, 0, :, pl.ds(640, 1152)], kv_ss.at[m])

        @pl.when(jnp.logical_not(decoder))
        def _():
            arrived(part.at[m, 0], q_ss.at[m])

        arrived(cs.at[m, 0], c_ss.at[m])
        arrived(dpart.at[m, 0], d_ss.at[m])
        arrived(dd.at[m, :, 0], dd_ss.at[m])
        arrived(cc.at[m, :, 0], cc_ss.at[m])

        @pl.when(decoder & (s < 7))
        def _():
            arrived(xs.at[0, m, 0], f_ss.at[m])

        @pl.when(s > 4)
        def _():
            for k in range(3):
                arrived(xs.at[0, m, 0], fp_ss.at[m, k])

        @pl.when(s < 7)
        def _():
            for k in range(3):
                arrived(ost.at[m, k], o_ss.at[m, k])
            for k in range(4):
                arrived(xn.at[m], n_ss.at[m, k])

        @pl.when((s > 0) & (s != 4))
        def _():
            for k in range(3):
                arrived(ust.at[m, k], u_ss.at[m, k])

        @pl.when(s > 0)
        def _():
            for k in range(4):
                arrived(gn.at[m], gn_ss.at[m, k])

        @pl.when(s >= 4)
        def _():
            for k in range(3):
                arrived(wst.at[m, k], w_ss.at[m, k])

        @pl.when(s > 4)
        def _():
            arrived(geout.at[m], e_ss.at[m])

        return carry

    lax.fori_loop(0, MICRO, finish, 0)


def per_device(enc_input, dec_input, cotangent, target_lengths, weights):
    tokens = MICRO * lax.axis_size("dp") * enc_input.shape[1] * enc_input.shape[2]
    dma = pltpu.SemaphoreType.DMA
    tile = (2, 16, 512)
    scratch = [
        pltpu.VMEM((4, 4, 512, 512), BF),
        pltpu.VMEM((3, MICRO, 4) + tile, BF),
        pltpu.VMEM((MICRO, 2, 16, 512), BF),
        pltpu.VMEM((MICRO, 16, 1024), BF),
        pltpu.VMEM((MICRO, 2, 16, 1792), F32),
        pltpu.VMEM((MICRO, 16, 1792), F32),
        pltpu.VMEM((MICRO, 16, 512), BF),
        pltpu.VMEM((MICRO, 16, 512), BF),
        pltpu.VMEM((MICRO, 16, 512), BF),
        pltpu.VMEM((MICRO, 2, 16, 16), F32),
        pltpu.VMEM((MICRO, 2, 16, 128), F32),
        pltpu.VMEM((MICRO,) + tile, BF),
        pltpu.VMEM((MICRO, 32, 512), F32),
        pltpu.VMEM((MICRO, 3, 32, 512), BF),
        pltpu.VMEM((MICRO, 3, 32, 512), BF),
        pltpu.VMEM((MICRO,) + tile, BF),
        pltpu.VMEM((MICRO,) + tile, F32),
        pltpu.VMEM((MICRO, 16, 512), F32),
        pltpu.VMEM((MICRO, 3) + tile, BF),
        pltpu.VMEM((MICRO, 2, 2, 16, 128), F32),
        pltpu.VMEM((MICRO, 32, 512), F32),
        pltpu.VMEM((MICRO, 3, 32, 512), BF),
        pltpu.VMEM((MICRO, 3, 32, 512), BF),
        pltpu.VMEM((MICRO, 32, 512), F32),
        pltpu.VMEM((MICRO, 3, 32, 512), BF),
        pltpu.VMEM((MICRO, 3, 32, 512), BF),
        pltpu.VMEM((MICRO,) + tile, BF),
        pltpu.VMEM((MICRO,) + tile, BF),
        pltpu.VMEM((MICRO,) + tile, BF),
        pltpu.VMEM((7, MICRO, 4) + tile, BF),
        dma,
        dma((8,)), dma((8,)),
        dma((8, 2)), dma((8,)),
        dma((8,)), dma((8,)),
        dma((MICRO, 4)), dma((3, MICRO, 4)),
        dma((MICRO,)), dma((MICRO, 3)),
        dma((MICRO,)), dma((MICRO,)),
        dma((MICRO,)), dma((MICRO,)),
        dma((MICRO,)), dma((MICRO,)),
        dma((MICRO, 3)), dma((MICRO,)),
        dma((MICRO, 4)),
        dma((MICRO,)), dma((MICRO,)),
        dma((MICRO,)), dma((MICRO,)),
        dma((MICRO,)), dma((MICRO,)),
        dma((MICRO, 3)), dma((MICRO,)),
        dma((MICRO, 3)), dma((MICRO,)),
        dma((MICRO,)), dma((MICRO,)),
        dma((MICRO, 4)),
        dma((7, 4)), dma((7,)),
    ]
    grads = pl.pallas_call(
        functools.partial(layer_kernel, 4096, float(tokens) ** (-0.5)),
        out_shape=jax.ShapeDtypeStruct((4, 512, 512), BF),
        in_specs=[pl.BlockSpec(memory_space=pltpu.SMEM)] + [pl.BlockSpec(memory_space=pl.ANY)] * 4,
        out_specs=pl.BlockSpec(memory_space=pltpu.VMEM),
        scratch_shapes=scratch,
        compiler_params=pltpu.CompilerParams(
            collective_id=0, has_side_effects=True, vmem_limit_bytes=60 << 20
        ),
        name="layers",
    )(target_lengths, enc_input, dec_input, cotangent, weights)
    return grads[None].astype(F32)


def solution(mesh):
    in_specs = (
        P(None, "dp", None, "mp"),
        P(None, "dp", None, "mp"),
        P(None, "dp", None, "mp"),
        P(None, "dp"),
        P("section", None, "dp", "mp"),
    )
    return jax.shard_map(
        per_device,
        mesh=mesh,
        in_specs=in_specs,
        out_specs=P("section", None, "dp", "mp"),
        check_vma=False,
    )
```

```python
import functools

import jax
import jax.numpy as jnp
from jax import lax
from jax.experimental import pallas as pl
from jax.experimental.pallas import tpu as pltpu
from jax.sharding import PartitionSpec as P

HEAD_DIM = 256
EPSILON = 1e-06
MICRO = 4
BF = jnp.bfloat16
F32 = jnp.float32
MESH = pl.DeviceIdType.MESH
SPREAD = 3
ORDER = (2, 1, 3, 0)
NT = (((1,), (1,)), ((), ()))
NN = (((1,), (0,)), ((), ()))
TN = (((0,), (0,)), ((), ()))


def dot(a, b, dims=NN):
    return lax.dot_general(a, b, dims, preferred_element_type=F32)


def layer_kernel(
    width, loss_scale,
    lengths_ref, enc_ref, dec_ref, cot_ref, weights_ref, out_ref,
    w, wl, xs, sb, rb, tot, seed, seed_in, part, qrecv, qs, ks, vs, ps, rr, cs, oown, ost, orecv, xn,
    dpart, drecv, dd, cc, uown, ust, urecv, wown, wst, wrecv, gn, gein, geout, ob,
    s_sem, l_sem, rb_ss, rb_rs, cb_ss, cb_rs, xb_rs, xa_ss, xa_rs, ga_ss, ga_rs, gb_ss, gb_rs, gc_ss, gc_rs, i_ss, x_rs, f_ss, fp_ss, q_ss, q_rs, kv_ss, kv_rs,
    c_ss, c_rs, o_ss, o_rs, n_ss,
    d_ss, d_rs, dd_ss, dd_rs, cc_ss, cc_rs, u_ss, u_rs, w_ss, w_rs, e_ss, e_rs, gn_ss,
    b_ss, b_rs,
):
    s = lax.axis_index("section")
    d = lax.axis_index("dp")
    p = lax.axis_index("mp")
    t = d // 2
    c = lax.rem(p, 2)
    j = 2 * (p // 2) + lax.rem(d, 2)
    odd = lax.rem(t, 2)
    decoder = s >= 4
    sel = jnp.where(decoder, 1, 0)
    spread_out = s < SPREAD
    starts = (s == 4) | (s == 7)
    other = (d, p + 1 - 2 * c)

    def place(tt, jj, ccc):
        return 2 * tt + lax.rem(jj, 2), 2 * (jj // 2) + ccc

    def member(k):
        return place(t, lax.rem(j + k, 4), c)

    def fellow(k):
        return d, lax.rem(p + k, 4)

    def column(tt):
        return 2 * tt + lax.rem(d, 2), p

    collector = place(t, p, d // 4)
    inner = t // 2 == c
    beside = column(t + 1 - 2 * odd)
    across = column(lax.rem(t + 3 - 2 * odd, 4))
    senders = [place(k, p, d // 4) for k in range(4)]
    owner = [(4 * c + b, j) for b in range(4)]
    heads_at = [place(q, p, e) for q in range(4) for e in range(2)]
    heads_of = [(jnp.int32(k), j) for k in range(8)]
    tokens_at = [place(p, jnp.int32(k), d // 4) for k in range(4)]
    tokens_of = [(4 * c + b, t) for b in range(4)]
    start_to = [place(t, jnp.int32(k), p // 2) for k in range(4)]
    start_from = [(2 * t + a, 2 * c + e) for a in range(2) for e in range(2)]
    first_to = [(2 * p + e, jnp.int32(k)) for k in range(4) for e in range(2)]
    first_from = [(jnp.int32(k), d // 2) for k in range(8)]

    def same(dev):
        return (dev[0] == d) & (dev[1] == p)

    def remote(src, dst, ss, rs, dev, sec=None):
        ids = {"dp": dev[0], "mp": dev[1]}
        if sec is not None:
            ids["section"] = sec
        return pltpu.make_async_remote_copy(
            src_ref=src, dst_ref=dst, send_sem=ss, recv_sem=rs, device_id=ids, device_id_type=MESH
        )

    def arrived(ref, sem):
        pltpu.make_async_copy(ref, ref, sem).wait()

    def send_any(src, dst, ss, rs, dev):
        here = same(dev)

        @pl.when(here)
        def _():
            pltpu.make_async_copy(src, dst, rs).start()

        @pl.when(jnp.logical_not(here))
        def _():
            remote(src, dst, ss, rs, dev).start()

    def sent_any(src, ss, dev):
        @pl.when(jnp.logical_not(same(dev)))
        def _():
            arrived(src, ss)

    bar = pltpu.get_barrier_semaphore()

    def greet(dev, sec=None):
        ids = {"dp": dev[0], "mp": dev[1]}
        if sec is not None:
            ids["section"] = sec
        pl.semaphore_signal(bar, inc=1, device_id=ids, device_id_type=MESH)

    def greet_other(dev):
        @pl.when(jnp.logical_not(same(dev)))
        def _():
            greet(dev)

    greet(other)
    greet(beside)
    greet(across)
    for k in range(1, 4):
        greet(member(k))

    @pl.when(spread_out)
    def _():
        for k in range(1, 4):
            greet(fellow(k))
        for dev in heads_at + heads_of:
            greet_other(dev)

    @pl.when((s > 0) & spread_out)
    def _():
        for k in range(4):
            greet(fellow(k), s - 1)
        for dev in tokens_of:
            greet_other(dev)

    @pl.when(s == SPREAD)
    def _():
        for dev in tokens_of:
            greet(dev, SPREAD - 1)

    @pl.when(s > SPREAD)
    def _():
        for k in range(4):
            greet(member(k), s - 1)

    @pl.when(s < 7)
    def _():
        for k in range(4):
            greet(member(k), s + 1)

    for dev in senders:
        greet_other(dev)

    @pl.when(inner)
    def _():
        for e in range(2):
            greet_other((2 * t + e, j))

    @pl.when(s == 0)
    def _():
        for dev in first_from:
            greet_other(dev)

    @pl.when(starts)
    def _():
        for dev in start_from:
            greet_other(dev)

    def others(devs):
        return sum(jnp.where(same(dev), 0, 1) for dev in devs)

    count = 6 + jnp.where(s > 0, 4, 0) + jnp.where(s < 7, 4, 0) + others(owner)
    count = count + others([collector]) + jnp.where(starts, others(start_to), 0)
    count = count + jnp.where(spread_out, 3 + others(heads_at) + others(heads_of), 0)
    count = count + jnp.where((s > 0) & spread_out, others(tokens_at), 0)
    count = count + jnp.where(s == 0, others(first_to), 0)
    pl.semaphore_wait(bar, count)

    def shards(piece, first, number):
        return w.at[piece // 2, pl.ds(first, number), pl.ds(256 * lax.rem(piece, 2), 256)]

    def shard(piece, which):
        return w.at[piece // 2, which, pl.ds(256 * lax.rem(piece, 2), 256)]

    def own_shard(piece):
        return weights_ref.at[0, piece // 2, pl.ds(256 * lax.rem(piece, 2), 256)]

    def give(piece, carry):
        send_any(
            own_shard(piece), shard(piece, lax.rem(d, 4)), ga_ss.at[piece], ga_rs.at[piece],
            collector,
        )
        return carry

    local = pltpu.make_async_copy(weights_ref.at[0], wl, l_sem)

    @pl.when(spread_out)
    def _():
        local.start()


    def begin(src_of, stream):
        for m in range(MICRO):
            for k in range(4):
                for e in range(2):
                    block = 2 * lax.rem(p, 2) + e
                    send_any(
                        src_of(m, e), xs.at[stream, m, block, lax.rem(d, 2)],
                        i_ss.at[m, 2 * k + e], x_rs.at[stream, m, block], start_to[k],
                    )

    @pl.when(s == 0)
    def _():
        for m in range(MICRO):
            for k in range(8):
                send_any(
                    enc_ref.at[m, 0, :, pl.ds(512 * (k % 2), 512)],
                    ob.at[0, m, t, lax.rem(d, 2)], i_ss.at[m, k], xb_rs.at[m, t], first_to[k],
                )

    @pl.when(s == 4)
    def _():
        begin(lambda m, e: dec_ref.at[m, 0, :, pl.ds(512 * e, 512)], 1)

    @pl.when(s == 7)
    def _():
        loss = pltpu.make_async_copy(cot_ref.at[:, 0], seed_in, s_sem)
        loss.start()
        loss.wait()
        for m in range(MICRO):
            offsets = lax.broadcasted_iota(jnp.int32, (16, 1024), 0)
            live = jnp.where(offsets < lengths_ref[m, 0], loss_scale, 0.0)
            value = (seed_in[m].astype(F32) * live).astype(BF)
            for e in range(2):
                seed[m, e] = value[:, 512 * e:512 * e + 512]
        begin(lambda m, e: seed.at[m, e], 2)

    def pass_on(piece):
        arrived(shards(piece, 2 * (1 - odd), 2), gb_rs.at[piece])
        half = shard(piece, 2 * (1 - odd))
        remote(half, half, gc_ss.at[piece], gc_rs.at[piece], across).start()

    def collected(piece):
        mine = shards(piece, 2 * odd, 2)
        arrived(mine, ga_rs.at[piece])
        remote(mine, mine, gb_ss.at[piece, 0], gb_rs.at[piece], beside).start()
        remote(mine, mine, gb_ss.at[piece, 1], gb_rs.at[piece], across).start()

    def swap(piece):
        arrived(shards(piece, 2 * (1 - odd), 2), gb_rs.at[piece])
        half = shard(piece, 2 * (1 - odd) + 1)
        remote(half, half, gc_ss.at[piece], gc_rs.at[piece], beside).start()

    def swapped(piece):
        arrived(shards(piece, 2 * odd, 2), gc_rs.at[piece])

    def gather(first, last):
        lax.fori_loop(first, last, give, 0)

        @pl.when(inner)
        def _():
            def one(piece, carry):
                collected(piece)

                @pl.when(piece > first)
                def _():
                    pass_on(piece - 1)

                return carry

            lax.fori_loop(first, last, one, 0)

            @pl.when(last > first)
            def _():
                pass_on(last - 1)

        @pl.when(jnp.logical_not(inner))
        def _():
            def one(piece, carry):
                swap(piece)
                return carry

            def other_one(piece, carry):
                swapped(piece)
                return carry

            lax.fori_loop(first, last, one, 0)
            lax.fori_loop(first, last, other_one, 0)

    gather(0, jnp.where(spread_out, 0, 8))

    @pl.when(spread_out)
    def _():
        local.wait()

    def rows(value):
        return value.reshape(32, 512)

    def block_at(k):
        return lax.rem(j + 4 - k, 4)

    def project(m, stream, mats, start, ss, rs, relayed=None):
        sums = [None] * len(mats)
        squares = None
        for k in ORDER:
            block = block_at(k)
            if k == 0 and relayed is not None:
                @pl.when(jnp.logical_not(relayed))
                def _():
                    arrived(xs.at[stream, m, block], x_rs.at[stream, m, block])
            else:
                arrived(xs.at[stream, m, block], x_rs.at[stream, m, block])
            left = rows(xs[stream, m, block])
            wide = left.astype(F32)
            square = jnp.sum(wide * wide, axis=-1, keepdims=True)
            squares = square if squares is None else squares + square
            for i, mat in enumerate(mats):
                term = dot(left, w[mat, block])
                sums[i] = term if sums[i] is None else sums[i] + term
        squares = jnp.broadcast_to(squares, (32, 128)).reshape(2, 16, 128)
        for i, mat in enumerate(mats):
            first = (0, 640, 1152)[mat]
            part[m, :, :, first:first + 512] = sums[i].reshape(2, 16, 512)
        if 0 in mats:
            part[m, :, :, 512:640] = squares
        if 1 in mats:
            part[m, :, :, 1664:1792] = squares
        cols = pl.ds(*start)
        remote(part.at[m, 1 - c, :, cols], qrecv.at[m, :, cols], ss.at[m], rs.at[m], other).start()

    def project_all(m):
        project(m, 0, (0, 1, 2), (0, 1792), q_ss, q_rs)

    def project_query(m):
        project(m, 1, (0,), (0, 640), q_ss, q_rs)

    def project_key(m):
        project(m, 0, (1, 2), (640, 1152), kv_ss, kv_rs, s > 4)

        @pl.when(s == 4)
        def _():
            onward(m)

    def onward(m):
        remote(
            xs.at[0, m, j], xs.at[0, m, j], f_ss.at[m], x_rs.at[0, m, j], (d, p), s + 1
        ).start()

    def relay(m):
        arrived(xs.at[0, m, j], x_rs.at[0, m, j])

        @pl.when(s < 7)
        def _():
            onward(m)

        for k in (2, 1, 3):
            remote(
                xs.at[0, m, j], xs.at[0, m, j], fp_ss.at[m, k - 1], x_rs.at[0, m, j], member(k)
            ).start()

    def project_first(m):
        for k in ORDER:
            quarter = lax.rem(p + 4 - k, 4)
            arrived(ob.at[0, m, quarter], xb_rs.at[m, quarter])
            left = rows(ob[0, m, quarter])
            wide = left.astype(F32)
            square = jnp.sum(wide * wide, axis=-1, keepdims=True)
            high = square.astype(BF)
            low = (square - high.astype(F32)).astype(BF)
            for i in range(3):
                sb[m, quarter, :, :, 512 * i:512 * i + 512] = dot(left, wl[i]).astype(BF).reshape(
                    2, 16, 512
                )
            lane = lax.broadcasted_iota(jnp.int32, (32, 128), 1)
            parts = jnp.where(
                lane < 64, jnp.broadcast_to(high.astype(F32), (32, 128)),
                jnp.broadcast_to(low.astype(F32), (32, 128)),
            )
            sb[m, quarter, :, :, 1536:] = parts.astype(BF).reshape(2, 16, 128)
            for e in range(2):
                send_any(
                    sb.at[m, quarter, e], rb.at[m, d], rb_ss.at[m, 2 * quarter + e], rb_rs.at[m],
                    place(quarter, p, e),
                )

    def output_first(m):
        arrived(ob.at[3, m], cb_rs.at[m])
        for k in ORDER:
            term = dot(rows(ob[3, m, lax.rem(p + k, 4)]), wl[3], NT)
            if k == 0:
                oown[m] = term
            else:
                ost[m, k - 1] = term.astype(BF)
                remote(
                    ost.at[m, k - 1], orecv.at[m, k - 1], o_ss.at[m, k - 1], o_rs.at[m], fellow(k)
                ).start()

    def advance_first(m):
        total = rows(ob[0, m, p]).astype(F32) + oown[m]
        arrived(orecv.at[m], o_rs.at[m])
        for k in range(3):
            total = total + orecv[m, k].astype(F32)
        xn[m] = total.astype(BF).reshape(2, 16, 512)

        @pl.when(s < SPREAD - 1)
        def _():
            for k in ORDER:
                remote(
                    xn.at[m], ob.at[0, m, p], n_ss.at[m, k], xb_rs.at[m, p], fellow(k), s + 1
                ).start()

        @pl.when(s == SPREAD - 1)
        def _():
            block = lax.rem(d, 4)
            for k in ORDER:
                remote(
                    xn.at[m], xs.at[0, m, block], n_ss.at[m, k], x_rs.at[0, m, block],
                    place(p, lax.rem(j + k, 4), d // 4), s + 1,
                ).start()

    def attend(m):
        @pl.when(decoder)
        def _():
            arrived(qrecv.at[m, :, pl.ds(0, 640)], q_rs.at[m])
            arrived(qrecv.at[m, :, pl.ds(640, 1152)], kv_rs.at[m])

        @pl.when(jnp.logical_not(decoder | spread_out))
        def _():
            arrived(qrecv.at[m], q_rs.at[m])

        @pl.when(jnp.logical_not(spread_out))
        def _():
            tot[...] = part[m, c] + qrecv[m]

        @pl.when(spread_out)
        def _():
            arrived(rb.at[m], rb_rs.at[m])
            summed = rb[m, 0].astype(F32)
            for k in range(1, 8):
                summed = summed + rb[m, k].astype(F32)
            square = summed[:, 1536:1537] + summed[:, 1600:1601]
            square = jnp.broadcast_to(square, (16, 128))
            tot[:, :512] = summed[:, :512]
            tot[:, 512:640] = square
            tot[:, 640:1664] = summed[:, 512:1536]
            tot[:, 1664:] = square

        total = tot[...]
        factor_q = lax.rsqrt(total[:, 512:513] * (1.0 / width) + EPSILON)
        factor_k = lax.rsqrt(total[:, 1664:1665] * (1.0 / width) + EPSILON)
        rr[m, 0] = jnp.broadcast_to(factor_q, (16, 128))
        rr[m, 1] = jnp.broadcast_to(factor_k, (16, 128))
        query = (total[:, :512] * factor_q).astype(BF)
        key = (total[:, 640:1152] * factor_k).astype(BF)
        value = (total[:, 1152:1664] * factor_k).astype(BF)
        qs[m] = query
        ks[m] = key
        vs[m] = value
        contexts = []
        for h in range(2):
            cols = slice(h * HEAD_DIM, (h + 1) * HEAD_DIM)
            raised = jnp.exp(dot(query[:, cols], key[:, cols], NT) * HEAD_DIM ** (-0.5))
            weight = (raised / jnp.sum(raised, axis=-1, keepdims=True)).astype(BF)
            ps[m, h] = weight.astype(F32)
            contexts.append(dot(weight, value[:, cols]).astype(BF))
        cs[m, c] = jnp.concatenate(contexts, axis=1)

        @pl.when(jnp.logical_not(spread_out))
        def _():
            remote(cs.at[m, c], cs.at[m, c], c_ss.at[m], c_rs.at[m], other).start()

        @pl.when(spread_out)
        def _():
            for k in range(8):
                send_any(
                    cs.at[m, c], ob.at[3, m, t, c], cb_ss.at[m, k], cb_rs.at[m], heads_of[k]
                )

    def output(m):
        arrived(cs.at[m, c], c_rs.at[m])
        context = rows(cs[m])
        for k in ORDER:
            term = dot(context, w[3, lax.rem(j + k, 4)], NT)
            if k == 0:
                oown[m] = term
            else:
                ost[m, k - 1] = term.astype(BF)
                remote(
                    ost.at[m, k - 1], orecv.at[m, k - 1], o_ss.at[m, k - 1], o_rs.at[m], member(k)
                ).start()

    def advance(m):
        total = rows(xs[sel, m, j]).astype(F32) + oown[m]
        arrived(orecv.at[m], o_rs.at[m])
        for k in range(3):
            total = total + orecv[m, k].astype(F32)
        xn[m] = total.astype(BF).reshape(2, 16, 512)
        for k in ORDER:
            remote(
                xn.at[m], xs.at[sel, m, j], n_ss.at[m, k], x_rs.at[sel, m, j], member(k), s + 1
            ).start()

    def forward_step(i):
        @pl.when((i < MICRO) & spread_out)
        def _():
            project_first(i)

        @pl.when((i > 2) & spread_out)
        def _():
            advance_first(i - 3)

        @pl.when((i > 1) & (i < MICRO + 2) & spread_out)
        def _():
            output_first(i - 2)

        @pl.when((i < MICRO) & jnp.logical_not(decoder | spread_out))
        def _():
            project_all(i)

        @pl.when((i < MICRO - 1) & (s == 4))
        def _():
            project_query(i + 1)

        @pl.when(((i < MICRO) & (s == 4)) | ((i < MICRO - 1) & (s > 4)))
        def _():
            project_key(i + jnp.where(s > 4, 1, 0))

        @pl.when((i < MICRO) & (s > 4))
        def _():
            project_query(i)

            @pl.when(i < MICRO - 2)
            def _():
                relay(i + 2)

        @pl.when((i > 0) & (i <= MICRO) & (s >= SPREAD) & (s < 7))
        def _():
            advance(i - 1)

        late = jnp.where(spread_out, 1, 0)

        @pl.when((i >= late) & (i < MICRO + late))
        def _():
            attend(i - late)

        @pl.when((i < MICRO) & (s >= SPREAD) & (s < 7))
        def _():
            output(i)

    def to_owners(src_of, slot, m=None):
        for b in range(4):
            dst = ob.at[slot, :, t] if m is None else ob.at[slot, m, t]
            send_any(src_of(b), dst, b_ss.at[slot, b], b_rs.at[slot], owner[b])

    def owners_sent(src_of, slot):
        for b in range(4):
            sent_any(src_of(b), b_ss.at[slot, b], owner[b])

    def project_back(m):
        total = None
        for k in ORDER:
            block = block_at(k)
            arrived(xs.at[2, m, block], x_rs.at[2, m, block])
            term = dot(rows(xs[2, m, block]), w[3, block])
            total = term if total is None else total + term
        dpart[m] = total.reshape(2, 16, 512)
        remote(dpart.at[m, 1 - c], drecv.at[m], d_ss.at[m], d_rs.at[m], other).start()

    def attend_back(m):
        query, key, value = qs[m], ks[m], vs[m]
        arrived(drecv.at[m], d_rs.at[m])
        grad = (dpart[m, c] + drecv[m]).astype(BF)
        pieces = [[], [], []]
        for h in range(2):
            cols = slice(h * HEAD_DIM, (h + 1) * HEAD_DIM)
            weight = ps[m, h]
            grad_weight = dot(grad[:, cols], value[:, cols], NT)
            pieces[2].append(dot(weight.astype(BF), grad[:, cols], TN))
            inside = jnp.sum(grad_weight * weight, axis=-1, keepdims=True)
            scores = (weight * (grad_weight - inside) * HEAD_DIM ** (-0.5)).astype(BF)
            pieces[0].append(dot(scores, key[:, cols]))
            pieces[1].append(dot(scores, query[:, cols], TN))
        grads = [jnp.concatenate(piece, axis=1) for piece in pieces]
        factors = [rr[m, 0][:, :1], rr[m, 1][:, :1], rr[m, 1][:, :1]]
        for i in range(3):
            dd[m, i, c] = (grads[i] * factors[i]).astype(BF)
        remote(dd.at[m, :, c], dd.at[m, :, c], dd_ss.at[m], dd_rs.at[m], other).start()
        means = [
            jnp.sum(g * v.astype(F32), axis=-1, keepdims=True) * (1.0 / width)
            for g, v in zip(grads, (query, key, value))
        ]
        cc[m, 0, c] = jnp.broadcast_to(means[0] * factors[0] * factors[0], (16, 128))
        cc[m, 1, c] = jnp.broadcast_to((means[1] + means[2]) * factors[1] * factors[1], (16, 128))
        remote(cc.at[m, :, c], cc.at[m, :, c], cc_ss.at[m], cc_rs.at[m], other).start()

    def spread_back(m):
        arrived(dd.at[m, :, c], dd_rs.at[m])
        arrived(cc.at[m, :, c], cc_rs.at[m])

        def spread(pairs, stream, kinds, own, stage, recv, ss, rs):
            lefts = [rows(dd[m, i]) for i in pairs]
            shift = sum(cc[m, i].reshape(32, 128)[:, :1] for i in kinds)
            for k in ORDER:
                block = lax.rem(j + k, 4)
                term = -rows(xs[stream, m, block]).astype(F32) * shift
                for i, left in zip(pairs, lefts):
                    term = term + dot(left, w[i, block], NT)
                if k == 0:
                    own[m] = term
                else:
                    stage[m, k - 1] = term.astype(BF)
                    remote(
                        stage.at[m, k - 1], recv.at[m, k - 1], ss.at[m, k - 1], rs.at[m], member(k)
                    ).start()

        @pl.when((s > 0) & (s < 4))
        def _():
            spread((0, 1, 2), 0, (0, 1), uown, ust, urecv, u_ss, u_rs)

        @pl.when(s > 4)
        def _():
            spread((0,), 1, (0,), uown, ust, urecv, u_ss, u_rs)

        @pl.when(s >= 4)
        def _():
            spread((1, 2), 0, (1,), wown, wst, wrecv, w_ss, w_rs)

    def hand_back(m):
        for k in ORDER:
            remote(
                gn.at[m], xs.at[2, m, j], gn_ss.at[m, k], x_rs.at[2, m, j], member(k), s - 1
            ).start()

    def advance_back(m):
        total = rows(xs[2, m, j]).astype(F32) + uown[m]
        arrived(urecv.at[m], u_rs.at[m])
        for k in range(3):
            total = total + urecv[m, k].astype(F32)
        gn[m] = total.astype(BF).reshape(2, 16, 512)
        hand_back(m)

    def advance_key(m):
        arrived(wrecv.at[m], w_rs.at[m])
        total = wown[m]
        for k in range(3):
            total = total + wrecv[m, k].astype(F32)
        geout[m] = total.astype(BF).reshape(2, 16, 512)

        @pl.when(s < 7)
        def _():
            arrived(gein.at[m], e_rs.at[m])
            geout[m] = (total + rows(gein[m]).astype(F32)).astype(BF).reshape(2, 16, 512)

        @pl.when(s > 4)
        def _():
            remote(geout.at[m], gein.at[m], e_ss.at[m], e_rs.at[m], (d, p), s - 1).start()

        @pl.when(s == 4)
        def _():
            gn[m] = geout[m]
            hand_back(m)

    def backward_step(i):
        @pl.when(i < MICRO)
        def _():
            project_back(i)

        @pl.when((i < MICRO) & (s < 4))
        def _():
            attend_back(i)

        @pl.when((i > 0) & (s > 0) & (s != 4))
        def _():
            advance_back(i - 1)

        @pl.when((i > 0) & (s == 4))
        def _():
            advance_key(i - 1)

        @pl.when((i < MICRO) & (s >= 4))
        def _():
            attend_back(i)

        @pl.when(i < MICRO)
        def _():
            spread_back(i)

            @pl.when(s < 2)
            def _():
                to_owners(lambda b: xs.at[2, i, b], 2, i)
                for k in range(3):
                    to_owners(lambda b: dd.at[i, k], 4 + k, i)

        @pl.when((i > 0) & (s > 4))
        def _():
            advance_key(i - 1)

    def last_step(i):
        @pl.when(i < MICRO)
        def _():
            project_query(i)

        @pl.when(i > 0)
        def _():
            advance_back(i - 1)

        @pl.when(i < MICRO)
        def _():
            attend(i)
            attend_back(i)

        @pl.when(i < MICRO - 1)
        def _():
            project_key(i + 1)

        @pl.when(i < MICRO)
        def _():
            spread_back(i)

        @pl.when(i < MICRO - 2)
        def _():
            relay(i + 2)

        @pl.when(i > 0)
        def _():
            advance_key(i - 1)

    @pl.when(s == 4)
    def _():
        project_query(0)

    @pl.when(s == 7)
    def _():
        def one(m, carry):
            project_back(m)
            return carry

        lax.fori_loop(0, MICRO, one, 0)

    @pl.when(s > 4)
    def _():
        relay(0)
        relay(1)
        project_key(0)

    def forward_to_owners():
        to_owners(lambda b: xs.at[sel, :, b], 0)
        to_owners(lambda b: cs, 3)

    def step(n, carry):
        @pl.when((s == 7) & (n <= MICRO))
        def _():
            last_step(n)

        @pl.when((s < 7) & (n <= MICRO + 2))
        def _():
            forward_step(n)

        @pl.when(n == MICRO + 3)
        def _():
            @pl.when(s == SPREAD)
            def _():
                forward_to_owners()

            @pl.when((s > 0) & spread_out)
            def _():
                for k in range(4):
                    send_any(
                        ob.at[0, :, p], xs.at[0, :, lax.rem(d, 4)], xa_ss.at[k], xa_rs, tokens_at[k]
                    )

            gather(0, jnp.where(spread_out, 8, 0))

            @pl.when((s > 0) & spread_out)
            def _():
                arrived(xs.at[0], xa_rs)

        @pl.when((s < 7) & (n >= MICRO + 3))
        def _():
            backward_step(n - MICRO - 3)

        return carry

    lax.fori_loop(0, 2 * MICRO + 4, step, 0)

    @pl.when(s > 1)
    def _():
        to_owners(lambda b: xs.at[2, :, b], 2)
        for i in range(3):
            to_owners(lambda b: dd.at[:, i], 4 + i)

    @pl.when(decoder)
    def _():
        @pl.when(s == 7)
        def _():
            for m in range(MICRO):
                arrived(cs.at[m, c], c_rs.at[m])

        forward_to_owners()
        to_owners(lambda b: xs.at[0, :, b], 1)

    key_slot = jnp.where(decoder, 1, 0)

    @pl.when(s >= SPREAD)
    def _():
        arrived(ob.at[3], b_rs.at[3])

    arrived(ob.at[2], b_rs.at[2])
    out_ref[3] = dot(ob[2].reshape(512, 512), ob[3].reshape(512, 512), TN).astype(BF)

    @pl.when(s >= SPREAD)
    def _():
        arrived(ob.at[0], b_rs.at[0])

    @pl.when(decoder)
    def _():
        arrived(ob.at[1], b_rs.at[1])

    for i in range(3):
        arrived(ob.at[4 + i], b_rs.at[4 + i])
        left = ob[0] if i == 0 else ob[key_slot]
        out_ref[i] = dot(left.reshape(512, 512), ob[4 + i].reshape(512, 512), TN).astype(BF)

    @pl.when(starts)
    def _():
        for m in range(MICRO):
            for k in range(8):
                sent_any(seed.at[m, 0], i_ss.at[m, k], start_to[k // 2])

    @pl.when(s == 0)
    def _():
        for m in range(MICRO):
            for k in range(8):
                sent_any(seed.at[m, 0], i_ss.at[m, k], first_to[k])

    @pl.when((s > 0) & spread_out)
    def _():
        for k in range(4):
            sent_any(ob.at[0, :, 0], xa_ss.at[k], tokens_at[k])

    def given(piece, carry):
        sent_any(own_shard(piece), ga_ss.at[piece], collector)
        arrived(shard(piece, 0), gc_ss.at[piece])

        @pl.when(inner)
        def _():
            for k in range(2):
                arrived(shards(piece, 0, 2), gb_ss.at[piece, k])

        return carry

    lax.fori_loop(0, 8, given, 0)


    @pl.when(s >= SPREAD)
    def _():
        owners_sent(lambda b: xs.at[sel, :, b], 0)
        owners_sent(lambda b: cs, 3)

    @pl.when(decoder)
    def _():
        owners_sent(lambda b: xs.at[0, :, b], 1)

    owners_sent(lambda b: xs.at[2, :, b], 2)
    for i in range(3):
        owners_sent(lambda b: dd.at[:, i], 4 + i)

    def finish(m, carry):
        @pl.when(decoder)
        def _():
            arrived(part.at[m, 0, :, pl.ds(0, 640)], q_ss.at[m])
            arrived(part.at[m, 0, :, pl.ds(640, 1152)], kv_ss.at[m])

        @pl.when(jnp.logical_not(decoder | spread_out))
        def _():
            arrived(part.at[m, 0], q_ss.at[m])

        @pl.when(jnp.logical_not(spread_out))
        def _():
            arrived(cs.at[m, 0], c_ss.at[m])

        @pl.when(spread_out)
        def _():
            for k in range(8):
                sent_any(sb.at[m, 0, 0], rb_ss.at[m, k], heads_at[k])
                sent_any(cs.at[m, 0], cb_ss.at[m, k], heads_of[k])

        arrived(dpart.at[m, 0], d_ss.at[m])
        arrived(dd.at[m, :, 0], dd_ss.at[m])
        arrived(cc.at[m, :, 0], cc_ss.at[m])

        @pl.when(decoder & (s < 7))
        def _():
            arrived(xs.at[0, m, 0], f_ss.at[m])

        @pl.when(s > 4)
        def _():
            for k in range(3):
                arrived(xs.at[0, m, 0], fp_ss.at[m, k])

        @pl.when(s < 7)
        def _():
            for k in range(3):
                arrived(ost.at[m, k], o_ss.at[m, k])
            for k in range(4):
                arrived(xn.at[m], n_ss.at[m, k])

        @pl.when((s > 0) & (s != 4))
        def _():
            for k in range(3):
                arrived(ust.at[m, k], u_ss.at[m, k])

        @pl.when(s > 0)
        def _():
            for k in range(4):
                arrived(gn.at[m], gn_ss.at[m, k])

        @pl.when(s >= 4)
        def _():
            for k in range(3):
                arrived(wst.at[m, k], w_ss.at[m, k])

        @pl.when(s > 4)
        def _():
            arrived(geout.at[m], e_ss.at[m])

        return carry

    lax.fori_loop(0, MICRO, finish, 0)


def per_device(enc_input, dec_input, cotangent, target_lengths, weights):
    tokens = MICRO * lax.axis_size("dp") * enc_input.shape[1] * enc_input.shape[2]
    dma = pltpu.SemaphoreType.DMA
    tile = (2, 16, 512)
    scratch = [
        pltpu.VMEM((4, 4, 512, 512), BF),
        pltpu.VMEM((4, 512, 512), BF),
        pltpu.VMEM((3, MICRO, 4) + tile, BF),
        pltpu.VMEM((MICRO, 4, 2, 16, 1664), BF),
        pltpu.VMEM((MICRO, 8, 16, 1664), BF),
        pltpu.VMEM((16, 1792), F32),
        pltpu.VMEM((MICRO, 2, 16, 512), BF),
        pltpu.VMEM((MICRO, 16, 1024), BF),
        pltpu.VMEM((MICRO, 2, 16, 1792), F32),
        pltpu.VMEM((MICRO, 16, 1792), F32),
        pltpu.VMEM((MICRO, 16, 512), BF),
        pltpu.VMEM((MICRO, 16, 512), BF),
        pltpu.VMEM((MICRO, 16, 512), BF),
        pltpu.VMEM((MICRO, 2, 16, 16), F32),
        pltpu.VMEM((MICRO, 2, 16, 128), F32),
        pltpu.VMEM((MICRO,) + tile, BF),
        pltpu.VMEM((MICRO, 32, 512), F32),
        pltpu.VMEM((MICRO, 3, 32, 512), BF),
        pltpu.VMEM((MICRO, 3, 32, 512), BF),
        pltpu.VMEM((MICRO,) + tile, BF),
        pltpu.VMEM((MICRO,) + tile, F32),
        pltpu.VMEM((MICRO, 16, 512), F32),
        pltpu.VMEM((MICRO, 3) + tile, BF),
        pltpu.VMEM((MICRO, 2, 2, 16, 128), F32),
        pltpu.VMEM((MICRO, 32, 512), F32),
        pltpu.VMEM((MICRO, 3, 32, 512), BF),
        pltpu.VMEM((MICRO, 3, 32, 512), BF),
        pltpu.VMEM((MICRO, 32, 512), F32),
        pltpu.VMEM((MICRO, 3, 32, 512), BF),
        pltpu.VMEM((MICRO, 3, 32, 512), BF),
        pltpu.VMEM((MICRO,) + tile, BF),
        pltpu.VMEM((MICRO,) + tile, BF),
        pltpu.VMEM((MICRO,) + tile, BF),
        pltpu.VMEM((7, MICRO, 4) + tile, BF),
        dma, dma,
        dma((MICRO, 8)), dma((MICRO,)),
        dma((MICRO, 8)), dma((MICRO,)),
        dma((MICRO, 4)), dma((4,)), dma,
        dma((8,)), dma((8,)),
        dma((8, 2)), dma((8,)),
        dma((8,)), dma((8,)),
        dma((MICRO, 8)), dma((3, MICRO, 4)),
        dma((MICRO,)), dma((MICRO, 3)),
        dma((MICRO,)), dma((MICRO,)),
        dma((MICRO,)), dma((MICRO,)),
        dma((MICRO,)), dma((MICRO,)),
        dma((MICRO, 3)), dma((MICRO,)),
        dma((MICRO, 4)),
        dma((MICRO,)), dma((MICRO,)),
        dma((MICRO,)), dma((MICRO,)),
        dma((MICRO,)), dma((MICRO,)),
        dma((MICRO, 3)), dma((MICRO,)),
        dma((MICRO, 3)), dma((MICRO,)),
        dma((MICRO,)), dma((MICRO,)),
        dma((MICRO, 4)),
        dma((7, 4)), dma((7,)),
    ]
    grads = pl.pallas_call(
        functools.partial(layer_kernel, 4096, float(tokens) ** (-0.5)),
        out_shape=jax.ShapeDtypeStruct((4, 512, 512), BF),
        in_specs=[pl.BlockSpec(memory_space=pltpu.SMEM)] + [pl.BlockSpec(memory_space=pl.ANY)] * 4,
        out_specs=pl.BlockSpec(memory_space=pltpu.VMEM),
        scratch_shapes=scratch,
        compiler_params=pltpu.CompilerParams(
            collective_id=0, has_side_effects=True, vmem_limit_bytes=60 << 20
        ),
        name="layers",
    )(target_lengths, enc_input, dec_input, cotangent, weights)
    return grads[None].astype(F32)


def solution(mesh):
    in_specs = (
        P(None, "dp", None, "mp"),
        P(None, "dp", None, "mp"),
        P(None, "dp", None, "mp"),
        P(None, "dp"),
        P("section", None, "dp", "mp"),
    )
    return jax.shard_map(
        per_device,
        mesh=mesh,
        in_specs=in_specs,
        out_specs=P("section", None, "dp", "mp"),
        check_vma=False,
    )
```

```python
import functools

import jax
import jax.numpy as jnp
from jax import lax
from jax.experimental import pallas as pl
from jax.experimental.pallas import tpu as pltpu
from jax.sharding import PartitionSpec as P

HEAD_DIM = 256
EPSILON = 1e-06
MICRO = 4
BF = jnp.bfloat16
F32 = jnp.float32
MESH = pl.DeviceIdType.MESH
SPREAD = 2
ORDER = (2, 1, 3, 0)
NT = (((1,), (1,)), ((), ()))
NN = (((1,), (0,)), ((), ()))
TN = (((0,), (0,)), ((), ()))


def dot(a, b, dims=NN):
    return lax.dot_general(a, b, dims, preferred_element_type=F32)


def layer_kernel(
    width, loss_scale,
    lengths_ref, enc_ref, dec_ref, cot_ref, weights_ref, out_ref,
    w, wt, wl, xs, sb, rb, tot, seed, seed_in, part, qrecv, qs, ks, vs, ps, rr, cs, oown, ost, orecv, xn,
    dpart, drecv, dd, cc, uown, ust, urecv, wown, wst, wrecv, gn, gein, geout, ob,
    s_sem, l_sem, rb_ss, rb_rs, cb_ss, cb_rs, xb_rs, xa_ss, xa_rs, ga_ss, ga_rs, gb_ss, gb_rs, gc_ss, gc_rs, i_ss, x_rs, f_ss, fp_ss, q_ss, q_rs, kv_ss, kv_rs,
    c_ss, c_rs, o_ss, o_rs, n_ss,
    d_ss, d_rs, dd_ss, dd_rs, cc_ss, cc_rs, u_ss, u_rs, w_ss, w_rs, e_ss, e_rs, gn_ss,
    b_ss, b_rs,
):
    s = lax.axis_index("section")
    d = lax.axis_index("dp")
    p = lax.axis_index("mp")
    t = d // 2
    c = lax.rem(p, 2)
    j = 2 * (p // 2) + lax.rem(d, 2)
    odd = lax.rem(t, 2)
    decoder = s >= 4
    sel = jnp.where(decoder, 1, 0)
    spread_out = s < SPREAD
    starts = (s == 4) | (s == 7)
    other = (d, p + 1 - 2 * c)

    def place(tt, jj, ccc):
        return 2 * tt + lax.rem(jj, 2), 2 * (jj // 2) + ccc

    def member(k):
        return place(t, lax.rem(j + k, 4), c)

    def fellow(k):
        return d, lax.rem(p + k, 4)

    def column(tt):
        return 2 * tt + lax.rem(d, 2), p

    collector = place(t, p, d // 4)
    inner = t // 2 == c
    beside = column(t + 1 - 2 * odd)
    across = column(lax.rem(t + 3 - 2 * odd, 4))
    senders = [place(k, p, d // 4) for k in range(4)]
    owner = [(4 * c + b, j) for b in range(4)]
    heads_at = [place(q, p, e) for q in range(4) for e in range(2)]
    heads_of = [(jnp.int32(k), j) for k in range(8)]
    tokens_at = [place(p, jnp.int32(k), d // 4) for k in range(4)]
    tokens_of = [(4 * c + b, t) for b in range(4)]
    start_to = [place(t, jnp.int32(k), p // 2) for k in range(4)]
    start_from = [(2 * t + a, 2 * c + e) for a in range(2) for e in range(2)]
    first_to = [(2 * p + e, jnp.int32(k)) for k in range(4) for e in range(2)]
    first_from = [(jnp.int32(k), d // 2) for k in range(8)]

    def same(dev):
        return (dev[0] == d) & (dev[1] == p)

    def remote(src, dst, ss, rs, dev, sec=None):
        ids = {"dp": dev[0], "mp": dev[1]}
        if sec is not None:
            ids["section"] = sec
        return pltpu.make_async_remote_copy(
            src_ref=src, dst_ref=dst, send_sem=ss, recv_sem=rs, device_id=ids, device_id_type=MESH
        )

    def arrived(ref, sem):
        pltpu.make_async_copy(ref, ref, sem).wait()

    def send_any(src, dst, ss, rs, dev):
        here = same(dev)

        @pl.when(here)
        def _():
            pltpu.make_async_copy(src, dst, rs).start()

        @pl.when(jnp.logical_not(here))
        def _():
            remote(src, dst, ss, rs, dev).start()

    def sent_any(src, ss, dev):
        @pl.when(jnp.logical_not(same(dev)))
        def _():
            arrived(src, ss)

    bar = pltpu.get_barrier_semaphore()

    def greet(dev, sec=None):
        ids = {"dp": dev[0], "mp": dev[1]}
        if sec is not None:
            ids["section"] = sec
        pl.semaphore_signal(bar, inc=1, device_id=ids, device_id_type=MESH)

    def greet_other(dev):
        @pl.when(jnp.logical_not(same(dev)))
        def _():
            greet(dev)

    greet(other)
    greet(beside)
    greet(across)
    for k in range(1, 4):
        greet(member(k))

    @pl.when(spread_out)
    def _():
        for k in range(1, 4):
            greet(fellow(k))
        for dev in heads_at + heads_of:
            greet_other(dev)

    @pl.when((s > 0) & spread_out)
    def _():
        for k in range(4):
            greet(fellow(k), s - 1)
        for dev in tokens_of:
            greet_other(dev)

    @pl.when(s == SPREAD)
    def _():
        for dev in tokens_of:
            greet(dev, SPREAD - 1)

    @pl.when(s > SPREAD)
    def _():
        for k in range(4):
            greet(member(k), s - 1)

    @pl.when(s < 7)
    def _():
        for k in range(4):
            greet(member(k), s + 1)

    for dev in senders:
        greet_other(dev)

    @pl.when(inner)
    def _():
        for e in range(2):
            greet_other((2 * t + e, j))

    @pl.when(s == 0)
    def _():
        for dev in first_from:
            greet_other(dev)

    @pl.when(starts)
    def _():
        for dev in start_from:
            greet_other(dev)

    def others(devs):
        return sum(jnp.where(same(dev), 0, 1) for dev in devs)

    count = 6 + jnp.where(s > 0, 4, 0) + jnp.where(s < 7, 4, 0) + others(owner)
    count = count + others([collector]) + jnp.where(starts, others(start_to), 0)
    count = count + jnp.where(spread_out, 3 + others(heads_at) + others(heads_of), 0)
    count = count + jnp.where((s > 0) & spread_out, others(tokens_at), 0)
    count = count + jnp.where(s == 0, others(first_to), 0)
    pl.semaphore_wait(bar, count)

    def shards(piece, first, number):
        return w.at[piece // 2, pl.ds(first, number), pl.ds(256 * lax.rem(piece, 2), 256)]

    def shard(piece, which):
        return w.at[piece // 2, which, pl.ds(256 * lax.rem(piece, 2), 256)]

    def own_shard(piece):
        return weights_ref.at[0, piece // 2, pl.ds(256 * lax.rem(piece, 2), 256)]

    def give(piece):
        send_any(
            own_shard(piece), shard(piece, lax.rem(d, 4)), ga_ss.at[piece], ga_rs.at[piece],
            collector,
        )

    local = pltpu.make_async_copy(weights_ref.at[0], wl, l_sem)

    @pl.when(spread_out)
    def _():
        local.start()


    def begin(src_of, stream):
        for m in range(MICRO):
            for k in range(4):
                for e in range(2):
                    block = 2 * lax.rem(p, 2) + e
                    send_any(
                        src_of(m, e), xs.at[stream, m, block, lax.rem(d, 2)],
                        i_ss.at[m, 2 * k + e], x_rs.at[stream, m, block], start_to[k],
                    )

    @pl.when(s == 0)
    def _():
        for m in range(MICRO):
            for k in range(8):
                send_any(
                    enc_ref.at[m, 0, :, pl.ds(512 * (k % 2), 512)],
                    ob.at[0, m, t, lax.rem(d, 2)], i_ss.at[m, k], xb_rs.at[m, t], first_to[k],
                )

    @pl.when(s == 4)
    def _():
        begin(lambda m, e: dec_ref.at[m, 0, :, pl.ds(512 * e, 512)], 1)

    @pl.when(s == 7)
    def _():
        loss = pltpu.make_async_copy(cot_ref.at[:, 0], seed_in, s_sem)
        loss.start()
        loss.wait()
        for m in range(MICRO):
            offsets = lax.broadcasted_iota(jnp.int32, (16, 1024), 0)
            live = jnp.where(offsets < lengths_ref[m, 0], loss_scale, 0.0)
            value = (seed_in[m].astype(F32) * live).astype(BF)
            for e in range(2):
                seed[m, e] = value[:, 512 * e:512 * e + 512]
        begin(lambda m, e: seed.at[m, e], 2)

    def pass_on(piece):
        arrived(shards(piece, 2 * (1 - odd), 2), gb_rs.at[piece])
        half = shard(piece, 2 * (1 - odd))
        remote(half, half, gc_ss.at[piece], gc_rs.at[piece], across).start()

    def collected(piece):
        mine = shards(piece, 2 * odd, 2)
        arrived(mine, ga_rs.at[piece])
        remote(mine, mine, gb_ss.at[piece, 0], gb_rs.at[piece], beside).start()
        remote(mine, mine, gb_ss.at[piece, 1], gb_rs.at[piece], across).start()

    def swap(piece):
        arrived(shards(piece, 2 * (1 - odd), 2), gb_rs.at[piece])
        half = shard(piece, 2 * (1 - odd) + 1)
        remote(half, half, gc_ss.at[piece], gc_rs.at[piece], beside).start()

    def swapped(piece):
        arrived(shards(piece, 2 * odd, 2), gc_rs.at[piece])

    def when(cond, what, *args):
        @pl.when(cond)
        def _():
            what(*args)

    def repeat(first, last, what):
        def one(piece, carry):
            what(piece)
            return carry

        lax.fori_loop(first, last, one, 0)

    def collect_on(piece):
        collected(piece)
        when(piece > 0, pass_on, piece - 1)

    def gather_some(pieces):
        repeat(0, 8, give)

        @pl.when(inner)
        def _():
            repeat(0, pieces + 1, collect_on)
            repeat(pieces + 1, 8, collected)

        @pl.when(jnp.logical_not(inner))
        def _():
            repeat(0, pieces, swap)
            repeat(0, pieces, swapped)

    def gather_one(piece):
        when(inner, pass_on, piece)
        when(jnp.logical_not(inner), swap, piece)

    def gather_end(pieces):
        @pl.when(jnp.logical_not(inner))
        def _():
            repeat(pieces, 8, swapped)

    when(jnp.logical_not(spread_out), gather_some, 6)

    @pl.when(spread_out)
    def _():
        local.wait()

    def rows(value):
        return value.reshape(32, 512)

    def block_at(k):
        return lax.rem(j + 4 - k, 4)

    def project(m, stream, mats, start, ss, rs, relayed=None):
        sums = [None] * len(mats)
        squares = None
        for k in ORDER:
            block = block_at(k)
            if k == 0 and relayed is not None:
                @pl.when(jnp.logical_not(relayed))
                def _():
                    arrived(xs.at[stream, m, block], x_rs.at[stream, m, block])
            else:
                arrived(xs.at[stream, m, block], x_rs.at[stream, m, block])
            left = rows(xs[stream, m, block])
            wide = left.astype(F32)
            square = jnp.sum(wide * wide, axis=-1, keepdims=True)
            squares = square if squares is None else squares + square
            for i, mat in enumerate(mats):
                term = dot(left, w[mat, block])
                sums[i] = term if sums[i] is None else sums[i] + term
        squares = jnp.broadcast_to(squares, (32, 128)).reshape(2, 16, 128)
        for i, mat in enumerate(mats):
            first = (0, 640, 1152)[mat]
            part[m, :, :, first:first + 512] = sums[i].reshape(2, 16, 512)
        if 0 in mats:
            part[m, :, :, 512:640] = squares
        if 1 in mats:
            part[m, :, :, 1664:1792] = squares
        cols = pl.ds(*start)
        remote(part.at[m, 1 - c, :, cols], qrecv.at[m, :, cols], ss.at[m], rs.at[m], other).start()

    def project_all(m):
        project(m, 0, (0, 1, 2), (0, 1792), q_ss, q_rs)

    def project_query(m):
        project(m, 1, (0,), (0, 640), q_ss, q_rs)

    def project_key(m):
        project(m, 0, (1, 2), (640, 1152), kv_ss, kv_rs, s > 4)

        @pl.when(s == 4)
        def _():
            onward(m)

    def onward(m):
        remote(
            xs.at[0, m, j], xs.at[0, m, j], f_ss.at[m], x_rs.at[0, m, j], (d, p), s + 1
        ).start()

    def relay(m):
        arrived(xs.at[0, m, j], x_rs.at[0, m, j])

        @pl.when(s < 7)
        def _():
            onward(m)

        for k in (2, 1, 3):
            remote(
                xs.at[0, m, j], xs.at[0, m, j], fp_ss.at[m, k - 1], x_rs.at[0, m, j], member(k)
            ).start()

    def project_first(m):
        for k in ORDER:
            quarter = lax.rem(p + 4 - k, 4)
            arrived(ob.at[0, m, quarter], xb_rs.at[m, quarter])
            left = rows(ob[0, m, quarter])
            wide = left.astype(F32)
            square = jnp.sum(wide * wide, axis=-1, keepdims=True)
            high = square.astype(BF)
            low = (square - high.astype(F32)).astype(BF)
            for i in range(3):
                sb[m, quarter, :, :, 512 * i:512 * i + 512] = dot(left, wl[i]).astype(BF).reshape(
                    2, 16, 512
                )
            lane = lax.broadcasted_iota(jnp.int32, (32, 128), 1)
            parts = jnp.where(
                lane < 64, jnp.broadcast_to(high.astype(F32), (32, 128)),
                jnp.broadcast_to(low.astype(F32), (32, 128)),
            )
            sb[m, quarter, :, :, 1536:] = parts.astype(BF).reshape(2, 16, 128)
            for e in range(2):
                send_any(
                    sb.at[m, quarter, e], rb.at[m, d], rb_ss.at[m, 2 * quarter + e], rb_rs.at[m],
                    place(quarter, p, e),
                )

    def output_first(m):
        arrived(ob.at[3, m], cb_rs.at[m])
        for k in ORDER:
            term = dot(rows(ob[3, m, lax.rem(p + k, 4)]), wl[3], NT)
            if k == 0:
                oown[m] = term
            else:
                ost[m, k - 1] = term.astype(BF)
                remote(
                    ost.at[m, k - 1], orecv.at[m, k - 1], o_ss.at[m, k - 1], o_rs.at[m], fellow(k)
                ).start()

    def advance_first(m):
        total = rows(ob[0, m, p]).astype(F32) + oown[m]
        arrived(orecv.at[m], o_rs.at[m])
        for k in range(3):
            total = total + orecv[m, k].astype(F32)
        xn[m] = total.astype(BF).reshape(2, 16, 512)

        @pl.when(s < SPREAD - 1)
        def _():
            for k in ORDER:
                remote(
                    xn.at[m], ob.at[0, m, p], n_ss.at[m, k], xb_rs.at[m, p], fellow(k), s + 1
                ).start()

        @pl.when(s == SPREAD - 1)
        def _():
            block = lax.rem(d, 4)
            for k in ORDER:
                remote(
                    xn.at[m], xs.at[0, m, block], n_ss.at[m, k], x_rs.at[0, m, block],
                    place(p, lax.rem(j + k, 4), d // 4), s + 1,
                ).start()

    def attend(m):
        @pl.when(decoder)
        def _():
            arrived(qrecv.at[m, :, pl.ds(0, 640)], q_rs.at[m])
            arrived(qrecv.at[m, :, pl.ds(640, 1152)], kv_rs.at[m])

        @pl.when(jnp.logical_not(decoder | spread_out))
        def _():
            arrived(qrecv.at[m], q_rs.at[m])

        @pl.when(jnp.logical_not(spread_out))
        def _():
            tot[...] = part[m, c] + qrecv[m]

        @pl.when(spread_out)
        def _():
            arrived(rb.at[m], rb_rs.at[m])
            summed = rb[m, 0].astype(F32)
            for k in range(1, 8):
                summed = summed + rb[m, k].astype(F32)
            square = summed[:, 1536:1537] + summed[:, 1600:1601]
            square = jnp.broadcast_to(square, (16, 128))
            tot[:, :512] = summed[:, :512]
            tot[:, 512:640] = square
            tot[:, 640:1664] = summed[:, 512:1536]
            tot[:, 1664:] = square

        total = tot[...]
        factor_q = lax.rsqrt(total[:, 512:513] * (1.0 / width) + EPSILON)
        factor_k = lax.rsqrt(total[:, 1664:1665] * (1.0 / width) + EPSILON)
        rr[m, 0] = jnp.broadcast_to(factor_q, (16, 128))
        rr[m, 1] = jnp.broadcast_to(factor_k, (16, 128))
        query = (total[:, :512] * factor_q).astype(BF)
        key = (total[:, 640:1152] * factor_k).astype(BF)
        value = (total[:, 1152:1664] * factor_k).astype(BF)
        qs[m] = query
        ks[m] = key
        vs[m] = value
        contexts = []
        for h in range(2):
            cols = slice(h * HEAD_DIM, (h + 1) * HEAD_DIM)
            raised = jnp.exp(dot(query[:, cols], key[:, cols], NT) * HEAD_DIM ** (-0.5))
            weight = (raised / jnp.sum(raised, axis=-1, keepdims=True)).astype(BF)
            ps[m, h] = weight.astype(F32)
            contexts.append(dot(weight, value[:, cols]).astype(BF))
        cs[m, c] = jnp.concatenate(contexts, axis=1)

        @pl.when(jnp.logical_not(spread_out))
        def _():
            remote(cs.at[m, c], cs.at[m, c], c_ss.at[m], c_rs.at[m], other).start()

        @pl.when(spread_out)
        def _():
            for k in range(8):
                send_any(
                    cs.at[m, c], ob.at[3, m, t, c], cb_ss.at[m, k], cb_rs.at[m], heads_of[k]
                )

    def output(m):
        arrived(cs.at[m, c], c_rs.at[m])
        context = rows(cs[m])
        for k in ORDER:
            term = dot(context, w[3, lax.rem(j + k, 4)], NT)
            if k == 0:
                oown[m] = term
            else:
                ost[m, k - 1] = term.astype(BF)
                remote(
                    ost.at[m, k - 1], orecv.at[m, k - 1], o_ss.at[m, k - 1], o_rs.at[m], member(k)
                ).start()

    def advance(m):
        total = rows(xs[sel, m, j]).astype(F32) + oown[m]
        arrived(orecv.at[m], o_rs.at[m])
        for k in range(3):
            total = total + orecv[m, k].astype(F32)
        xn[m] = total.astype(BF).reshape(2, 16, 512)
        for k in ORDER:
            remote(
                xn.at[m], xs.at[sel, m, j], n_ss.at[m, k], x_rs.at[sel, m, j], member(k), s + 1
            ).start()

    def forward_step(i):
        @pl.when((i < MICRO) & spread_out)
        def _():
            project_first(i)

        @pl.when((i > 2) & spread_out)
        def _():
            advance_first(i - 3)

        @pl.when((i > 1) & (i < MICRO + 2) & spread_out)
        def _():
            output_first(i - 2)

        begun = jnp.where(s == SPREAD, 2, 0)

        @pl.when((i >= begun) & (i < MICRO) & jnp.logical_not(decoder | spread_out))
        def _():
            project_all(i)

        @pl.when((i < MICRO - 1) & (s == 4))
        def _():
            project_query(i + 1)

        @pl.when(((i < MICRO) & (s == 4)) | ((i < MICRO - 1) & (s > 4)))
        def _():
            project_key(i + jnp.where(s > 4, 1, 0))

        @pl.when((i < MICRO) & (s > 4))
        def _():
            project_query(i)

            @pl.when(i < MICRO - 2)
            def _():
                relay(i + 2)

        @pl.when((i > 0) & (i <= MICRO) & (s >= SPREAD) & (s < 7))
        def _():
            advance(i - 1)

        late = jnp.where(spread_out, 1, 0)

        @pl.when((i >= jnp.where(s == SPREAD, 1, late)) & (i < MICRO + late))
        def _():
            attend(i - late)

        @pl.when((i < MICRO) & (s >= SPREAD) & (s < 7))
        def _():
            output(i)

    def to_owners(src_of, slot, m=None):
        for b in range(4):
            dst = ob.at[slot, :, t] if m is None else ob.at[slot, m, t]
            send_any(src_of(b), dst, b_ss.at[slot, b], b_rs.at[slot], owner[b])

    def owners_sent(src_of, slot):
        for b in range(4):
            sent_any(src_of(b), b_ss.at[slot, b], owner[b])

    def project_back(m):
        total = None
        for k in ORDER:
            block = block_at(k)
            arrived(xs.at[2, m, block], x_rs.at[2, m, block])
            term = dot(rows(xs[2, m, block]), w[3, block])
            total = term if total is None else total + term
        dpart[m] = total.reshape(2, 16, 512)
        remote(dpart.at[m, 1 - c], drecv.at[m], d_ss.at[m], d_rs.at[m], other).start()

    def attend_back(m):
        query, key, value = qs[m], ks[m], vs[m]
        arrived(drecv.at[m], d_rs.at[m])
        grad = (dpart[m, c] + drecv[m]).astype(BF)
        pieces = [[], [], []]
        for h in range(2):
            cols = slice(h * HEAD_DIM, (h + 1) * HEAD_DIM)
            weight = ps[m, h]
            grad_weight = dot(grad[:, cols], value[:, cols], NT)
            pieces[2].append(dot(weight.astype(BF), grad[:, cols], TN))
            inside = jnp.sum(grad_weight * weight, axis=-1, keepdims=True)
            scores = (weight * (grad_weight - inside) * HEAD_DIM ** (-0.5)).astype(BF)
            pieces[0].append(dot(scores, key[:, cols]))
            pieces[1].append(dot(scores, query[:, cols], TN))
        grads = [jnp.concatenate(piece, axis=1) for piece in pieces]
        factors = [rr[m, 0][:, :1], rr[m, 1][:, :1], rr[m, 1][:, :1]]
        for i in range(3):
            dd[m, i, c] = (grads[i] * factors[i]).astype(BF)
        remote(dd.at[m, :, c], dd.at[m, :, c], dd_ss.at[m], dd_rs.at[m], other).start()
        means = [
            jnp.sum(g * v.astype(F32), axis=-1, keepdims=True) * (1.0 / width)
            for g, v in zip(grads, (query, key, value))
        ]
        cc[m, 0, c] = jnp.broadcast_to(means[0] * factors[0] * factors[0], (16, 128))
        cc[m, 1, c] = jnp.broadcast_to((means[1] + means[2]) * factors[1] * factors[1], (16, 128))
        remote(cc.at[m, :, c], cc.at[m, :, c], cc_ss.at[m], cc_rs.at[m], other).start()

    def spread_back(m):
        arrived(dd.at[m, :, c], dd_rs.at[m])
        arrived(cc.at[m, :, c], cc_rs.at[m])

        def spread(pairs, stream, kinds, own, stage, recv, ss, rs):
            lefts = [rows(dd[m, i]) for i in pairs]
            shift = sum(cc[m, i].reshape(32, 128)[:, :1] for i in kinds)
            for k in ORDER:
                block = lax.rem(j + k, 4)
                term = -rows(xs[stream, m, block]).astype(F32) * shift
                for i, left in zip(pairs, lefts):
                    term = term + dot(left, wt[i, block])
                if k == 0:
                    own[m] = term
                else:
                    stage[m, k - 1] = term.astype(BF)
                    remote(
                        stage.at[m, k - 1], recv.at[m, k - 1], ss.at[m, k - 1], rs.at[m], member(k)
                    ).start()

        @pl.when((s > 0) & (s < 4))
        def _():
            spread((0, 1, 2), 0, (0, 1), uown, ust, urecv, u_ss, u_rs)

        @pl.when(s > 4)
        def _():
            spread((0,), 1, (0,), uown, ust, urecv, u_ss, u_rs)

        @pl.when(s >= 4)
        def _():
            spread((1, 2), 0, (1,), wown, wst, wrecv, w_ss, w_rs)

    def hand_back(m):
        for k in ORDER:
            remote(
                gn.at[m], xs.at[2, m, j], gn_ss.at[m, k], x_rs.at[2, m, j], member(k), s - 1
            ).start()

    def advance_back(m):
        total = rows(xs[2, m, j]).astype(F32) + uown[m]
        arrived(urecv.at[m], u_rs.at[m])
        for k in range(3):
            total = total + urecv[m, k].astype(F32)
        gn[m] = total.astype(BF).reshape(2, 16, 512)
        hand_back(m)

    def advance_key(m):
        arrived(wrecv.at[m], w_rs.at[m])
        total = wown[m]
        for k in range(3):
            total = total + wrecv[m, k].astype(F32)
        geout[m] = total.astype(BF).reshape(2, 16, 512)

        @pl.when(s < 7)
        def _():
            arrived(gein.at[m], e_rs.at[m])
            geout[m] = (total + rows(gein[m]).astype(F32)).astype(BF).reshape(2, 16, 512)

        @pl.when(s > 4)
        def _():
            remote(geout.at[m], gein.at[m], e_ss.at[m], e_rs.at[m], (d, p), s - 1).start()

        @pl.when(s == 4)
        def _():
            gn[m] = geout[m]
            hand_back(m)

    def backward_step(i):
        @pl.when(i < MICRO)
        def _():
            project_back(i)

        @pl.when((i < MICRO) & (s < 4))
        def _():
            attend_back(i)

        @pl.when((i > 0) & (s > 0) & (s != 4))
        def _():
            advance_back(i - 1)

        @pl.when((i > 0) & (s == 4))
        def _():
            advance_key(i - 1)

        @pl.when((i < MICRO) & (s >= 4))
        def _():
            attend_back(i)

        @pl.when(i < MICRO)
        def _():
            spread_back(i)

            @pl.when(s < 2)
            def _():
                to_owners(lambda b: xs.at[2, i, b], 2, i)
                for k in range(3):
                    to_owners(lambda b: dd.at[i, k], 4 + k, i)

        @pl.when((i > 0) & (s > 4))
        def _():
            advance_key(i - 1)

    def last_step(i):
        @pl.when(i < MICRO)
        def _():
            project_query(i)

        @pl.when(i > 0)
        def _():
            advance_back(i - 1)

        @pl.when(i < MICRO)
        def _():
            attend(i)
            attend_back(i)

        @pl.when(i < MICRO - 1)
        def _():
            project_key(i + 1)

        @pl.when(i < MICRO)
        def _():
            spread_back(i)

        @pl.when(i < MICRO - 2)
        def _():
            relay(i + 2)

        @pl.when(i > 0)
        def _():
            advance_key(i - 1)

    @pl.when(jnp.logical_not(spread_out))
    def _():
        when(s == SPREAD, project_all, 0)
        gather_one(6)

        @pl.when(s == SPREAD)
        def _():
            attend(0)
            project_all(1)

        gather_one(7)
        gather_end(6)

    def turn(which):
        wt[which // 4, lax.rem(which, 4)] = w[which // 4, lax.rem(which, 4)].T

    when(decoder, repeat, 0, 12, turn)

    @pl.when(s == 4)
    def _():
        project_query(0)

    @pl.when(s == 7)
    def _():
        def one(m, carry):
            project_back(m)
            return carry

        lax.fori_loop(0, MICRO, one, 0)

    @pl.when(s > 4)
    def _():
        relay(0)
        relay(1)
        project_key(0)

    def forward_to_owners():
        to_owners(lambda b: xs.at[sel, :, b], 0)
        to_owners(lambda b: cs, 3)

    def step(n, carry):
        @pl.when((s == 7) & (n <= MICRO))
        def _():
            last_step(n)

        @pl.when((s < 7) & (n <= MICRO + 2))
        def _():
            forward_step(n)

        @pl.when(n == MICRO + 3)
        def _():
            @pl.when((s >= SPREAD) & (s < 4))
            def _():
                forward_to_owners()

            @pl.when((s > 0) & spread_out)
            def _():
                for k in range(4):
                    send_any(
                        ob.at[0, :, p], xs.at[0, :, lax.rem(d, 4)], xa_ss.at[k], xa_rs, tokens_at[k]
                    )

            @pl.when(spread_out)
            def _():
                gather_some(6)
                gather_one(6)
                gather_one(7)
                gather_end(6)

            when((s > 0) & (s < 4), repeat, 0, 12, turn)

            @pl.when((s > 0) & spread_out)
            def _():
                arrived(xs.at[0], xa_rs)

        @pl.when((s < 7) & (n >= MICRO + 3))
        def _():
            backward_step(n - MICRO - 3)

        return carry

    lax.fori_loop(0, 2 * MICRO + 4, step, 0)

    @pl.when(s > 1)
    def _():
        to_owners(lambda b: xs.at[2, :, b], 2)
        for i in range(3):
            to_owners(lambda b: dd.at[:, i], 4 + i)

    @pl.when(decoder)
    def _():
        @pl.when(s == 7)
        def _():
            for m in range(MICRO):
                arrived(cs.at[m, c], c_rs.at[m])

        forward_to_owners()
        to_owners(lambda b: xs.at[0, :, b], 1)

    key_slot = jnp.where(decoder, 1, 0)

    @pl.when(s >= SPREAD)
    def _():
        arrived(ob.at[3], b_rs.at[3])

    arrived(ob.at[2], b_rs.at[2])
    out_ref[3] = dot(ob[2].reshape(512, 512), ob[3].reshape(512, 512), TN).astype(BF)

    @pl.when(s >= SPREAD)
    def _():
        arrived(ob.at[0], b_rs.at[0])

    @pl.when(decoder)
    def _():
        arrived(ob.at[1], b_rs.at[1])

    for i in range(3):
        arrived(ob.at[4 + i], b_rs.at[4 + i])
        left = ob[0] if i == 0 else ob[key_slot]
        out_ref[i] = dot(left.reshape(512, 512), ob[4 + i].reshape(512, 512), TN).astype(BF)

    @pl.when(starts)
    def _():
        for m in range(MICRO):
            for k in range(8):
                sent_any(seed.at[m, 0], i_ss.at[m, k], start_to[k // 2])

    @pl.when(s == 0)
    def _():
        for m in range(MICRO):
            for k in range(8):
                sent_any(seed.at[m, 0], i_ss.at[m, k], first_to[k])

    @pl.when((s > 0) & spread_out)
    def _():
        for k in range(4):
            sent_any(ob.at[0, :, 0], xa_ss.at[k], tokens_at[k])

    def given(piece, carry):
        sent_any(own_shard(piece), ga_ss.at[piece], collector)
        arrived(shard(piece, 0), gc_ss.at[piece])

        @pl.when(inner)
        def _():
            for k in range(2):
                arrived(shards(piece, 0, 2), gb_ss.at[piece, k])

        return carry

    lax.fori_loop(0, 8, given, 0)


    @pl.when(s >= SPREAD)
    def _():
        owners_sent(lambda b: xs.at[sel, :, b], 0)
        owners_sent(lambda b: cs, 3)

    @pl.when(decoder)
    def _():
        owners_sent(lambda b: xs.at[0, :, b], 1)

    owners_sent(lambda b: xs.at[2, :, b], 2)
    for i in range(3):
        owners_sent(lambda b: dd.at[:, i], 4 + i)

    def finish(m, carry):
        @pl.when(decoder)
        def _():
            arrived(part.at[m, 0, :, pl.ds(0, 640)], q_ss.at[m])
            arrived(part.at[m, 0, :, pl.ds(640, 1152)], kv_ss.at[m])

        @pl.when(jnp.logical_not(decoder | spread_out))
        def _():
            arrived(part.at[m, 0], q_ss.at[m])

        @pl.when(jnp.logical_not(spread_out))
        def _():
            arrived(cs.at[m, 0], c_ss.at[m])

        @pl.when(spread_out)
        def _():
            for k in range(8):
                sent_any(sb.at[m, 0, 0], rb_ss.at[m, k], heads_at[k])
                sent_any(cs.at[m, 0], cb_ss.at[m, k], heads_of[k])

        arrived(dpart.at[m, 0], d_ss.at[m])
        arrived(dd.at[m, :, 0], dd_ss.at[m])
        arrived(cc.at[m, :, 0], cc_ss.at[m])

        @pl.when(decoder & (s < 7))
        def _():
            arrived(xs.at[0, m, 0], f_ss.at[m])

        @pl.when(s > 4)
        def _():
            for k in range(3):
                arrived(xs.at[0, m, 0], fp_ss.at[m, k])

        @pl.when(s < 7)
        def _():
            for k in range(3):
                arrived(ost.at[m, k], o_ss.at[m, k])
            for k in range(4):
                arrived(xn.at[m], n_ss.at[m, k])

        @pl.when((s > 0) & (s != 4))
        def _():
            for k in range(3):
                arrived(ust.at[m, k], u_ss.at[m, k])

        @pl.when(s > 0)
        def _():
            for k in range(4):
                arrived(gn.at[m], gn_ss.at[m, k])

        @pl.when(s >= 4)
        def _():
            for k in range(3):
                arrived(wst.at[m, k], w_ss.at[m, k])

        @pl.when(s > 4)
        def _():
            arrived(geout.at[m], e_ss.at[m])

        return carry

    lax.fori_loop(0, MICRO, finish, 0)


def per_device(enc_input, dec_input, cotangent, target_lengths, weights):
    tokens = MICRO * lax.axis_size("dp") * enc_input.shape[1] * enc_input.shape[2]
    dma = pltpu.SemaphoreType.DMA
    tile = (2, 16, 512)
    scratch = [
        pltpu.VMEM((4, 4, 512, 512), BF),
        pltpu.VMEM((3, 4, 512, 512), BF),
        pltpu.VMEM((4, 512, 512), BF),
        pltpu.VMEM((3, MICRO, 4) + tile, BF),
        pltpu.VMEM((MICRO, 4, 2, 16, 1664), BF),
        pltpu.VMEM((MICRO, 8, 16, 1664), BF),
        pltpu.VMEM((16, 1792), F32),
        pltpu.VMEM((MICRO, 2, 16, 512), BF),
        pltpu.VMEM((MICRO, 16, 1024), BF),
        pltpu.VMEM((MICRO, 2, 16, 1792), F32),
        pltpu.VMEM((MICRO, 16, 1792), F32),
        pltpu.VMEM((MICRO, 16, 512), BF),
        pltpu.VMEM((MICRO, 16, 512), BF),
        pltpu.VMEM((MICRO, 16, 512), BF),
        pltpu.VMEM((MICRO, 2, 16, 16), F32),
        pltpu.VMEM((MICRO, 2, 16, 128), F32),
        pltpu.VMEM((MICRO,) + tile, BF),
        pltpu.VMEM((MICRO, 32, 512), F32),
        pltpu.VMEM((MICRO, 3, 32, 512), BF),
        pltpu.VMEM((MICRO, 3, 32, 512), BF),
        pltpu.VMEM((MICRO,) + tile, BF),
        pltpu.VMEM((MICRO,) + tile, F32),
        pltpu.VMEM((MICRO, 16, 512), F32),
        pltpu.VMEM((MICRO, 3) + tile, BF),
        pltpu.VMEM((MICRO, 2, 2, 16, 128), F32),
        pltpu.VMEM((MICRO, 32, 512), F32),
        pltpu.VMEM((MICRO, 3, 32, 512), BF),
        pltpu.VMEM((MICRO, 3, 32, 512), BF),
        pltpu.VMEM((MICRO, 32, 512), F32),
        pltpu.VMEM((MICRO, 3, 32, 512), BF),
        pltpu.VMEM((MICRO, 3, 32, 512), BF),
        pltpu.VMEM((MICRO,) + tile, BF),
        pltpu.VMEM((MICRO,) + tile, BF),
        pltpu.VMEM((MICRO,) + tile, BF),
        pltpu.VMEM((7, MICRO, 4) + tile, BF),
        dma, dma,
        dma((MICRO, 8)), dma((MICRO,)),
        dma((MICRO, 8)), dma((MICRO,)),
        dma((MICRO, 4)), dma((4,)), dma,
        dma((8,)), dma((8,)),
        dma((8, 2)), dma((8,)),
        dma((8,)), dma((8,)),
        dma((MICRO, 8)), dma((3, MICRO, 4)),
        dma((MICRO,)), dma((MICRO, 3)),
        dma((MICRO,)), dma((MICRO,)),
        dma((MICRO,)), dma((MICRO,)),
        dma((MICRO,)), dma((MICRO,)),
        dma((MICRO, 3)), dma((MICRO,)),
        dma((MICRO, 4)),
        dma((MICRO,)), dma((MICRO,)),
        dma((MICRO,)), dma((MICRO,)),
        dma((MICRO,)), dma((MICRO,)),
        dma((MICRO, 3)), dma((MICRO,)),
        dma((MICRO, 3)), dma((MICRO,)),
        dma((MICRO,)), dma((MICRO,)),
        dma((MICRO, 4)),
        dma((7, 4)), dma((7,)),
    ]
    grads = pl.pallas_call(
        functools.partial(layer_kernel, 4096, float(tokens) ** (-0.5)),
        out_shape=jax.ShapeDtypeStruct((4, 512, 512), BF),
        in_specs=[pl.BlockSpec(memory_space=pltpu.SMEM)] + [pl.BlockSpec(memory_space=pl.ANY)] * 4,
        out_specs=pl.BlockSpec(memory_space=pltpu.VMEM),
        scratch_shapes=scratch,
        compiler_params=pltpu.CompilerParams(
            collective_id=0, has_side_effects=True, vmem_limit_bytes=60 << 20
        ),
        name="layers",
    )(target_lengths, enc_input, dec_input, cotangent, weights)
    return grads[None].astype(F32)


def solution(mesh):
    in_specs = (
        P(None, "dp", None, "mp"),
        P(None, "dp", None, "mp"),
        P(None, "dp", None, "mp"),
        P(None, "dp"),
        P("section", None, "dp", "mp"),
    )
    return jax.shard_map(
        per_device,
        mesh=mesh,
        in_specs=in_specs,
        out_specs=P("section", None, "dp", "mp"),
        check_vma=False,
    )
```

```python
import functools

import jax
import jax.numpy as jnp
from jax import lax
from jax.experimental import pallas as pl
from jax.experimental.pallas import tpu as pltpu
from jax.sharding import PartitionSpec as P

HEAD_DIM = 256
EPSILON = 1e-06
MICRO = 4
BF = jnp.bfloat16
F32 = jnp.float32
MESH = pl.DeviceIdType.MESH
SPREAD = 2
ORDER = (2, 1, 3, 0)
NT = (((1,), (1,)), ((), ()))
NN = (((1,), (0,)), ((), ()))
TN = (((0,), (0,)), ((), ()))


def dot(a, b, dims=NN):
    return lax.dot_general(a, b, dims, preferred_element_type=F32)


def layer_kernel(
    width, loss_scale,
    lengths_ref, enc_ref, dec_ref, cot_ref, weights_ref, out_ref,
    w, wt, wl, xs, sb, rb, tot, seed, seed_in, part, qrecv, qs, ks, vs, ps, rr, cs, oown, ost, orecv, xn,
    dpart, drecv, dd, cc, uown, ust, urecv, wown, wst, wrecv, gn, gein, geout, ob,
    s_sem, l_sem, rb_ss, rb_rs, cb_ss, cb_rs, xb_rs, xa_ss, xa_rs, ga_ss, ga_rs, gb_ss, gb_rs, gc_ss, gc_rs, i_ss, x_rs, f_ss, fp_ss, q_ss, q_rs, kv_ss, kv_rs,
    c_ss, c_rs, o_ss, o_rs, n_ss,
    d_ss, d_rs, dd_ss, dd_rs, cc_ss, cc_rs, u_ss, u_rs, w_ss, w_rs, e_ss, e_rs, gn_ss,
    b_ss, b_rs,
):
    s = lax.axis_index("section")
    d = lax.axis_index("dp")
    p = lax.axis_index("mp")
    t = d // 2
    c = lax.rem(p, 2)
    j = 2 * (p // 2) + lax.rem(d, 2)
    odd = lax.rem(t, 2)
    decoder = s >= 4
    sel = jnp.where(decoder, 1, 0)
    spread_out = s < SPREAD
    starts = (s == 4) | (s == 7)
    other = (d, p + 1 - 2 * c)

    def place(tt, jj, ccc):
        return 2 * tt + lax.rem(jj, 2), 2 * (jj // 2) + ccc

    def member(k):
        return place(t, lax.rem(j + k, 4), c)

    def fellow(k):
        return d, lax.rem(p + k, 4)

    def column(tt):
        return 2 * tt + lax.rem(d, 2), p

    collector = place(t, p, d // 4)
    inner = t // 2 == c
    beside = column(t + 1 - 2 * odd)
    across = column(lax.rem(t + 3 - 2 * odd, 4))
    senders = [place(k, p, d // 4) for k in range(4)]
    owner = [(4 * c + b, j) for b in range(4)]
    heads_at = [place(q, p, e) for q in range(4) for e in range(2)]
    heads_of = [(jnp.int32(k), j) for k in range(8)]
    tokens_at = [place(p, jnp.int32(k), d // 4) for k in range(4)]
    tokens_of = [(4 * c + b, t) for b in range(4)]
    start_to = [place(t, jnp.int32(k), p // 2) for k in range(4)]
    start_from = [(2 * t + a, 2 * c + e) for a in range(2) for e in range(2)]
    first_to = [(2 * p + e, jnp.int32(k)) for k in range(4) for e in range(2)]
    first_from = [(jnp.int32(k), d // 2) for k in range(8)]

    def same(dev):
        return (dev[0] == d) & (dev[1] == p)

    def remote(src, dst, ss, rs, dev, sec=None):
        ids = {"dp": dev[0], "mp": dev[1]}
        if sec is not None:
            ids["section"] = sec
        return pltpu.make_async_remote_copy(
            src_ref=src, dst_ref=dst, send_sem=ss, recv_sem=rs, device_id=ids, device_id_type=MESH
        )

    def arrived(ref, sem):
        pltpu.make_async_copy(ref, ref, sem).wait()

    def send_any(src, dst, ss, rs, dev):
        here = same(dev)

        @pl.when(here)
        def _():
            pltpu.make_async_copy(src, dst, rs).start()

        @pl.when(jnp.logical_not(here))
        def _():
            remote(src, dst, ss, rs, dev).start()

    def sent_any(src, ss, dev):
        @pl.when(jnp.logical_not(same(dev)))
        def _():
            arrived(src, ss)

    bar = pltpu.get_barrier_semaphore()

    def greet(dev, sec=None):
        ids = {"dp": dev[0], "mp": dev[1]}
        if sec is not None:
            ids["section"] = sec
        pl.semaphore_signal(bar, inc=1, device_id=ids, device_id_type=MESH)

    def greet_other(dev):
        @pl.when(jnp.logical_not(same(dev)))
        def _():
            greet(dev)

    greet(other)
    greet(beside)
    greet(across)
    for k in range(1, 4):
        greet(member(k))

    @pl.when(spread_out)
    def _():
        for k in range(1, 4):
            greet(fellow(k))
        for dev in heads_at + heads_of:
            greet_other(dev)

    @pl.when((s > 0) & spread_out)
    def _():
        for k in range(4):
            greet(fellow(k), s - 1)
        for dev in tokens_of:
            greet_other(dev)

    @pl.when(s == SPREAD)
    def _():
        for dev in tokens_of:
            greet(dev, SPREAD - 1)

    @pl.when(s > SPREAD)
    def _():
        for k in range(4):
            greet(member(k), s - 1)

    @pl.when(s < 7)
    def _():
        for k in range(4):
            greet(member(k), s + 1)

    for dev in senders:
        greet_other(dev)

    @pl.when(inner)
    def _():
        for e in range(2):
            greet_other((2 * t + e, j))

    @pl.when(s == 0)
    def _():
        for dev in first_from:
            greet_other(dev)

    @pl.when(starts)
    def _():
        for dev in start_from:
            greet_other(dev)

    def others(devs):
        return sum(jnp.where(same(dev), 0, 1) for dev in devs)

    count = 6 + jnp.where(s > 0, 4, 0) + jnp.where(s < 7, 4, 0) + others(owner)
    count = count + others([collector]) + jnp.where(starts, others(start_to), 0)
    count = count + jnp.where(spread_out, 3 + others(heads_at) + others(heads_of), 0)
    count = count + jnp.where((s > 0) & spread_out, others(tokens_at), 0)
    count = count + jnp.where(s == 0, others(first_to), 0)
    pl.semaphore_wait(bar, count)

    def shards(piece, first, number):
        return w.at[piece // 2, pl.ds(first, number), pl.ds(256 * lax.rem(piece, 2), 256)]

    def shard(piece, which):
        return w.at[piece // 2, which, pl.ds(256 * lax.rem(piece, 2), 256)]

    def own_shard(piece):
        return weights_ref.at[0, piece // 2, pl.ds(256 * lax.rem(piece, 2), 256)]

    def give(piece):
        send_any(
            own_shard(piece), shard(piece, lax.rem(d, 4)), ga_ss.at[piece], ga_rs.at[piece],
            collector,
        )

    local = pltpu.make_async_copy(weights_ref.at[0], wl, l_sem)

    @pl.when(spread_out)
    def _():
        local.start()


    def begin(src_of, stream):
        for m in range(MICRO):
            for k in range(4):
                for e in range(2):
                    block = 2 * lax.rem(p, 2) + e
                    send_any(
                        src_of(m, e), xs.at[stream, m, block, lax.rem(d, 2)],
                        i_ss.at[m, 2 * k + e], x_rs.at[stream, m, block], start_to[k],
                    )

    @pl.when(s == 0)
    def _():
        for m in range(MICRO):
            for k in range(8):
                send_any(
                    enc_ref.at[m, 0, :, pl.ds(512 * (k % 2), 512)],
                    ob.at[0, m, t, lax.rem(d, 2)], i_ss.at[m, k], xb_rs.at[m, t], first_to[k],
                )

    @pl.when(s == 4)
    def _():
        begin(lambda m, e: dec_ref.at[m, 0, :, pl.ds(512 * e, 512)], 1)

    @pl.when(s == 7)
    def _():
        loss = pltpu.make_async_copy(cot_ref.at[:, 0], seed_in, s_sem)
        loss.start()
        loss.wait()
        for m in range(MICRO):
            offsets = lax.broadcasted_iota(jnp.int32, (16, 1024), 0)
            live = jnp.where(offsets < lengths_ref[m, 0], loss_scale, 0.0)
            value = (seed_in[m].astype(F32) * live).astype(BF)
            for e in range(2):
                seed[m, e] = value[:, 512 * e:512 * e + 512]
        begin(lambda m, e: seed.at[m, e], 2)

    def pass_on(piece):
        arrived(shards(piece, 2 * (1 - odd), 2), gb_rs.at[piece])
        half = shard(piece, 2 * (1 - odd))
        remote(half, half, gc_ss.at[piece], gc_rs.at[piece], across).start()

    def collected(piece):
        mine = shards(piece, 2 * odd, 2)
        arrived(mine, ga_rs.at[piece])
        remote(mine, mine, gb_ss.at[piece, 0], gb_rs.at[piece], beside).start()
        remote(mine, mine, gb_ss.at[piece, 1], gb_rs.at[piece], across).start()

    def swap(piece):
        arrived(shards(piece, 2 * (1 - odd), 2), gb_rs.at[piece])
        half = shard(piece, 2 * (1 - odd) + 1)
        remote(half, half, gc_ss.at[piece], gc_rs.at[piece], beside).start()

    def swapped(piece):
        arrived(shards(piece, 2 * odd, 2), gc_rs.at[piece])

    def when(cond, what, *args):
        @pl.when(cond)
        def _():
            what(*args)

    def repeat(first, last, what):
        def one(piece, carry):
            what(piece)
            return carry

        lax.fori_loop(first, last, one, 0)

    def collect_on(piece):
        collected(piece)
        when(piece > 0, pass_on, piece - 1)

    def gather_some(pieces):
        repeat(0, 8, give)

        @pl.when(inner)
        def _():
            repeat(0, pieces + 1, collect_on)
            repeat(pieces + 1, 8, collected)

        @pl.when(jnp.logical_not(inner))
        def _():
            repeat(0, pieces, swap)
            repeat(0, pieces, swapped)

    def gather_one(piece):
        when(inner, pass_on, piece)
        when(jnp.logical_not(inner), swap, piece)

    def gather_end(pieces):
        @pl.when(jnp.logical_not(inner))
        def _():
            repeat(pieces, 8, swapped)

    when(jnp.logical_not(spread_out), gather_some, 6)

    @pl.when(spread_out)
    def _():
        local.wait()

    def rows(value):
        return value.reshape(32, 512)

    def block_at(k):
        return lax.rem(j + 4 - k, 4)

    def project(m, stream, mats, start, ss, rs, relayed=None):
        sums = [None] * len(mats)
        squares = None
        for k in ORDER:
            block = block_at(k)
            if k == 0 and relayed is not None:
                @pl.when(jnp.logical_not(relayed))
                def _():
                    arrived(xs.at[stream, m, block], x_rs.at[stream, m, block])
            else:
                arrived(xs.at[stream, m, block], x_rs.at[stream, m, block])
            left = rows(xs[stream, m, block])
            wide = left.astype(F32)
            square = jnp.sum(wide * wide, axis=-1, keepdims=True)
            squares = square if squares is None else squares + square
            for i, mat in enumerate(mats):
                term = dot(left, w[mat, block])
                sums[i] = term if sums[i] is None else sums[i] + term
        squares = jnp.broadcast_to(squares, (32, 128)).reshape(2, 16, 128)
        for i, mat in enumerate(mats):
            first = (0, 640, 1152)[mat]
            part[m, :, :, first:first + 512] = sums[i].reshape(2, 16, 512)
        if 0 in mats:
            part[m, :, :, 512:640] = squares
        if 1 in mats:
            part[m, :, :, 1664:1792] = squares
        cols = pl.ds(*start)
        remote(part.at[m, 1 - c, :, cols], qrecv.at[m, :, cols], ss.at[m], rs.at[m], other).start()

    def project_all(m):
        project(m, 0, (0, 1, 2), (0, 1792), q_ss, q_rs)

    def project_query(m):
        project(m, 1, (0,), (0, 640), q_ss, q_rs)

    def project_key(m):
        project(m, 0, (1, 2), (640, 1152), kv_ss, kv_rs, s > 4)

        @pl.when(s == 4)
        def _():
            onward(m)

    def onward(m):
        remote(
            xs.at[0, m, j], xs.at[0, m, j], f_ss.at[m], x_rs.at[0, m, j], (d, p), s + 1
        ).start()

    def relay(m):
        arrived(xs.at[0, m, j], x_rs.at[0, m, j])

        @pl.when(s < 7)
        def _():
            onward(m)

        for k in (2, 1, 3):
            remote(
                xs.at[0, m, j], xs.at[0, m, j], fp_ss.at[m, k - 1], x_rs.at[0, m, j], member(k)
            ).start()

    def project_first(m):
        for k in ORDER:
            quarter = lax.rem(p + 4 - k, 4)
            arrived(ob.at[0, m, quarter], xb_rs.at[m, quarter])
            left = rows(ob[0, m, quarter])
            wide = left.astype(F32)
            square = jnp.sum(wide * wide, axis=-1, keepdims=True)
            high = square.astype(BF)
            low = (square - high.astype(F32)).astype(BF)
            for i in range(3):
                sb[m, quarter, :, :, 512 * i:512 * i + 512] = dot(left, wl[i]).astype(BF).reshape(
                    2, 16, 512
                )
            lane = lax.broadcasted_iota(jnp.int32, (32, 128), 1)
            parts = jnp.where(
                lane < 64, jnp.broadcast_to(high.astype(F32), (32, 128)),
                jnp.broadcast_to(low.astype(F32), (32, 128)),
            )
            sb[m, quarter, :, :, 1536:] = parts.astype(BF).reshape(2, 16, 128)
            for e in range(2):
                send_any(
                    sb.at[m, quarter, e], rb.at[m, d], rb_ss.at[m, 2 * quarter + e], rb_rs.at[m],
                    place(quarter, p, e),
                )

    def output_first(m):
        arrived(ob.at[3, m], cb_rs.at[m])
        for k in ORDER:
            term = dot(rows(ob[3, m, lax.rem(p + k, 4)]), wl[3], NT)
            if k == 0:
                oown[m] = term
            else:
                ost[m, k - 1] = term.astype(BF)
                remote(
                    ost.at[m, k - 1], orecv.at[m, k - 1], o_ss.at[m, k - 1], o_rs.at[m], fellow(k)
                ).start()

    def advance_first(m):
        total = rows(ob[0, m, p]).astype(F32) + oown[m]
        arrived(orecv.at[m], o_rs.at[m])
        for k in range(3):
            total = total + orecv[m, k].astype(F32)
        xn[m] = total.astype(BF).reshape(2, 16, 512)

        @pl.when(s < SPREAD - 1)
        def _():
            for k in ORDER:
                remote(
                    xn.at[m], ob.at[0, m, p], n_ss.at[m, k], xb_rs.at[m, p], fellow(k), s + 1
                ).start()

        @pl.when(s == SPREAD - 1)
        def _():
            block = lax.rem(d, 4)
            for k in ORDER:
                remote(
                    xn.at[m], xs.at[0, m, block], n_ss.at[m, k], x_rs.at[0, m, block],
                    place(p, lax.rem(j + k, 4), d // 4), s + 1,
                ).start()

    def attend(m):
        @pl.when(decoder)
        def _():
            arrived(qrecv.at[m, :, pl.ds(0, 640)], q_rs.at[m])
            arrived(qrecv.at[m, :, pl.ds(640, 1152)], kv_rs.at[m])

        @pl.when(jnp.logical_not(decoder | spread_out))
        def _():
            arrived(qrecv.at[m], q_rs.at[m])

        @pl.when(jnp.logical_not(spread_out))
        def _():
            tot[...] = part[m, c] + qrecv[m]

        @pl.when(spread_out)
        def _():
            arrived(rb.at[m], rb_rs.at[m])
            summed = rb[m, 0].astype(F32)
            for k in range(1, 8):
                summed = summed + rb[m, k].astype(F32)
            square = summed[:, 1536:1537] + summed[:, 1600:1601]
            square = jnp.broadcast_to(square, (16, 128))
            tot[:, :512] = summed[:, :512]
            tot[:, 512:640] = square
            tot[:, 640:1664] = summed[:, 512:1536]
            tot[:, 1664:] = square

        total = tot[...]
        factor_q = lax.rsqrt(total[:, 512:513] * (1.0 / width) + EPSILON)
        factor_k = lax.rsqrt(total[:, 1664:1665] * (1.0 / width) + EPSILON)
        rr[m, 0] = jnp.broadcast_to(factor_q, (16, 128))
        rr[m, 1] = jnp.broadcast_to(factor_k, (16, 128))
        query = (total[:, :512] * factor_q).astype(BF)
        key = (total[:, 640:1152] * factor_k).astype(BF)
        value = (total[:, 1152:1664] * factor_k).astype(BF)
        qs[m] = query
        ks[m] = key
        vs[m] = value
        contexts = []
        for h in range(2):
            cols = slice(h * HEAD_DIM, (h + 1) * HEAD_DIM)
            raised = jnp.exp(dot(query[:, cols], key[:, cols], NT) * HEAD_DIM ** (-0.5))
            weight = (raised / jnp.sum(raised, axis=-1, keepdims=True)).astype(BF)
            ps[m, h] = weight.astype(F32)
            contexts.append(dot(weight, value[:, cols]).astype(BF))
        cs[m, c] = jnp.concatenate(contexts, axis=1)

        @pl.when(jnp.logical_not(spread_out))
        def _():
            remote(cs.at[m, c], cs.at[m, c], c_ss.at[m], c_rs.at[m], other).start()

        @pl.when(spread_out)
        def _():
            for k in range(8):
                send_any(
                    cs.at[m, c], ob.at[3, m, t, c], cb_ss.at[m, k], cb_rs.at[m], heads_of[k]
                )

    def output(m):
        arrived(cs.at[m, c], c_rs.at[m])
        context = rows(cs[m])
        for k in ORDER:
            term = dot(context, w[3, lax.rem(j + k, 4)], NT)
            if k == 0:
                oown[m] = term
            else:
                ost[m, k - 1] = term.astype(BF)
                remote(
                    ost.at[m, k - 1], orecv.at[m, k - 1], o_ss.at[m, k - 1], o_rs.at[m], member(k)
                ).start()

    def advance(m):
        total = rows(xs[sel, m, j]).astype(F32) + oown[m]
        arrived(orecv.at[m], o_rs.at[m])
        for k in range(3):
            total = total + orecv[m, k].astype(F32)
        xn[m] = total.astype(BF).reshape(2, 16, 512)
        for k in ORDER:
            remote(
                xn.at[m], xs.at[sel, m, j], n_ss.at[m, k], x_rs.at[sel, m, j], member(k), s + 1
            ).start()

    def forward_step(i):
        @pl.when((i < MICRO) & spread_out)
        def _():
            project_first(i)

        @pl.when((i > 2) & spread_out)
        def _():
            advance_first(i - 3)

        @pl.when((i > 1) & (i < MICRO + 2) & spread_out)
        def _():
            output_first(i - 2)

        begun = jnp.where(s == SPREAD, 2, 0)

        @pl.when((i >= begun) & (i < MICRO) & jnp.logical_not(decoder | spread_out))
        def _():
            project_all(i)

        @pl.when((i < MICRO - 1) & (s == 4))
        def _():
            project_query(i + 1)

        @pl.when(((i < MICRO) & (s == 4)) | ((i < MICRO - 1) & (s > 4)))
        def _():
            project_key(i + jnp.where(s > 4, 1, 0))

        @pl.when((i < MICRO) & (s > 4))
        def _():
            project_query(i)

            @pl.when(i < MICRO - 2)
            def _():
                relay(i + 2)

        @pl.when((i > 0) & (i <= MICRO) & (s >= SPREAD) & (s < 7))
        def _():
            advance(i - 1)

        late = jnp.where(spread_out, 1, 0)

        @pl.when((i >= jnp.where(s == SPREAD, 1, late)) & (i < MICRO + late))
        def _():
            attend(i - late)

        @pl.when((i < MICRO) & (s >= SPREAD) & (s < 7))
        def _():
            output(i)

    def to_owners(src_of, slot, m=None):
        for b in range(4):
            dst = ob.at[slot, :, t] if m is None else ob.at[slot, m, t]
            send_any(src_of(b), dst, b_ss.at[slot, b], b_rs.at[slot], owner[b])

    def owners_sent(src_of, slot):
        for b in range(4):
            sent_any(src_of(b), b_ss.at[slot, b], owner[b])

    def project_back(m):
        total = None
        for k in ORDER:
            block = block_at(k)
            arrived(xs.at[2, m, block], x_rs.at[2, m, block])
            term = dot(rows(xs[2, m, block]), w[3, block])
            total = term if total is None else total + term
        dpart[m] = total.reshape(2, 16, 512)
        remote(dpart.at[m, 1 - c], drecv.at[m], d_ss.at[m], d_rs.at[m], other).start()

    def attend_back(m):
        query, key, value = qs[m], ks[m], vs[m]
        arrived(drecv.at[m], d_rs.at[m])
        grad = (dpart[m, c] + drecv[m]).astype(BF)
        pieces = [[], [], []]
        for h in range(2):
            cols = slice(h * HEAD_DIM, (h + 1) * HEAD_DIM)
            weight = ps[m, h]
            grad_weight = dot(grad[:, cols], value[:, cols], NT)
            pieces[2].append(dot(weight.astype(BF), grad[:, cols], TN))
            inside = jnp.sum(grad_weight * weight, axis=-1, keepdims=True)
            scores = (weight * (grad_weight - inside) * HEAD_DIM ** (-0.5)).astype(BF)
            pieces[0].append(dot(scores, key[:, cols]))
            pieces[1].append(dot(scores, query[:, cols], TN))
        grads = [jnp.concatenate(piece, axis=1) for piece in pieces]
        factors = [rr[m, 0][:, :1], rr[m, 1][:, :1], rr[m, 1][:, :1]]
        for i in range(3):
            dd[m, i, c] = (grads[i] * factors[i]).astype(BF)
        remote(dd.at[m, :, c], dd.at[m, :, c], dd_ss.at[m], dd_rs.at[m], other).start()
        means = [
            jnp.sum(g * v.astype(F32), axis=-1, keepdims=True) * (1.0 / width)
            for g, v in zip(grads, (query, key, value))
        ]
        cc[m, 0, c] = jnp.broadcast_to(means[0] * factors[0] * factors[0], (16, 128))
        cc[m, 1, c] = jnp.broadcast_to((means[1] + means[2]) * factors[1] * factors[1], (16, 128))
        remote(cc.at[m, :, c], cc.at[m, :, c], cc_ss.at[m], cc_rs.at[m], other).start()

    def spread_back(m):
        arrived(dd.at[m, :, c], dd_rs.at[m])
        arrived(cc.at[m, :, c], cc_rs.at[m])

        def spread(pairs, stream, kinds, own, stage, recv, ss, rs):
            lefts = [rows(dd[m, i]) for i in pairs]
            shift = sum(cc[m, i].reshape(32, 128)[:, :1] for i in kinds)
            for k in ORDER:
                block = lax.rem(j + k, 4)
                term = -rows(xs[stream, m, block]).astype(F32) * shift
                for i, left in zip(pairs, lefts):
                    term = term + dot(left, wt[i, block])
                if k == 0:
                    own[m] = term
                else:
                    stage[m, k - 1] = term.astype(BF)
                    remote(
                        stage.at[m, k - 1], recv.at[m, k - 1], ss.at[m, k - 1], rs.at[m], member(k)
                    ).start()

        @pl.when((s > 0) & (s < 4))
        def _():
            spread((0, 1, 2), 0, (0, 1), uown, ust, urecv, u_ss, u_rs)

        @pl.when(s > 4)
        def _():
            spread((0,), 1, (0,), uown, ust, urecv, u_ss, u_rs)

        @pl.when(s >= 4)
        def _():
            spread((1, 2), 0, (1,), wown, wst, wrecv, w_ss, w_rs)

    def hand_back(m):
        for k in ORDER:
            remote(
                gn.at[m], xs.at[2, m, j], gn_ss.at[m, k], x_rs.at[2, m, j], member(k), s - 1
            ).start()

    def advance_back(m):
        total = rows(xs[2, m, j]).astype(F32) + uown[m]
        arrived(urecv.at[m], u_rs.at[m])
        for k in range(3):
            total = total + urecv[m, k].astype(F32)
        gn[m] = total.astype(BF).reshape(2, 16, 512)
        hand_back(m)

    def advance_key(m):
        arrived(wrecv.at[m], w_rs.at[m])
        total = wown[m]
        for k in range(3):
            total = total + wrecv[m, k].astype(F32)
        geout[m] = total.astype(BF).reshape(2, 16, 512)

        @pl.when(s < 7)
        def _():
            arrived(gein.at[m], e_rs.at[m])
            geout[m] = (total + rows(gein[m]).astype(F32)).astype(BF).reshape(2, 16, 512)

        @pl.when(s > 4)
        def _():
            remote(geout.at[m], gein.at[m], e_ss.at[m], e_rs.at[m], (d, p), s - 1).start()

        @pl.when(s == 4)
        def _():
            gn[m] = geout[m]
            hand_back(m)

    def backward_step(i):
        @pl.when(i < MICRO)
        def _():
            project_back(i)

        @pl.when((i < MICRO) & (s < 4))
        def _():
            attend_back(i)

        @pl.when((i > 0) & (s > 0) & (s != 4))
        def _():
            advance_back(i - 1)

        @pl.when((i > 0) & (s == 4))
        def _():
            advance_key(i - 1)

        @pl.when((i < MICRO) & (s >= 4))
        def _():
            attend_back(i)

        @pl.when(i < MICRO)
        def _():
            spread_back(i)

            @pl.when((s == 0) | ((s == 1) & (i < 2)))
            def _():
                to_owners(lambda b: xs.at[2, i, b], 2, i)
                for k in range(3):
                    to_owners(lambda b: dd.at[i, k], 4 + k, i)

        @pl.when((i > 0) & (s > 4))
        def _():
            advance_key(i - 1)

    def last_step(i):
        @pl.when(i < MICRO)
        def _():
            project_query(i)

        @pl.when(i > 0)
        def _():
            advance_back(i - 1)

        @pl.when(i < MICRO)
        def _():
            attend(i)
            attend_back(i)

        @pl.when(i < MICRO - 1)
        def _():
            project_key(i + 1)

        @pl.when(i < MICRO)
        def _():
            spread_back(i)

        @pl.when(i < MICRO - 2)
        def _():
            relay(i + 2)

        @pl.when(i > 0)
        def _():
            advance_key(i - 1)

    @pl.when(jnp.logical_not(spread_out))
    def _():
        when(s == SPREAD, project_all, 0)
        gather_one(6)

        @pl.when(s == SPREAD)
        def _():
            attend(0)
            project_all(1)

        gather_one(7)
        gather_end(6)

    def turn(which):
        wt[which // 4, lax.rem(which, 4)] = w[which // 4, lax.rem(which, 4)].T

    when(decoder, repeat, 0, 12, turn)

    @pl.when(s == 4)
    def _():
        project_query(0)

    @pl.when(s == 7)
    def _():
        def one(m, carry):
            project_back(m)
            return carry

        lax.fori_loop(0, MICRO, one, 0)

    @pl.when(s > 4)
    def _():
        relay(0)
        relay(1)
        project_key(0)

    def forward_to_owners():
        to_owners(lambda b: xs.at[sel, :, b], 0)
        to_owners(lambda b: cs, 3)

    def step(n, carry):
        @pl.when((s == 7) & (n <= MICRO))
        def _():
            last_step(n)

        @pl.when((s < 7) & (n <= MICRO + 2))
        def _():
            forward_step(n)

        @pl.when(n == MICRO + 3)
        def _():
            @pl.when((s >= SPREAD) & (s < 4))
            def _():
                forward_to_owners()

            @pl.when((s > 0) & spread_out)
            def _():
                for k in range(4):
                    send_any(
                        ob.at[0, :, p], xs.at[0, :, lax.rem(d, 4)], xa_ss.at[k], xa_rs, tokens_at[k]
                    )

            @pl.when(spread_out)
            def _():
                gather_some(6)
                gather_one(6)
                gather_one(7)
                gather_end(6)

            when((s > 0) & (s < 4), repeat, 0, 12, turn)

            @pl.when((s > 0) & spread_out)
            def _():
                arrived(xs.at[0], xa_rs)

        @pl.when((s < 7) & (n >= MICRO + 3))
        def _():
            backward_step(n - MICRO - 3)

        return carry

    lax.fori_loop(0, 2 * MICRO + 4, step, 0)

    @pl.when(s == 1)
    def _():
        for m in range(2, MICRO):
            to_owners(lambda b: xs.at[2, m, b], 2, m)
            for i in range(3):
                to_owners(lambda b: dd.at[m, i], 4 + i, m)

    @pl.when(s > 1)
    def _():
        to_owners(lambda b: xs.at[2, :, b], 2)
        for i in range(3):
            to_owners(lambda b: dd.at[:, i], 4 + i)

    @pl.when(decoder)
    def _():
        @pl.when(s == 7)
        def _():
            for m in range(MICRO):
                arrived(cs.at[m, c], c_rs.at[m])

        forward_to_owners()
        to_owners(lambda b: xs.at[0, :, b], 1)

    key_slot = jnp.where(decoder, 1, 0)

    @pl.when(s >= SPREAD)
    def _():
        arrived(ob.at[3], b_rs.at[3])

    arrived(ob.at[2], b_rs.at[2])
    out_ref[3] = dot(ob[2].reshape(512, 512), ob[3].reshape(512, 512), TN).astype(BF)

    @pl.when(s >= SPREAD)
    def _():
        arrived(ob.at[0], b_rs.at[0])

    @pl.when(decoder)
    def _():
        arrived(ob.at[1], b_rs.at[1])

    for i in range(3):
        arrived(ob.at[4 + i], b_rs.at[4 + i])
        left = ob[0] if i == 0 else ob[key_slot]
        out_ref[i] = dot(left.reshape(512, 512), ob[4 + i].reshape(512, 512), TN).astype(BF)

    @pl.when(starts)
    def _():
        for m in range(MICRO):
            for k in range(8):
                sent_any(seed.at[m, 0], i_ss.at[m, k], start_to[k // 2])

    @pl.when(s == 0)
    def _():
        for m in range(MICRO):
            for k in range(8):
                sent_any(seed.at[m, 0], i_ss.at[m, k], first_to[k])

    @pl.when((s > 0) & spread_out)
    def _():
        for k in range(4):
            sent_any(ob.at[0, :, 0], xa_ss.at[k], tokens_at[k])

    def given(piece, carry):
        sent_any(own_shard(piece), ga_ss.at[piece], collector)
        arrived(shard(piece, 0), gc_ss.at[piece])

        @pl.when(inner)
        def _():
            for k in range(2):
                arrived(shards(piece, 0, 2), gb_ss.at[piece, k])

        return carry

    lax.fori_loop(0, 8, given, 0)


    @pl.when(s >= SPREAD)
    def _():
        owners_sent(lambda b: xs.at[sel, :, b], 0)
        owners_sent(lambda b: cs, 3)

    @pl.when(decoder)
    def _():
        owners_sent(lambda b: xs.at[0, :, b], 1)

    owners_sent(lambda b: xs.at[2, :, b], 2)
    for i in range(3):
        owners_sent(lambda b: dd.at[:, i], 4 + i)

    def finish(m, carry):
        @pl.when(decoder)
        def _():
            arrived(part.at[m, 0, :, pl.ds(0, 640)], q_ss.at[m])
            arrived(part.at[m, 0, :, pl.ds(640, 1152)], kv_ss.at[m])

        @pl.when(jnp.logical_not(decoder | spread_out))
        def _():
            arrived(part.at[m, 0], q_ss.at[m])

        @pl.when(jnp.logical_not(spread_out))
        def _():
            arrived(cs.at[m, 0], c_ss.at[m])

        @pl.when(spread_out)
        def _():
            for k in range(8):
                sent_any(sb.at[m, 0, 0], rb_ss.at[m, k], heads_at[k])
                sent_any(cs.at[m, 0], cb_ss.at[m, k], heads_of[k])

        arrived(dpart.at[m, 0], d_ss.at[m])
        arrived(dd.at[m, :, 0], dd_ss.at[m])
        arrived(cc.at[m, :, 0], cc_ss.at[m])

        @pl.when(decoder & (s < 7))
        def _():
            arrived(xs.at[0, m, 0], f_ss.at[m])

        @pl.when(s > 4)
        def _():
            for k in range(3):
                arrived(xs.at[0, m, 0], fp_ss.at[m, k])

        @pl.when(s < 7)
        def _():
            for k in range(3):
                arrived(ost.at[m, k], o_ss.at[m, k])
            for k in range(4):
                arrived(xn.at[m], n_ss.at[m, k])

        @pl.when((s > 0) & (s != 4))
        def _():
            for k in range(3):
                arrived(ust.at[m, k], u_ss.at[m, k])

        @pl.when(s > 0)
        def _():
            for k in range(4):
                arrived(gn.at[m], gn_ss.at[m, k])

        @pl.when(s >= 4)
        def _():
            for k in range(3):
                arrived(wst.at[m, k], w_ss.at[m, k])

        @pl.when(s > 4)
        def _():
            arrived(geout.at[m], e_ss.at[m])

        return carry

    lax.fori_loop(0, MICRO, finish, 0)


def per_device(enc_input, dec_input, cotangent, target_lengths, weights):
    tokens = MICRO * lax.axis_size("dp") * enc_input.shape[1] * enc_input.shape[2]
    dma = pltpu.SemaphoreType.DMA
    tile = (2, 16, 512)
    scratch = [
        pltpu.VMEM((4, 4, 512, 512), BF),
        pltpu.VMEM((3, 4, 512, 512), BF),
        pltpu.VMEM((4, 512, 512), BF),
        pltpu.VMEM((3, MICRO, 4) + tile, BF),
        pltpu.VMEM((MICRO, 4, 2, 16, 1664), BF),
        pltpu.VMEM((MICRO, 8, 16, 1664), BF),
        pltpu.VMEM((16, 1792), F32),
        pltpu.VMEM((MICRO, 2, 16, 512), BF),
        pltpu.VMEM((MICRO, 16, 1024), BF),
        pltpu.VMEM((MICRO, 2, 16, 1792), F32),
        pltpu.VMEM((MICRO, 16, 1792), F32),
        pltpu.VMEM((MICRO, 16, 512), BF),
        pltpu.VMEM((MICRO, 16, 512), BF),
        pltpu.VMEM((MICRO, 16, 512), BF),
        pltpu.VMEM((MICRO, 2, 16, 16), F32),
        pltpu.VMEM((MICRO, 2, 16, 128), F32),
        pltpu.VMEM((MICRO,) + tile, BF),
        pltpu.VMEM((MICRO, 32, 512), F32),
        pltpu.VMEM((MICRO, 3, 32, 512), BF),
        pltpu.VMEM((MICRO, 3, 32, 512), BF),
        pltpu.VMEM((MICRO,) + tile, BF),
        pltpu.VMEM((MICRO,) + tile, F32),
        pltpu.VMEM((MICRO, 16, 512), F32),
        pltpu.VMEM((MICRO, 3) + tile, BF),
        pltpu.VMEM((MICRO, 2, 2, 16, 128), F32),
        pltpu.VMEM((MICRO, 32, 512), F32),
        pltpu.VMEM((MICRO, 3, 32, 512), BF),
        pltpu.VMEM((MICRO, 3, 32, 512), BF),
        pltpu.VMEM((MICRO, 32, 512), F32),
        pltpu.VMEM((MICRO, 3, 32, 512), BF),
        pltpu.VMEM((MICRO, 3, 32, 512), BF),
        pltpu.VMEM((MICRO,) + tile, BF),
        pltpu.VMEM((MICRO,) + tile, BF),
        pltpu.VMEM((MICRO,) + tile, BF),
        pltpu.VMEM((7, MICRO, 4) + tile, BF),
        dma, dma,
        dma((MICRO, 8)), dma((MICRO,)),
        dma((MICRO, 8)), dma((MICRO,)),
        dma((MICRO, 4)), dma((4,)), dma,
        dma((8,)), dma((8,)),
        dma((8, 2)), dma((8,)),
        dma((8,)), dma((8,)),
        dma((MICRO, 8)), dma((3, MICRO, 4)),
        dma((MICRO,)), dma((MICRO, 3)),
        dma((MICRO,)), dma((MICRO,)),
        dma((MICRO,)), dma((MICRO,)),
        dma((MICRO,)), dma((MICRO,)),
        dma((MICRO, 3)), dma((MICRO,)),
        dma((MICRO, 4)),
        dma((MICRO,)), dma((MICRO,)),
        dma((MICRO,)), dma((MICRO,)),
        dma((MICRO,)), dma((MICRO,)),
        dma((MICRO, 3)), dma((MICRO,)),
        dma((MICRO, 3)), dma((MICRO,)),
        dma((MICRO,)), dma((MICRO,)),
        dma((MICRO, 4)),
        dma((7, 4)), dma((7,)),
    ]
    grads = pl.pallas_call(
        functools.partial(layer_kernel, 4096, float(tokens) ** (-0.5)),
        out_shape=jax.ShapeDtypeStruct((4, 512, 512), BF),
        in_specs=[pl.BlockSpec(memory_space=pltpu.SMEM)] + [pl.BlockSpec(memory_space=pl.ANY)] * 4,
        out_specs=pl.BlockSpec(memory_space=pltpu.VMEM),
        scratch_shapes=scratch,
        compiler_params=pltpu.CompilerParams(
            collective_id=0, has_side_effects=True, vmem_limit_bytes=60 << 20
        ),
        name="layers",
    )(target_lengths, enc_input, dec_input, cotangent, weights)
    return grads[None].astype(F32)


def solution(mesh):
    in_specs = (
        P(None, "dp", None, "mp"),
        P(None, "dp", None, "mp"),
        P(None, "dp", None, "mp"),
        P(None, "dp"),
        P("section", None, "dp", "mp"),
    )
    return jax.shard_map(
        per_device,
        mesh=mesh,
        in_specs=in_specs,
        out_specs=P("section", None, "dp", "mp"),
        check_vma=False,
    )
```

```python
import functools

import jax
import jax.numpy as jnp
from jax import lax
from jax.experimental import pallas as pl
from jax.experimental.pallas import tpu as pltpu
from jax.sharding import PartitionSpec as P

HEAD_DIM = 256
EPSILON = 1e-06
MICRO = 4
BF = jnp.bfloat16
F32 = jnp.float32
MESH = pl.DeviceIdType.MESH
SPREAD = 2
ORDER = (2, 1, 3, 0)
NT = (((1,), (1,)), ((), ()))
NN = (((1,), (0,)), ((), ()))
TN = (((0,), (0,)), ((), ()))


def dot(a, b, dims=NN):
    return lax.dot_general(a, b, dims, preferred_element_type=F32)


def layer_kernel(
    width, loss_scale,
    lengths_ref, enc_ref, dec_ref, cot_ref, weights_ref, out_ref,
    w, wt, wl, xs, sb, rb, tot, seed, seed_in, part, qrecv, qs, ks, vs, ps, rr, cs, oown, ost, orecv, xn,
    dpart, drecv, dd, cc, uown, ust, urecv, wown, wst, wrecv, gn, gein, geout, ob,
    s_sem, l_sem, rb_ss, rb_rs, cb_ss, cb_rs, xb_rs, xa_ss, xa_rs, ga_ss, ga_rs, gb_ss, gb_rs, gc_ss, gc_rs, i_ss, x_rs, f_ss, fp_ss, q_ss, q_rs, kv_ss, kv_rs,
    c_ss, c_rs, o_ss, o_rs, n_ss,
    d_ss, d_rs, dd_ss, dd_rs, cc_ss, cc_rs, u_ss, u_rs, w_ss, w_rs, e_ss, e_rs, gn_ss,
    b_ss, b_rs,
):
    s = lax.axis_index("section")
    d = lax.axis_index("dp")
    p = lax.axis_index("mp")
    t = d // 2
    c = lax.rem(p, 2)
    j = 2 * (p // 2) + lax.rem(d, 2)
    odd = lax.rem(t, 2)
    decoder = s >= 4
    sel = jnp.where(decoder, 1, 0)
    spread_out = s < SPREAD
    starts = (s == 4) | (s == 7)
    other = (d, p + 1 - 2 * c)

    def place(tt, jj, ccc):
        return 2 * tt + lax.rem(jj, 2), 2 * (jj // 2) + ccc

    def member(k):
        return place(t, lax.rem(j + k, 4), c)

    def fellow(k):
        return d, lax.rem(p + k, 4)

    def column(tt):
        return 2 * tt + lax.rem(d, 2), p

    collector = place(t, p, d // 4)
    inner = t // 2 == c
    beside = column(t + 1 - 2 * odd)
    across = column(lax.rem(t + 3 - 2 * odd, 4))
    senders = [place(k, p, d // 4) for k in range(4)]
    owner = [(4 * c + b, j) for b in range(4)]
    heads_at = [place(q, p, e) for q in range(4) for e in range(2)]
    heads_of = [(jnp.int32(k), j) for k in range(8)]
    tokens_at = [place(p, jnp.int32(k), d // 4) for k in range(4)]
    tokens_of = [(4 * c + b, t) for b in range(4)]
    start_to = [place(t, jnp.int32(k), p // 2) for k in range(4)]
    start_from = [(2 * t + a, 2 * c + e) for a in range(2) for e in range(2)]
    first_to = [(2 * p + e, jnp.int32(k)) for k in range(4) for e in range(2)]
    first_from = [(jnp.int32(k), d // 2) for k in range(8)]

    def same(dev):
        return (dev[0] == d) & (dev[1] == p)

    def remote(src, dst, ss, rs, dev, sec=None):
        ids = {"dp": dev[0], "mp": dev[1]}
        if sec is not None:
            ids["section"] = sec
        return pltpu.make_async_remote_copy(
            src_ref=src, dst_ref=dst, send_sem=ss, recv_sem=rs, device_id=ids, device_id_type=MESH
        )

    def arrived(ref, sem):
        pltpu.make_async_copy(ref, ref, sem).wait()

    def send_any(src, dst, ss, rs, dev):
        here = same(dev)

        @pl.when(here)
        def _():
            pltpu.make_async_copy(src, dst, rs).start()

        @pl.when(jnp.logical_not(here))
        def _():
            remote(src, dst, ss, rs, dev).start()

    def sent_any(src, ss, dev):
        @pl.when(jnp.logical_not(same(dev)))
        def _():
            arrived(src, ss)

    bar = pltpu.get_barrier_semaphore()

    def greet(dev, sec=None):
        ids = {"dp": dev[0], "mp": dev[1]}
        if sec is not None:
            ids["section"] = sec
        pl.semaphore_signal(bar, inc=1, device_id=ids, device_id_type=MESH)

    def greet_other(dev):
        @pl.when(jnp.logical_not(same(dev)))
        def _():
            greet(dev)

    greet(other)
    greet(beside)
    greet(across)
    for k in range(1, 4):
        greet(member(k))

    @pl.when(spread_out)
    def _():
        for k in range(1, 4):
            greet(fellow(k))
        for dev in heads_at + heads_of:
            greet_other(dev)

    @pl.when((s > 0) & spread_out)
    def _():
        for k in range(4):
            greet(fellow(k), s - 1)
        for dev in tokens_of:
            greet_other(dev)

    @pl.when(s == SPREAD)
    def _():
        for dev in tokens_of:
            greet(dev, SPREAD - 1)

    @pl.when(s > SPREAD)
    def _():
        for k in range(4):
            greet(member(k), s - 1)

    @pl.when(s < 7)
    def _():
        for k in range(4):
            greet(member(k), s + 1)

    for dev in senders:
        greet_other(dev)

    @pl.when(inner)
    def _():
        for e in range(2):
            greet_other((2 * t + e, j))

    @pl.when(s == 0)
    def _():
        for dev in first_from:
            greet_other(dev)

    @pl.when(starts)
    def _():
        for dev in start_from:
            greet_other(dev)

    def others(devs):
        return sum(jnp.where(same(dev), 0, 1) for dev in devs)

    count = 6 + jnp.where(s > 0, 4, 0) + jnp.where(s < 7, 4, 0) + others(owner)
    count = count + others([collector]) + jnp.where(starts, others(start_to), 0)
    count = count + jnp.where(spread_out, 3 + others(heads_at) + others(heads_of), 0)
    count = count + jnp.where((s > 0) & spread_out, others(tokens_at), 0)
    count = count + jnp.where(s == 0, others(first_to), 0)
    pl.semaphore_wait(bar, count)

    def shards(piece, first, number):
        return w.at[piece // 2, pl.ds(first, number), pl.ds(256 * lax.rem(piece, 2), 256)]

    def shard(piece, which):
        return w.at[piece // 2, which, pl.ds(256 * lax.rem(piece, 2), 256)]

    def own_shard(piece):
        return weights_ref.at[0, piece // 2, pl.ds(256 * lax.rem(piece, 2), 256)]

    def give(piece):
        send_any(
            own_shard(piece), shard(piece, lax.rem(d, 4)), ga_ss.at[piece], ga_rs.at[piece],
            collector,
        )

    local = pltpu.make_async_copy(weights_ref.at[0], wl, l_sem)

    @pl.when(spread_out)
    def _():
        local.start()


    def begin(src_of, stream):
        for m in range(MICRO):
            for k in range(4):
                for e in range(2):
                    block = 2 * lax.rem(p, 2) + e
                    send_any(
                        src_of(m, e), xs.at[stream, m, block, lax.rem(d, 2)],
                        i_ss.at[m, 2 * k + e], x_rs.at[stream, m, block], start_to[k],
                    )

    @pl.when(s == 0)
    def _():
        for m in range(MICRO):
            for k in range(8):
                send_any(
                    enc_ref.at[m, 0, :, pl.ds(512 * (k % 2), 512)],
                    ob.at[0, m, t, lax.rem(d, 2)], i_ss.at[m, k], xb_rs.at[m, t], first_to[k],
                )

    @pl.when(s == 4)
    def _():
        begin(lambda m, e: dec_ref.at[m, 0, :, pl.ds(512 * e, 512)], 1)

    @pl.when(s == 7)
    def _():
        loss = pltpu.make_async_copy(cot_ref.at[:, 0], seed_in, s_sem)
        loss.start()
        loss.wait()
        for m in range(MICRO):
            offsets = lax.broadcasted_iota(jnp.int32, (16, 1024), 0)
            live = jnp.where(offsets < lengths_ref[m, 0], loss_scale, 0.0)
            value = (seed_in[m].astype(F32) * live).astype(BF)
            for e in range(2):
                seed[m, e] = value[:, 512 * e:512 * e + 512]
        begin(lambda m, e: seed.at[m, e], 2)

    def pass_on(piece):
        arrived(shards(piece, 2 * (1 - odd), 2), gb_rs.at[piece])
        half = shard(piece, 2 * (1 - odd))
        remote(half, half, gc_ss.at[piece], gc_rs.at[piece], across).start()

    def collected(piece):
        mine = shards(piece, 2 * odd, 2)
        arrived(mine, ga_rs.at[piece])
        remote(mine, mine, gb_ss.at[piece, 0], gb_rs.at[piece], beside).start()
        remote(mine, mine, gb_ss.at[piece, 1], gb_rs.at[piece], across).start()

    def swap(piece):
        arrived(shards(piece, 2 * (1 - odd), 2), gb_rs.at[piece])
        half = shard(piece, 2 * (1 - odd) + 1)
        remote(half, half, gc_ss.at[piece], gc_rs.at[piece], beside).start()

    def swapped(piece):
        arrived(shards(piece, 2 * odd, 2), gc_rs.at[piece])

    def when(cond, what, *args):
        @pl.when(cond)
        def _():
            what(*args)

    def repeat(first, last, what):
        def one(piece, carry):
            what(piece)
            return carry

        lax.fori_loop(first, last, one, 0)

    def collect_on(piece):
        collected(piece)
        when(piece > 0, pass_on, piece - 1)

    def gather_some(pieces):
        repeat(0, 8, give)

        @pl.when(inner)
        def _():
            repeat(0, pieces + 1, collect_on)
            repeat(pieces + 1, 8, collected)

        @pl.when(jnp.logical_not(inner))
        def _():
            repeat(0, pieces, swap)
            repeat(0, pieces, swapped)

    def gather_one(piece):
        when(inner, pass_on, piece)
        when(jnp.logical_not(inner), swap, piece)

    def gather_end(pieces):
        @pl.when(jnp.logical_not(inner))
        def _():
            repeat(pieces, 8, swapped)

    when(jnp.logical_not(spread_out), gather_some, 6)

    @pl.when(spread_out)
    def _():
        local.wait()

    def rows(value):
        return value.reshape(32, 512)

    def block_at(k):
        return lax.rem(j + 4 - k, 4)

    def project(m, stream, mats, start, ss, rs, relayed=None):
        sums = [None] * len(mats)
        squares = None
        for k in ORDER:
            block = block_at(k)
            if k == 0 and relayed is not None:
                @pl.when(jnp.logical_not(relayed))
                def _():
                    arrived(xs.at[stream, m, block], x_rs.at[stream, m, block])
            else:
                arrived(xs.at[stream, m, block], x_rs.at[stream, m, block])
            left = rows(xs[stream, m, block])
            wide = left.astype(F32)
            square = jnp.sum(wide * wide, axis=-1, keepdims=True)
            squares = square if squares is None else squares + square
            for i, mat in enumerate(mats):
                term = dot(left, w[mat, block])
                sums[i] = term if sums[i] is None else sums[i] + term
        squares = jnp.broadcast_to(squares, (32, 128)).reshape(2, 16, 128)
        for i, mat in enumerate(mats):
            first = (0, 640, 1152)[mat]
            part[m, :, :, first:first + 512] = sums[i].reshape(2, 16, 512)
        if 0 in mats:
            part[m, :, :, 512:640] = squares
        if 1 in mats:
            part[m, :, :, 1664:1792] = squares
        cols = pl.ds(*start)
        remote(part.at[m, 1 - c, :, cols], qrecv.at[m, :, cols], ss.at[m], rs.at[m], other).start()

    def project_all(m):
        project(m, 0, (0, 1, 2), (0, 1792), q_ss, q_rs)

    def project_query(m):
        project(m, 1, (0,), (0, 640), q_ss, q_rs)

    def project_key(m):
        project(m, 0, (1, 2), (640, 1152), kv_ss, kv_rs, s > 4)

        @pl.when(s == 4)
        def _():
            onward(m)

    def onward(m):
        remote(
            xs.at[0, m, j], xs.at[0, m, j], f_ss.at[m], x_rs.at[0, m, j], (d, p), s + 1
        ).start()

    def relay(m):
        arrived(xs.at[0, m, j], x_rs.at[0, m, j])

        @pl.when(s < 7)
        def _():
            onward(m)

        for k in (2, 1, 3):
            remote(
                xs.at[0, m, j], xs.at[0, m, j], fp_ss.at[m, k - 1], x_rs.at[0, m, j], member(k)
            ).start()

    def project_first(m):
        for k in ORDER:
            quarter = lax.rem(p + 4 - k, 4)
            arrived(ob.at[0, m, quarter], xb_rs.at[m, quarter])
            left = rows(ob[0, m, quarter])
            wide = left.astype(F32)
            square = jnp.sum(wide * wide, axis=-1, keepdims=True)
            high = square.astype(BF)
            low = (square - high.astype(F32)).astype(BF)
            for i in range(3):
                sb[m, quarter, :, :, 512 * i:512 * i + 512] = dot(left, wl[i]).astype(BF).reshape(
                    2, 16, 512
                )
            lane = lax.broadcasted_iota(jnp.int32, (32, 128), 1)
            parts = jnp.where(
                lane < 64, jnp.broadcast_to(high.astype(F32), (32, 128)),
                jnp.broadcast_to(low.astype(F32), (32, 128)),
            )
            sb[m, quarter, :, :, 1536:] = parts.astype(BF).reshape(2, 16, 128)
            for e in range(2):
                send_any(
                    sb.at[m, quarter, e], rb.at[m, d], rb_ss.at[m, 2 * quarter + e], rb_rs.at[m],
                    place(quarter, p, e),
                )

    def output_first(m):
        arrived(ob.at[3, m], cb_rs.at[m])
        for k in ORDER:
            term = dot(rows(ob[3, m, lax.rem(p + k, 4)]), wl[3], NT)
            if k == 0:
                oown[m] = term
            else:
                ost[m, k - 1] = term.astype(BF)
                remote(
                    ost.at[m, k - 1], orecv.at[m, k - 1], o_ss.at[m, k - 1], o_rs.at[m], fellow(k)
                ).start()

    def advance_first(m):
        total = rows(ob[0, m, p]).astype(F32) + oown[m]
        arrived(orecv.at[m], o_rs.at[m])
        for k in range(3):
            total = total + orecv[m, k].astype(F32)
        xn[m] = total.astype(BF).reshape(2, 16, 512)

        @pl.when(s < SPREAD - 1)
        def _():
            for k in ORDER:
                remote(
                    xn.at[m], ob.at[0, m, p], n_ss.at[m, k], xb_rs.at[m, p], fellow(k), s + 1
                ).start()

        @pl.when(s == SPREAD - 1)
        def _():
            block = lax.rem(d, 4)
            for k in ORDER:
                remote(
                    xn.at[m], xs.at[0, m, block], n_ss.at[m, k], x_rs.at[0, m, block],
                    place(p, lax.rem(j + k, 4), d // 4), s + 1,
                ).start()

    def attend(m):
        @pl.when(decoder)
        def _():
            arrived(qrecv.at[m, :, pl.ds(0, 640)], q_rs.at[m])
            arrived(qrecv.at[m, :, pl.ds(640, 1152)], kv_rs.at[m])

        @pl.when(jnp.logical_not(decoder | spread_out))
        def _():
            arrived(qrecv.at[m], q_rs.at[m])

        @pl.when(jnp.logical_not(spread_out))
        def _():
            tot[...] = part[m, c] + qrecv[m]

        @pl.when(spread_out)
        def _():
            arrived(rb.at[m], rb_rs.at[m])
            summed = rb[m, 0].astype(F32)
            for k in range(1, 8):
                summed = summed + rb[m, k].astype(F32)
            square = summed[:, 1536:1537] + summed[:, 1600:1601]
            square = jnp.broadcast_to(square, (16, 128))
            tot[:, :512] = summed[:, :512]
            tot[:, 512:640] = square
            tot[:, 640:1664] = summed[:, 512:1536]
            tot[:, 1664:] = square

        total = tot[...]
        factor_q = lax.rsqrt(total[:, 512:513] * (1.0 / width) + EPSILON)
        factor_k = lax.rsqrt(total[:, 1664:1665] * (1.0 / width) + EPSILON)
        rr[m, 0] = jnp.broadcast_to(factor_q, (16, 128))
        rr[m, 1] = jnp.broadcast_to(factor_k, (16, 128))
        query = (total[:, :512] * factor_q).astype(BF)
        key = (total[:, 640:1152] * factor_k).astype(BF)
        value = (total[:, 1152:1664] * factor_k).astype(BF)
        qs[m] = query
        ks[m] = key
        vs[m] = value
        contexts = []
        for h in range(2):
            cols = slice(h * HEAD_DIM, (h + 1) * HEAD_DIM)
            raised = jnp.exp(dot(query[:, cols], key[:, cols], NT) * HEAD_DIM ** (-0.5))
            weight = (raised / jnp.sum(raised, axis=-1, keepdims=True)).astype(BF)
            ps[m, h] = weight.astype(F32)
            contexts.append(dot(weight, value[:, cols]).astype(BF))
        cs[m, c] = jnp.concatenate(contexts, axis=1)

        @pl.when(jnp.logical_not(spread_out))
        def _():
            remote(cs.at[m, c], cs.at[m, c], c_ss.at[m], c_rs.at[m], other).start()

        @pl.when(spread_out)
        def _():
            for k in range(8):
                send_any(
                    cs.at[m, c], ob.at[3, m, t, c], cb_ss.at[m, k], cb_rs.at[m], heads_of[k]
                )

    def output(m):
        arrived(cs.at[m, c], c_rs.at[m])
        context = rows(cs[m])
        for k in ORDER:
            term = dot(context, w[3, lax.rem(j + k, 4)], NT)
            if k == 0:
                oown[m] = term
            else:
                ost[m, k - 1] = term.astype(BF)
                remote(
                    ost.at[m, k - 1], orecv.at[m, k - 1], o_ss.at[m, k - 1], o_rs.at[m], member(k)
                ).start()

    def advance(m):
        total = rows(xs[sel, m, j]).astype(F32) + oown[m]
        arrived(orecv.at[m], o_rs.at[m])
        for k in range(3):
            total = total + orecv[m, k].astype(F32)
        xn[m] = total.astype(BF).reshape(2, 16, 512)
        for k in ORDER:
            remote(
                xn.at[m], xs.at[sel, m, j], n_ss.at[m, k], x_rs.at[sel, m, j], member(k), s + 1
            ).start()

    def forward_step(i):
        @pl.when((i < MICRO) & spread_out)
        def _():
            project_first(i)

        @pl.when((i > 2) & spread_out)
        def _():
            advance_first(i - 3)

        @pl.when((i > 1) & (i < MICRO + 2) & spread_out)
        def _():
            output_first(i - 2)

        begun = jnp.where(s == SPREAD, 2, 0)

        @pl.when((i >= begun) & (i < MICRO) & jnp.logical_not(decoder | spread_out))
        def _():
            project_all(i)

        @pl.when((i < MICRO - 1) & (s == 4))
        def _():
            project_query(i + 1)

        @pl.when((i < MICRO) & (s > 4))
        def _():
            project_query(i)

        @pl.when(((i < MICRO) & (s == 4)) | ((i < MICRO - 1) & (s > 4)))
        def _():
            project_key(i + jnp.where(s > 4, 1, 0))

        @pl.when((i < MICRO - 2) & (s > 4))
        def _():
            relay(i + 2)

        @pl.when((i > 0) & (i <= MICRO) & (s >= SPREAD) & (s < 7))
        def _():
            advance(i - 1)

        late = jnp.where(spread_out, 1, 0)

        @pl.when((i >= jnp.where(s == SPREAD, 1, late)) & (i < MICRO + late))
        def _():
            attend(i - late)

        @pl.when((i < MICRO) & (s >= SPREAD) & (s < 7))
        def _():
            output(i)

    def to_owners(src_of, slot, m=None):
        for b in range(4):
            dst = ob.at[slot, :, t] if m is None else ob.at[slot, m, t]
            send_any(src_of(b), dst, b_ss.at[slot, b], b_rs.at[slot], owner[b])

    def owners_sent(src_of, slot):
        for b in range(4):
            sent_any(src_of(b), b_ss.at[slot, b], owner[b])

    def project_back(m):
        total = None
        for k in ORDER:
            block = block_at(k)
            arrived(xs.at[2, m, block], x_rs.at[2, m, block])
            term = dot(rows(xs[2, m, block]), w[3, block])
            total = term if total is None else total + term
        dpart[m] = total.reshape(2, 16, 512)
        remote(dpart.at[m, 1 - c], drecv.at[m], d_ss.at[m], d_rs.at[m], other).start()

    def attend_back(m):
        query, key, value = qs[m], ks[m], vs[m]
        arrived(drecv.at[m], d_rs.at[m])
        grad = (dpart[m, c] + drecv[m]).astype(BF)
        pieces = [[], [], []]
        for h in range(2):
            cols = slice(h * HEAD_DIM, (h + 1) * HEAD_DIM)
            weight = ps[m, h]
            grad_weight = dot(grad[:, cols], value[:, cols], NT)
            pieces[2].append(dot(weight.astype(BF), grad[:, cols], TN))
            inside = jnp.sum(grad_weight * weight, axis=-1, keepdims=True)
            scores = (weight * (grad_weight - inside) * HEAD_DIM ** (-0.5)).astype(BF)
            pieces[0].append(dot(scores, key[:, cols]))
            pieces[1].append(dot(scores, query[:, cols], TN))
        grads = [jnp.concatenate(piece, axis=1) for piece in pieces]
        factors = [rr[m, 0][:, :1], rr[m, 1][:, :1], rr[m, 1][:, :1]]
        for i in range(3):
            dd[m, i, c] = (grads[i] * factors[i]).astype(BF)
        remote(dd.at[m, :, c], dd.at[m, :, c], dd_ss.at[m], dd_rs.at[m], other).start()
        means = [
            jnp.sum(g * v.astype(F32), axis=-1, keepdims=True) * (1.0 / width)
            for g, v in zip(grads, (query, key, value))
        ]
        cc[m, 0, c] = jnp.broadcast_to(means[0] * factors[0] * factors[0], (16, 128))
        cc[m, 1, c] = jnp.broadcast_to((means[1] + means[2]) * factors[1] * factors[1], (16, 128))
        remote(cc.at[m, :, c], cc.at[m, :, c], cc_ss.at[m], cc_rs.at[m], other).start()

    def spread_back(m):
        arrived(dd.at[m, :, c], dd_rs.at[m])
        arrived(cc.at[m, :, c], cc_rs.at[m])

        def spread(pairs, stream, kinds, own, stage, recv, ss, rs):
            lefts = [rows(dd[m, i]) for i in pairs]
            shift = sum(cc[m, i].reshape(32, 128)[:, :1] for i in kinds)
            for k in ORDER:
                block = lax.rem(j + k, 4)
                term = -rows(xs[stream, m, block]).astype(F32) * shift
                for i, left in zip(pairs, lefts):
                    term = term + dot(left, wt[i, block])
                if k == 0:
                    own[m] = term
                else:
                    stage[m, k - 1] = term.astype(BF)
                    remote(
                        stage.at[m, k - 1], recv.at[m, k - 1], ss.at[m, k - 1], rs.at[m], member(k)
                    ).start()

        @pl.when((s > 0) & (s < 4))
        def _():
            spread((0, 1, 2), 0, (0, 1), uown, ust, urecv, u_ss, u_rs)

        @pl.when(s > 4)
        def _():
            spread((0,), 1, (0,), uown, ust, urecv, u_ss, u_rs)

        @pl.when(s >= 4)
        def _():
            spread((1, 2), 0, (1,), wown, wst, wrecv, w_ss, w_rs)

    def hand_back(m):
        for k in ORDER:
            remote(
                gn.at[m], xs.at[2, m, j], gn_ss.at[m, k], x_rs.at[2, m, j], member(k), s - 1
            ).start()

    def advance_back(m):
        total = rows(xs[2, m, j]).astype(F32) + uown[m]
        arrived(urecv.at[m], u_rs.at[m])
        for k in range(3):
            total = total + urecv[m, k].astype(F32)
        gn[m] = total.astype(BF).reshape(2, 16, 512)
        hand_back(m)

    def advance_key(m):
        arrived(wrecv.at[m], w_rs.at[m])
        total = wown[m]
        for k in range(3):
            total = total + wrecv[m, k].astype(F32)
        geout[m] = total.astype(BF).reshape(2, 16, 512)

        @pl.when(s < 7)
        def _():
            arrived(gein.at[m], e_rs.at[m])
            geout[m] = (total + rows(gein[m]).astype(F32)).astype(BF).reshape(2, 16, 512)

        @pl.when(s > 4)
        def _():
            remote(geout.at[m], gein.at[m], e_ss.at[m], e_rs.at[m], (d, p), s - 1).start()

        @pl.when(s == 4)
        def _():
            gn[m] = geout[m]
            hand_back(m)

    def backward_step(i):
        @pl.when(i < MICRO)
        def _():
            project_back(i)

        @pl.when((i < MICRO) & (s < 4))
        def _():
            attend_back(i)

        @pl.when((i > 0) & (s > 0) & (s != 4))
        def _():
            advance_back(i - 1)

        @pl.when((i > 0) & (s == 4))
        def _():
            advance_key(i - 1)

        @pl.when((i < MICRO) & (s >= 4))
        def _():
            attend_back(i)

        @pl.when(i < MICRO)
        def _():
            spread_back(i)

            @pl.when((s == 0) | ((s == 1) & (i < 2)))
            def _():
                to_owners(lambda b: xs.at[2, i, b], 2, i)
                for k in range(3):
                    to_owners(lambda b: dd.at[i, k], 4 + k, i)

        @pl.when((i > 0) & (s > 4))
        def _():
            advance_key(i - 1)

    def last_step(i):
        @pl.when(i < MICRO)
        def _():
            project_query(i)

        @pl.when(i > 0)
        def _():
            advance_back(i - 1)

        @pl.when(i < MICRO)
        def _():
            attend(i)
            attend_back(i)

        @pl.when(i < MICRO - 1)
        def _():
            project_key(i + 1)

        @pl.when(i < MICRO)
        def _():
            spread_back(i)

        @pl.when(i < MICRO - 2)
        def _():
            relay(i + 2)

        @pl.when(i > 0)
        def _():
            advance_key(i - 1)

    @pl.when(jnp.logical_not(spread_out))
    def _():
        when(s == SPREAD, project_all, 0)
        gather_one(6)

        @pl.when(s == SPREAD)
        def _():
            attend(0)
            project_all(1)

        gather_one(7)
        gather_end(6)

    def turn(which):
        wt[which // 4, lax.rem(which, 4)] = w[which // 4, lax.rem(which, 4)].T

    when(decoder, repeat, 0, 12, turn)

    @pl.when(s == 4)
    def _():
        project_query(0)

    @pl.when(s == 7)
    def _():
        def one(m, carry):
            project_back(m)
            return carry

        lax.fori_loop(0, MICRO, one, 0)

    @pl.when(s > 4)
    def _():
        relay(0)
        relay(1)
        project_key(0)

    def forward_to_owners():
        to_owners(lambda b: xs.at[sel, :, b], 0)
        to_owners(lambda b: cs, 3)

    def step(n, carry):
        @pl.when((s == 7) & (n <= MICRO))
        def _():
            last_step(n)

        @pl.when((s < 7) & (n <= MICRO + 2))
        def _():
            forward_step(n)

        @pl.when(n == MICRO + 3)
        def _():
            @pl.when((s >= SPREAD) & (s < 4))
            def _():
                forward_to_owners()

            @pl.when((s > 0) & spread_out)
            def _():
                for k in range(4):
                    send_any(
                        ob.at[0, :, p], xs.at[0, :, lax.rem(d, 4)], xa_ss.at[k], xa_rs, tokens_at[k]
                    )

            @pl.when(spread_out)
            def _():
                gather_some(6)
                gather_one(6)
                gather_one(7)
                gather_end(6)

            when((s > 0) & (s < 4), repeat, 0, 12, turn)

            @pl.when((s > 0) & spread_out)
            def _():
                arrived(xs.at[0], xa_rs)

        @pl.when((s < 7) & (n >= MICRO + 3))
        def _():
            backward_step(n - MICRO - 3)

        return carry

    lax.fori_loop(0, 2 * MICRO + 4, step, 0)

    @pl.when(s == 1)
    def _():
        for m in range(2, MICRO):
            to_owners(lambda b: xs.at[2, m, b], 2, m)
            for i in range(3):
                to_owners(lambda b: dd.at[m, i], 4 + i, m)

    @pl.when(s > 1)
    def _():
        to_owners(lambda b: xs.at[2, :, b], 2)
        for i in range(3):
            to_owners(lambda b: dd.at[:, i], 4 + i)

    @pl.when(decoder)
    def _():
        @pl.when(s == 7)
        def _():
            for m in range(MICRO):
                arrived(cs.at[m, c], c_rs.at[m])

        forward_to_owners()
        to_owners(lambda b: xs.at[0, :, b], 1)

    key_slot = jnp.where(decoder, 1, 0)

    @pl.when(s >= SPREAD)
    def _():
        arrived(ob.at[3], b_rs.at[3])

    arrived(ob.at[2], b_rs.at[2])
    out_ref[3] = dot(ob[2].reshape(512, 512), ob[3].reshape(512, 512), TN).astype(BF)

    @pl.when(s >= SPREAD)
    def _():
        arrived(ob.at[0], b_rs.at[0])

    @pl.when(decoder)
    def _():
        arrived(ob.at[1], b_rs.at[1])

    for i in range(3):
        arrived(ob.at[4 + i], b_rs.at[4 + i])
        left = ob[0] if i == 0 else ob[key_slot]
        out_ref[i] = dot(left.reshape(512, 512), ob[4 + i].reshape(512, 512), TN).astype(BF)

    @pl.when(starts)
    def _():
        for m in range(MICRO):
            for k in range(8):
                sent_any(seed.at[m, 0], i_ss.at[m, k], start_to[k // 2])

    @pl.when(s == 0)
    def _():
        for m in range(MICRO):
            for k in range(8):
                sent_any(seed.at[m, 0], i_ss.at[m, k], first_to[k])

    @pl.when((s > 0) & spread_out)
    def _():
        for k in range(4):
            sent_any(ob.at[0, :, 0], xa_ss.at[k], tokens_at[k])

    def given(piece, carry):
        sent_any(own_shard(piece), ga_ss.at[piece], collector)
        arrived(shard(piece, 0), gc_ss.at[piece])

        @pl.when(inner)
        def _():
            for k in range(2):
                arrived(shards(piece, 0, 2), gb_ss.at[piece, k])

        return carry

    lax.fori_loop(0, 8, given, 0)


    @pl.when(s >= SPREAD)
    def _():
        owners_sent(lambda b: xs.at[sel, :, b], 0)
        owners_sent(lambda b: cs, 3)

    @pl.when(decoder)
    def _():
        owners_sent(lambda b: xs.at[0, :, b], 1)

    owners_sent(lambda b: xs.at[2, :, b], 2)
    for i in range(3):
        owners_sent(lambda b: dd.at[:, i], 4 + i)

    def finish(m, carry):
        @pl.when(decoder)
        def _():
            arrived(part.at[m, 0, :, pl.ds(0, 640)], q_ss.at[m])
            arrived(part.at[m, 0, :, pl.ds(640, 1152)], kv_ss.at[m])

        @pl.when(jnp.logical_not(decoder | spread_out))
        def _():
            arrived(part.at[m, 0], q_ss.at[m])

        @pl.when(jnp.logical_not(spread_out))
        def _():
            arrived(cs.at[m, 0], c_ss.at[m])

        @pl.when(spread_out)
        def _():
            for k in range(8):
                sent_any(sb.at[m, 0, 0], rb_ss.at[m, k], heads_at[k])
                sent_any(cs.at[m, 0], cb_ss.at[m, k], heads_of[k])

        arrived(dpart.at[m, 0], d_ss.at[m])
        arrived(dd.at[m, :, 0], dd_ss.at[m])
        arrived(cc.at[m, :, 0], cc_ss.at[m])

        @pl.when(decoder & (s < 7))
        def _():
            arrived(xs.at[0, m, 0], f_ss.at[m])

        @pl.when(s > 4)
        def _():
            for k in range(3):
                arrived(xs.at[0, m, 0], fp_ss.at[m, k])

        @pl.when(s < 7)
        def _():
            for k in range(3):
                arrived(ost.at[m, k], o_ss.at[m, k])
            for k in range(4):
                arrived(xn.at[m], n_ss.at[m, k])

        @pl.when((s > 0) & (s != 4))
        def _():
            for k in range(3):
                arrived(ust.at[m, k], u_ss.at[m, k])

        @pl.when(s > 0)
        def _():
            for k in range(4):
                arrived(gn.at[m], gn_ss.at[m, k])

        @pl.when(s >= 4)
        def _():
            for k in range(3):
                arrived(wst.at[m, k], w_ss.at[m, k])

        @pl.when(s > 4)
        def _():
            arrived(geout.at[m], e_ss.at[m])

        return carry

    lax.fori_loop(0, MICRO, finish, 0)


def per_device(enc_input, dec_input, cotangent, target_lengths, weights):
    tokens = MICRO * lax.axis_size("dp") * enc_input.shape[1] * enc_input.shape[2]
    dma = pltpu.SemaphoreType.DMA
    tile = (2, 16, 512)
    scratch = [
        pltpu.VMEM((4, 4, 512, 512), BF),
        pltpu.VMEM((3, 4, 512, 512), BF),
        pltpu.VMEM((4, 512, 512), BF),
        pltpu.VMEM((3, MICRO, 4) + tile, BF),
        pltpu.VMEM((MICRO, 4, 2, 16, 1664), BF),
        pltpu.VMEM((MICRO, 8, 16, 1664), BF),
        pltpu.VMEM((16, 1792), F32),
        pltpu.VMEM((MICRO, 2, 16, 512), BF),
        pltpu.VMEM((MICRO, 16, 1024), BF),
        pltpu.VMEM((MICRO, 2, 16, 1792), F32),
        pltpu.VMEM((MICRO, 16, 1792), F32),
        pltpu.VMEM((MICRO, 16, 512), BF),
        pltpu.VMEM((MICRO, 16, 512), BF),
        pltpu.VMEM((MICRO, 16, 512), BF),
        pltpu.VMEM((MICRO, 2, 16, 16), F32),
        pltpu.VMEM((MICRO, 2, 16, 128), F32),
        pltpu.VMEM((MICRO,) + tile, BF),
        pltpu.VMEM((MICRO, 32, 512), F32),
        pltpu.VMEM((MICRO, 3, 32, 512), BF),
        pltpu.VMEM((MICRO, 3, 32, 512), BF),
        pltpu.VMEM((MICRO,) + tile, BF),
        pltpu.VMEM((MICRO,) + tile, F32),
        pltpu.VMEM((MICRO, 16, 512), F32),
        pltpu.VMEM((MICRO, 3) + tile, BF),
        pltpu.VMEM((MICRO, 2, 2, 16, 128), F32),
        pltpu.VMEM((MICRO, 32, 512), F32),
        pltpu.VMEM((MICRO, 3, 32, 512), BF),
        pltpu.VMEM((MICRO, 3, 32, 512), BF),
        pltpu.VMEM((MICRO, 32, 512), F32),
        pltpu.VMEM((MICRO, 3, 32, 512), BF),
        pltpu.VMEM((MICRO, 3, 32, 512), BF),
        pltpu.VMEM((MICRO,) + tile, BF),
        pltpu.VMEM((MICRO,) + tile, BF),
        pltpu.VMEM((MICRO,) + tile, BF),
        pltpu.VMEM((7, MICRO, 4) + tile, BF),
        dma, dma,
        dma((MICRO, 8)), dma((MICRO,)),
        dma((MICRO, 8)), dma((MICRO,)),
        dma((MICRO, 4)), dma((4,)), dma,
        dma((8,)), dma((8,)),
        dma((8, 2)), dma((8,)),
        dma((8,)), dma((8,)),
        dma((MICRO, 8)), dma((3, MICRO, 4)),
        dma((MICRO,)), dma((MICRO, 3)),
        dma((MICRO,)), dma((MICRO,)),
        dma((MICRO,)), dma((MICRO,)),
        dma((MICRO,)), dma((MICRO,)),
        dma((MICRO, 3)), dma((MICRO,)),
        dma((MICRO, 4)),
        dma((MICRO,)), dma((MICRO,)),
        dma((MICRO,)), dma((MICRO,)),
        dma((MICRO,)), dma((MICRO,)),
        dma((MICRO, 3)), dma((MICRO,)),
        dma((MICRO, 3)), dma((MICRO,)),
        dma((MICRO,)), dma((MICRO,)),
        dma((MICRO, 4)),
        dma((7, 4)), dma((7,)),
    ]
    grads = pl.pallas_call(
        functools.partial(layer_kernel, 4096, float(tokens) ** (-0.5)),
        out_shape=jax.ShapeDtypeStruct((4, 512, 512), BF),
        in_specs=[pl.BlockSpec(memory_space=pltpu.SMEM)] + [pl.BlockSpec(memory_space=pl.ANY)] * 4,
        out_specs=pl.BlockSpec(memory_space=pltpu.VMEM),
        scratch_shapes=scratch,
        compiler_params=pltpu.CompilerParams(
            collective_id=0, has_side_effects=True, vmem_limit_bytes=60 << 20
        ),
        name="layers",
    )(target_lengths, enc_input, dec_input, cotangent, weights)
    return grads[None].astype(F32)


def solution(mesh):
    in_specs = (
        P(None, "dp", None, "mp"),
        P(None, "dp", None, "mp"),
        P(None, "dp", None, "mp"),
        P(None, "dp"),
        P("section", None, "dp", "mp"),
    )
    return jax.shard_map(
        per_device,
        mesh=mesh,
        in_specs=in_specs,
        out_specs=P("section", None, "dp", "mp"),
        check_vma=False,
    )
```
